128 devices in a mesh: tm: 16 (over z, y), space: 8 (over x, core).
Axes of the slice: x: 4, y: 4, z: 4, core: 2. Of those that a mesh axis runs over, the one named last changes fastest.
Arguments:
- start_state: float32 [4, 32768], P(None, 'space'), may hold values from -6 to 6
- guess: float32 [16, 4, 32768], P('tm', None, 'space'), may hold values from -6 to 6
- diag_blocks: bfloat16 [256, 128, 128], P('space'), may hold values from -3 to 1
- off_blocks: bfloat16 [256, 4, 128, 128], P('space'), may hold values from -0.125 to 0.125
- columns: int32 [256, 4], P('space'), may hold values from 0 to 255, as said below
- rates: float32 [32768], P('space'), may hold values from 0.2 to 2
- mixing: float32 [4, 4], replicated, may hold values from -3 to 3
- fine_inverse: bfloat16 [256, 128, 128], P('space'), may hold values from -1 to 2
- coarse_inverse: bfloat16 [256, 128, 128], P('space'), may hold values from -1 to 2
Outputs:
- node_values: float32 [16, 3, 4, 32768], P('tm', None, None, 'space')
The draws below stay inside these ranges and needn't reach their ends.
Inputs may be any that keep to these rules, and one draw needn't show every extreme that they name: `columns`: each entry lies within 8 blocks of its row's block; both -8 and +8 are reached by some row.
All inputs are finite; a program needn't handle non-finite values.
Results may differ from the reference program's by a relative error of at most 0.02.
Values may be sent and summed in bfloat16 or wider, within the bound.
A program may use at most 64 MiB of HBM per device.

```python
import math
import jax
import jax.numpy as jnp
from jax import lax

BS = 128
K = 4
SPECIES = 4
ITERS = 2
W = 8
NBLK = 256
NCELL = 32768
SLICES = 16


def draw_diag_blocks(key, part):
    key = jax.random.fold_in(key, 1)
    key_list = jax.random.split(key, 2)
    noise = jnp.clip(jax.random.normal(key_list[0], (NBLK, BS, BS), jnp.float32), -4.0, 4.0)
    levels = jax.random.uniform(key_list[1], (NBLK, BS, 1), jnp.float32, 1.0, 2.0)
    identity = (jnp.arange(BS)[:, None] == jnp.arange(BS)[None, :]).astype(jnp.float32)
    values = -levels * identity + 0.5 / jnp.sqrt(float(BS)) * noise
    return values.astype(jnp.bfloat16)


def draw_fine_inverse(key, part):
    key = jax.random.fold_in(key, 2)
    key_list = jax.random.split(key, 2)
    noise = jnp.clip(jax.random.normal(key_list[0], (NBLK, BS, BS), jnp.float32), -4.0, 4.0)
    levels = jax.random.uniform(key_list[1], (NBLK, BS, 1), jnp.float32, 0.65, 0.95)
    identity = (jnp.arange(BS)[:, None] == jnp.arange(BS)[None, :]).astype(jnp.float32)
    values = levels * identity + 0.25 / jnp.sqrt(float(BS)) * noise
    return values.astype(jnp.bfloat16)


def draw_coarse_inverse(key, part):
    key = jax.random.fold_in(key, 3)
    key_list = jax.random.split(key, 2)
    noise = jnp.clip(jax.random.normal(key_list[0], (NBLK, BS, BS), jnp.float32), -4.0, 4.0)
    levels = jax.random.uniform(key_list[1], (NBLK, BS, 1), jnp.float32, 0.5, 0.85)
    identity = (jnp.arange(BS)[:, None] == jnp.arange(BS)[None, :]).astype(jnp.float32)
    values = levels * identity + 0.25 / jnp.sqrt(float(BS)) * noise
    return values.astype(jnp.bfloat16)


def draw_columns(key, part):
    key = jax.random.fold_in(key, 4)
    key_list = jax.random.split(key, 4)
    row_index = jnp.arange(NBLK, dtype=jnp.int32)[:, None]
    left_step = jax.random.randint(key_list[0], (NBLK, 1), -W, 0)
    right_step = jax.random.randint(key_list[1], (NBLK, 1), 1, W + 1)
    other_steps = jax.random.randint(key_list[2], (NBLK, K - 2), -W, W + 1)
    offsets = jnp.concatenate([left_step, right_step, other_steps], axis=1).astype(jnp.int32)
    chosen_row = jax.random.randint(key_list[3], (), W, NBLK - W)
    marked = row_index == chosen_row
    entry_index = jnp.arange(K, dtype=jnp.int32)[None, :]
    offsets = jnp.where(marked & (entry_index == 0), -W, offsets)
    offsets = jnp.where(marked & (entry_index == 1), W, offsets)
    return jnp.clip(row_index + offsets, 0, NBLK - 1).astype(jnp.int32)


def block_levels(own_key, shape, cuts, smallest, high):
    def one(dim, shards_of):
        steps = jax.random.uniform(jax.random.fold_in(jax.random.fold_in(own_key, 6), dim), (shards_of,), jnp.float32, smallest / len(cuts), high / len(cuts))
        return jnp.repeat(jnp.exp(steps), shape[dim] // shards_of).reshape((-1,) + (1,) * (len(shape) - dim - 1))

    gain = one(*cuts[0])
    for cut in cuts[1:]:
        gain = gain * one(*cut)
    return gain


def bell_draw(own_key, dims, spread, most, pieces=(), kind=jnp.bfloat16):
    values = spread * jax.random.normal(own_key, dims, jnp.float32)
    if pieces:
        values = values * block_levels(own_key, dims, pieces, -0.22, 0.18)
    return jnp.clip(values, -most, most).astype(kind)


def setup_inputs(seed: int = 0) -> dict:
    streams_of = jax.random.split(jax.random.key(seed), 10)
    start_state = bell_draw(streams_of[0], (SPECIES, NCELL), 1.0, 6.0, ((1, 8),), jnp.float32)
    guess = bell_draw(streams_of[1], (SLICES, SPECIES, NCELL), 1.0, 6.0, ((0, 16), (2, 8)), jnp.float32)
    diag_blocks = draw_diag_blocks(jax.random.fold_in(streams_of[9], 71), 0)
    off_blocks = bell_draw(streams_of[3], (NBLK, K, BS, BS), (4 * BS * K) ** -0.5, 0.125, ((0, 8),))
    columns = draw_columns(jax.random.fold_in(streams_of[9], 71), 0)
    rates = jnp.clip(jnp.exp(math.log(2.0) - 2.3025851 * jax.random.uniform(streams_of[5], (NCELL,), jnp.float32) ** block_levels(streams_of[5], (NCELL,), ((0, 8),), -0.2, 0.2)), 0.2, 2.0)
    mixing = bell_draw(streams_of[6], (SPECIES, SPECIES), 0.5, 3.0, (), jnp.float32)
    fine_inverse = draw_fine_inverse(jax.random.fold_in(streams_of[9], 71), 0)
    coarse_inverse = draw_coarse_inverse(jax.random.fold_in(streams_of[9], 71), 0)
    return dict(start_state=start_state, guess=guess, diag_blocks=diag_blocks, off_blocks=off_blocks, columns=columns, rates=rates, mixing=mixing, fine_inverse=fine_inverse, coarse_inverse=coarse_inverse)


STEP = 0.25


def evaluate(field, diag_wide, off_wide, columns, rates, mixing):
    node_count = field.shape[0]
    narrow = field.astype(jnp.bfloat16).astype(jnp.float32)
    blocks = narrow.reshape(node_count, SPECIES, NBLK, BS)
    implicit = jnp.einsum("bij,nsbj->nsbi", diag_wide, blocks)
    nearby = blocks[:, :, columns]
    explicit = jnp.einsum("bkij,nsbkj->nsbi", off_wide, nearby)
    reaction = jnp.einsum("st,ntc->nsc", mixing, field, precision=lax.Precision.HIGHEST) * rates
    implicit = implicit.reshape(node_count, SPECIES, NCELL)
    explicit = explicit.reshape(node_count, SPECIES, NCELL) + reaction
    return implicit, explicit


def apply_inverse(rhs, inverse_wide):
    narrow = rhs.astype(jnp.bfloat16).astype(jnp.float32).reshape(SPECIES, NBLK, BS)
    return jnp.einsum("bij,sbj->sbi", inverse_wide, narrow).reshape(SPECIES, NCELL)


def reference(start_state, guess, diag_blocks, off_blocks, columns, rates, mixing, fine_inverse, coarse_inverse):
    diag_wide = diag_blocks.astype(jnp.float32)
    off_wide = off_blocks.astype(jnp.float32)
    fine_wide = fine_inverse.astype(jnp.float32)
    coarse_wide = coarse_inverse.astype(jnp.float32)
    half_step = STEP / 2

    def terms(field):
        return evaluate(field, diag_wide, off_wide, columns, rates, mixing)

    node_values = jnp.stack([guess, guess, guess], axis=1)
    node_values = node_values.at[0, 0].set(start_state)
    implicit_now, explicit_now = lax.map(terms, node_values)

    def fine_pass(item):
        values, implicit, explicit = item
        forces = implicit + explicit
        rhs_one = values[0] - half_step * implicit[1] + STEP * (5.0 / 24.0 * forces[0] + 1.0 / 3.0 * forces[1] - 1.0 / 24.0 * forces[2])
        node_one = apply_inverse(rhs_one, fine_wide)
        imp_one, exp_one = terms(node_one[None])
        rhs_two = node_one + half_step * (exp_one[0] - explicit[1]) - half_step * implicit[2] + STEP * (-1.0 / 24.0 * forces[0] + 1.0 / 3.0 * forces[1] + 5.0 / 24.0 * forces[2])
        node_two = apply_inverse(rhs_two, fine_wide)
        imp_two, exp_two = terms(node_two[None])
        one_force = imp_one[0] + exp_one[0]
        two_force = imp_two[0] + exp_two[0]
        fas_term = STEP * (2.0 / 3.0 * one_force - 1.0 / 3.0 * forces[0] - 1.0 / 3.0 * two_force)
        return node_one, node_two, imp_two[0], two_force, fas_term, forces[0], explicit[0]

    for sweep_round in range(ITERS):
        node_one, node_two, imp_two, two_force, fas_term, head_force, head_explicit = lax.map(fine_pass, (node_values, implicit_now, explicit_now))

        def chain(carry, item):
            index, exp_head, imp_end, force_head, force_end, fas = item
            start_value = jnp.where(index == 0, start_state, carry)
            start_imp, start_exp = terms(start_value[None])
            rhs_first = start_value + STEP * (start_exp[0] - exp_head) - STEP * imp_end + STEP / 2 * (force_head + force_end) + fas
            middle = apply_inverse(rhs_first, coarse_wide)
            mid_imp, mid_exp = terms(middle[None])
            rhs_second = start_value - STEP * mid_imp[0] + STEP / 2 * ((start_imp[0] + start_exp[0]) + (mid_imp[0] + mid_exp[0])) + fas
            end_value = apply_inverse(rhs_second, coarse_wide)
            return end_value, (start_value, end_value)

        slice_index = jnp.arange(SLICES, dtype=jnp.int32)
        initial = jnp.zeros((SPECIES, NCELL), jnp.float32)
        unused, (starts, ends) = lax.scan(chain, initial, (slice_index, head_explicit, imp_two, head_force, two_force, fas_term))
        middle_new = node_one + 0.5 * ((starts - node_values[:, 0]) + (ends - node_two))
        node_values = jnp.stack([starts, middle_new, ends], axis=1)
        implicit_now, explicit_now = lax.map(terms, node_values)
    return node_values
```

```python
import functools

import jax
import jax.numpy as jnp
from jax import lax
from jax.experimental import pallas as pl
from jax.experimental.pallas import tpu as pltpu
from jax.sharding import PartitionSpec as P

BS = 128
K = 4
SPECIES = 4
ITERS = 2
W = 8
STEP = 0.25
HALF = STEP / 2
MESH = pl.DeviceIdType.MESH
NODES, FIRST, SECOND, MIDDLE = range(4)
LEFT, RIGHT = 0, 1


def dot(lhs, rhs):
    return lax.dot_general(
        lhs.astype(jnp.bfloat16), rhs, (((1,), (0,)), ((), ())), preferred_element_type=jnp.float32
    )


def rows_loop(first, last, body):
    def step(i, carry):
        body(i)
        return carry

    lax.fori_loop(first, last, step, 0, unroll=True)


def kernel(
    n_tm, n_sp, rows,
    start, guess, cols, rates, mixing, diag_h, off_h, fine_h, coarse_h,
    out,
    diag_v, off_v, fine_v, coarse_v, raw_w, fine_w, comp_w,
    near, near_q, mix_v, nodes, imp_b, exp_b, mid_b, first_v, second_r,
    sum_c, sum_t, state, grown, partial, fresh,
    send_b, land, own_send, s_land, s_halo,
    place_of, load_sem, send_sem, recv_sem, s_send_sem, s_recv_sem,
):
    tm = lax.axis_index("tm")
    sp = lax.axis_index("space")
    base = sp * rows - W
    has_left, has_right = sp > 0, sp < n_sp - 1
    edge = W // 4

    loads = [
        pltpu.make_async_copy(src, dst, load_sem.at[i])
        for i, (src, dst) in enumerate(
            ((diag_h, diag_v), (off_h, off_v), (fine_h, fine_v), (coarse_h, coarse_v))
        )
    ]
    for load in loads:
        load.start()

    barrier = pltpu.get_barrier_semaphore()

    def greet(t, s, there):
        @pl.when(there)
        def _():
            pl.semaphore_signal(barrier, inc=1, device_id=(t, s), device_id_type=MESH)

    up, down = tm < n_tm - 1, tm > 0
    others = [
        (tm, sp - 1, has_left), (tm, sp + 1, has_right),
        (tm + 1, sp, up), (tm - 1, sp, down),
        (tm + 1, sp - 1, up & has_left), (tm + 1, sp + 1, up & has_right),
        (tm - 1, sp - 1, down & has_left), (tm - 1, sp + 1, down & has_right),
    ]
    for other in others:
        greet(*other)

    def local_place(b, carry):
        for k in range(K):
            place_of[b, k] = jnp.clip(cols[b, k] - base, 0, rows + 2 * W - 1)
        return carry

    lax.fori_loop(0, rows, local_place, 0)
    near[...] = jnp.zeros_like(near)
    near_q[...] = jnp.zeros_like(near_q)
    imp_b[...] = jnp.zeros_like(imp_b)
    exp_b[...] = jnp.zeros_like(exp_b)
    mid_b[...] = jnp.zeros_like(mid_b)
    for t in range(SPECIES):
        column = jnp.broadcast_to(mixing[:, t : t + 1], (SPECIES, BS))
        mix_v[t] = jnp.concatenate([column, column], axis=0)

    pl.semaphore_wait(barrier, sum(there.astype(jnp.int32) for _, _, there in others))

    def halo_copies(kind, count):
        to_left = pltpu.make_async_remote_copy(
            src_ref=send_b.at[kind, LEFT, pl.ds(0, count)],
            dst_ref=land.at[kind, RIGHT, pl.ds(0, count)],
            send_sem=send_sem.at[kind, LEFT], recv_sem=recv_sem.at[kind, RIGHT],
            device_id=(tm, sp - 1), device_id_type=MESH,
        )
        to_right = pltpu.make_async_remote_copy(
            src_ref=send_b.at[kind, RIGHT, pl.ds(0, count)],
            dst_ref=land.at[kind, LEFT, pl.ds(0, count)],
            send_sem=send_sem.at[kind, RIGHT], recv_sem=recv_sem.at[kind, LEFT],
            device_id=(tm, sp + 1), device_id_type=MESH,
        )
        return to_left, to_right

    def halo_send(kind, fields):
        for f, field in enumerate(fields):
            for j in range(edge):
                low = [field(4 * j + g) for g in range(4)]
                high = [field(rows - W + 4 * j + g) for g in range(4)]
                send_b[kind, LEFT, f * edge + j] = jnp.concatenate(low, axis=0).astype(jnp.bfloat16)
                send_b[kind, RIGHT, f * edge + j] = jnp.concatenate(high, axis=0).astype(jnp.bfloat16)
        to_left, to_right = halo_copies(kind, edge * len(fields))
        pl.when(has_left)(to_left.start)
        pl.when(has_right)(to_right.start)

    def halo_wait(kind, count):
        to_left, to_right = halo_copies(kind, edge * count)

        @pl.when(has_left)
        def _():
            to_right.wait_recv()
            to_left.wait_send()

        @pl.when(has_right)
        def _():
            to_left.wait_recv()
            to_right.wait_send()

    def spread(tile, target, block, row):
        wide = tile.astype(jnp.float32)
        for g in range(4):
            target[block + g, row : row + 4] = wide[4 * g : 4 * g + 4]

    def halo_place(kind, target, count):
        for f in range(count):
            for j in range(edge):
                spread(land[kind, LEFT, f * edge + j], target, 4 * j, 4 * f)
                spread(land[kind, RIGHT, f * edge + j], target, W + rows + 4 * j, 4 * f)

    def gather(source, b):
        return jnp.concatenate([source[place_of[b, k]] for k in range(K)], axis=1)

    def react(v, b):
        total = None
        for t in range(SPECIES):
            line = v[t : t + 1]
            if v.shape[0] == 8:
                second = v[4 + t : 5 + t]
                row = lax.broadcasted_iota(jnp.int32, (8, BS), 0)
                line = jnp.where(row < 4, jnp.broadcast_to(line, (8, BS)), jnp.broadcast_to(second, (8, BS)))
            term = mix_v[t, : v.shape[0]] * line
            total = term if total is None else total + term
        return total * rates[pl.ds(b, 1)]

    def implicit(b):
        return dot(near[W + b], raw_w[b, :BS])

    def explicit(b, count):
        got = dot(gather(near, b), raw_w[b, BS:])[: 4 * count]
        return got + react(near[W + b, : 4 * count], b)

    def begin(b):
        mine = guess[0, :, pl.ds(pl.multiple_of(b * BS, BS), BS)]
        first = start[:, pl.ds(pl.multiple_of(b * BS, BS), BS)]
        head = jnp.where(tm == 0, first, mine)
        nodes[b, 0:4] = head
        nodes[b, 4:8] = mine

    rows_loop(0, rows, begin)

    def transposed(b, carry):
        raw_w[b, :BS] = diag_v[b].T
        for k in range(K):
            raw_w[b, BS * (k + 1) : BS * (k + 2)] = off_v[b, k].T
        fine_w[b] = fine_v[b].T
        comp_w[b, BS : 2 * BS] = coarse_v[b].T
        return carry

    def composed(b, carry):
        both = dot(raw_w[b], comp_w[b, BS : 2 * BS]) * STEP
        comp_w[b, :BS] = both[:BS].astype(jnp.bfloat16)
        comp_w[b, 2 * BS :] = both[BS:].astype(jnp.bfloat16)
        return carry

    def order(body):
        return lambda: rows_loop(W, rows - W, body), lambda: (
            rows_loop(0, W, body), rows_loop(rows - W, rows, body)
        )

    def s_copies(it):
        return [
            (pltpu.make_async_remote_copy(
                src_ref=own_send.at[it], dst_ref=s_land.at[it],
                send_sem=s_send_sem.at[it, 0], recv_sem=s_recv_sem.at[it, 0],
                device_id=(tm + 1, sp), device_id_type=MESH), up, down),
            (pltpu.make_async_remote_copy(
                src_ref=own_send.at[it, pl.ds(0, edge)], dst_ref=s_halo.at[it, RIGHT],
                send_sem=s_send_sem.at[it, 1], recv_sem=s_recv_sem.at[it, 1],
                device_id=(tm + 1, sp - 1), device_id_type=MESH), up & has_left, down & has_right),
            (pltpu.make_async_remote_copy(
                src_ref=own_send.at[it, pl.ds(rows // 4 - edge, edge)], dst_ref=s_halo.at[it, LEFT],
                send_sem=s_send_sem.at[it, 2], recv_sem=s_recv_sem.at[it, 2],
                device_id=(tm + 1, sp + 1), device_id_type=MESH), up & has_right, down & has_left),
        ]

    def iteration(it, carry):
        halo_send(NODES, [lambda b: nodes[b, 0:4], lambda b: nodes[b, 4:8]])

        @pl.when(it == 0)
        def _():
            for load in loads:
                load.wait()
            lax.fori_loop(0, rows, transposed, 0)

        def place(b):
            near[W + b] = nodes[b]

        rows_loop(0, rows, place)
        own_part = jnp.where(it == 0, 0.0, 0.5)
        end_part = jnp.where(it == 0, 1.0, 0.5)

        def node_terms(b):
            imp = implicit(b)
            exp = explicit(b, 2)
            imp_0, exp_0, imp_2, exp_2 = imp[:4], exp[:4], imp[4:], exp[4:]
            one_i = imp_b[b] + own_part * imp_0 + end_part * imp_2
            one_e = exp_b[b] + own_part * exp_0 + end_part * exp_2
            f_0, f_1, f_2 = imp_0 + exp_0, one_i + one_e, imp_2 + exp_2
            rhs = near[W + b, 0:4] - HALF * one_i + STEP * (5 / 24 * f_0 + 1 / 3 * f_1 - 1 / 24 * f_2)
            second_r[b] = STEP * (-1 / 24 * f_0 + 1 / 3 * f_1 + 5 / 24 * f_2) - HALF * (one_e + imp_2)
            sum_c[b] = STEP * (1 / 6 * f_0 - exp_0)
            sum_t[b] = (-STEP / 3) * f_0
            imp_b[b] = -0.5 * imp_0
            exp_b[b] = -0.5 * exp_0
            first_v[b] = dot(rhs, fine_w[b])

        inner, outer = order(node_terms)
        inner()
        halo_wait(NODES, 2)
        halo_place(NODES, near, 2)
        outer()
        halo_send(FIRST, [lambda b: first_v[b]])

        def put_first(b):
            near[W + b, 0:4] = first_v[b]

        rows_loop(0, rows, put_first)

        def first_terms(b):
            imp = implicit(b)[:4]
            exp = explicit(b, 1)
            force = STEP * 2 / 3 * (imp + exp)
            sum_c[b] += force
            sum_t[b] += force
            imp_b[b] += imp
            exp_b[b] += exp
            fresh[b] = dot(first_v[b] + HALF * exp + second_r[b], fine_w[b])

        inner, outer = order(first_terms)
        inner()
        halo_wait(FIRST, 1)
        halo_place(FIRST, near, 1)
        outer()
        halo_send(SECOND, [lambda b: fresh[b]])

        @pl.when(it == 0)
        def _():
            lax.fori_loop(0, rows, composed, 0)

        def put_second(b):
            near[W + b, 0:4] = fresh[b]
            mid_b[b] = first_v[b] - 0.5 * (nodes[b, 0:4] + fresh[b])

        rows_loop(0, rows, put_second)

        def second_terms(b):
            imp = implicit(b)[:4]
            exp = explicit(b, 1)
            force = imp + exp
            sum_c[b] += STEP * (1 / 6 * force - imp)
            sum_t[b] += (-STEP / 3) * force
            imp_b[b] += -0.5 * imp
            exp_b[b] += -0.5 * exp

        inner, outer = order(second_terms)
        inner()
        halo_wait(SECOND, 1)
        halo_place(SECOND, near, 1)
        outer()

        @pl.when(tm == 0)
        def _():
            def own(b):
                near[W + b, 0:4] = start[:, pl.ds(pl.multiple_of(b * BS, BS), BS)]

            rows_loop(0, rows, own)
            for j in range(edge):
                spread(land[NODES, LEFT, j], near, 4 * j, 0)
                spread(land[NODES, RIGHT, j], near, W + rows + 4 * j, 0)

        @pl.when(tm > 0)
        def _():
            for copy, _, hears in s_copies(it):
                pl.when(hears)(copy.wait_recv)
            for j in range(rows // 4):
                spread(s_land[it, j], near, W + 4 * j, 0)
            for j in range(edge):
                spread(s_halo[it, LEFT, j], near, 4 * j, 0)
                spread(s_halo[it, RIGHT, j], near, W + rows + 4 * j, 0)

        def middle(b):
            own = near[W + b, 0:4]
            change = STEP * react(own, b)
            spread_s = dot(gather(near, b), comp_w[b, 2 * BS :])[:4]
            got = dot(own + change + sum_c[b], comp_w[b, BS : 2 * BS]) + spread_s
            near_q[W + b, 0:4] = got
            partial[b] = 0.5 * spread_s
            state[b] = own + sum_t[b] + 0.5 * change

        rows_loop(0, W, middle)
        rows_loop(rows - W, rows, middle)
        halo_send(MIDDLE, [lambda b: near_q[W + b, 0:4]])
        rows_loop(W, rows - W, middle)

        def local_end(b):
            own, mid = near[W + b, 0:4], near_q[W + b, 0:4]
            right = state[b] + HALF * react(mid, b)
            both = jnp.concatenate([0.5 * (own - mid), right], axis=1)
            partial[b] += dot(both, comp_w[b, : 2 * BS])

        rows_loop(0, rows, local_end)

        def end(b):
            grown[b] = partial[b] + 0.5 * dot(gather(near_q, b), comp_w[b, 2 * BS :])[:4]

        inner, outer = order(end)
        inner()
        halo_wait(MIDDLE, 1)
        halo_place(MIDDLE, near_q, 1)
        outer()

        for j in range(rows // 4):
            tile = jnp.concatenate([grown[4 * j + g] for g in range(4)], axis=0)
            own_send[it, j] = tile.astype(jnp.bfloat16)
        for copy, sends, _ in s_copies(it):
            pl.when(sends)(copy.start)

        def renew(b):
            own = near[W + b, 0:4]
            nodes[b, 0:4] = own
            nodes[b, 4:8] = grown[b]
            mid_b[b] += 0.5 * (own + grown[b])

        rows_loop(0, rows, renew)
        return carry

    lax.fori_loop(0, ITERS, iteration, 0)

    def write(b):
        at = pl.ds(pl.multiple_of(b * BS, BS), BS)
        out[0, 0, :, at] = nodes[b, 0:4]
        out[0, 1, :, at] = mid_b[b]
        out[0, 2, :, at] = nodes[b, 4:8]

    rows_loop(0, rows, write)
    for it in range(ITERS):
        for copy, sends, _ in s_copies(it):
            pl.when(sends)(copy.wait_send)


def shards(n_tm, n_sp, start, guess, diag, off, columns, rates, mixing, fine, coarse):
    rows = diag.shape[0]
    f32, bf16 = jnp.float32, jnp.bfloat16
    vmem = pl.BlockSpec(memory_space=pltpu.VMEM)
    smem = pl.BlockSpec(memory_space=pltpu.SMEM)
    hbm = pl.BlockSpec(memory_space=pl.ANY)
    field = pltpu.VMEM((rows, SPECIES, BS), f32)
    edge = W // 4
    scratch = [
        pltpu.VMEM((rows, BS, BS), bf16), pltpu.VMEM((rows, K, BS, BS), bf16),
        pltpu.VMEM((rows, BS, BS), bf16), pltpu.VMEM((rows, BS, BS), bf16),
        pltpu.VMEM((rows, (K + 1) * BS, BS), bf16), pltpu.VMEM((rows, BS, BS), bf16),
        pltpu.VMEM((rows, (K + 2) * BS, BS), bf16),
        pltpu.VMEM((rows + 2 * W, 8, BS), f32), pltpu.VMEM((rows + 2 * W, 8, BS), f32),
        pltpu.VMEM((SPECIES, 8, BS), f32), pltpu.VMEM((rows, 8, BS), f32),
        *[field] * 11,
        pltpu.VMEM((4, 2, 2 * edge, 16, BS), bf16), pltpu.VMEM((4, 2, 2 * edge, 16, BS), bf16),
        pltpu.VMEM((ITERS, rows // 4, 16, BS), bf16), pltpu.VMEM((ITERS, rows // 4, 16, BS), bf16),
        pltpu.VMEM((ITERS, 2, edge, 16, BS), bf16),
        pltpu.SMEM((rows, K), jnp.int32),
        pltpu.SemaphoreType.DMA((4,)), pltpu.SemaphoreType.DMA((4, 2)), pltpu.SemaphoreType.DMA((4, 2)),
        pltpu.SemaphoreType.DMA((ITERS, 3)), pltpu.SemaphoreType.DMA((ITERS, 3)),
    ]
    return pl.pallas_call(
        functools.partial(kernel, n_tm, n_sp, rows),
        out_shape=jax.ShapeDtypeStruct((1, 3, SPECIES, rows * BS), f32),
        in_specs=[vmem, vmem, smem, vmem, vmem, hbm, hbm, hbm, hbm],
        out_specs=vmem,
        scratch_shapes=scratch,
        compiler_params=pltpu.CompilerParams(
            collective_id=0, has_side_effects=True, vmem_limit_bytes=48 << 20
        ),
    )(start, guess, columns, rates.reshape(rows, BS), mixing, diag, off, fine, coarse)


def solution(mesh):
    in_specs = (
        P(None, "space"),
        P("tm", None, "space"),
        P("space", None, None),
        P("space", None, None, None),
        P("space", None),
        P("space"),
        P(),
        P("space", None, None),
        P("space", None, None),
    )
    out_specs = P("tm", None, None, "space")
    body = functools.partial(shards, mesh.shape["tm"], mesh.shape["space"])
    return jax.shard_map(body, mesh=mesh, in_specs=in_specs, out_specs=out_specs, check_vma=False)
```

```python
import functools

import jax
import jax.numpy as jnp
from jax import lax
from jax.experimental import pallas as pl
from jax.experimental.pallas import tpu as pltpu
from jax.sharding import PartitionSpec as P

BS = 128
K = 4
SPECIES = 4
ITERS = 2
W = 8
STEP = 0.25
HALF = STEP / 2
MESH = pl.DeviceIdType.MESH
NODES, FIRST, SECOND = range(3)
LEFT, RIGHT = 0, 1
GROUP = 4
OWN = 16
WINDOW = OWN + 2 * W
T_OWN, T_WINDOW, T_EDGE = OWN // 4, WINDOW // 4, W // 4


def dot(lhs, rhs):
    return lax.dot_general(
        lhs.astype(jnp.bfloat16), rhs, (((1,), (0,)), ((), ())), preferred_element_type=jnp.float32
    )


def rows_loop(first, last, body):
    def step(i, carry):
        body(i)
        return carry

    lax.fori_loop(first, last, step, 0, unroll=True)


def kernel(
    n_tm, n_sp, rows,
    start_h, guess_h, cols_h, rates_h, mixing_h, diag_h, off_h, fine_h, coarse_h,
    out,
    start, guess, cols, rates, mixing,
    diag_v, off_v, fine_v, raw_w, diag_w, fine_w, win_diag, win_off, win_coarse, win_rates, comp_w, inverse_w,
    near, near_q, mix_v, nodes, imp_b, exp_b, mid_b, first_v, second_r,
    sum_c, sum_t, state, solved, partial, fresh, right_v,
    send_b, land, terms_b, terms_land, rest_land, start_b, chain_land, end_b, value_land, value_halo,
    cols_land, cols_s, place_of, place_w,
    load_sem, send_sem, recv_sem, unit_send, unit_recv, cols_send, cols_recv,
    terms_send, terms_recv, start_send, chain_send, chain_recv, value_send, value_recv,
):
    tm = lax.axis_index("tm")
    sp = lax.axis_index("space")
    plane, line, chip, core = tm // GROUP, tm % GROUP, sp // 2, sp % 2
    has_left, has_right = sp > 0, sp < n_sp - 1
    edge = W // 4
    chunks = n_sp * rows // OWN

    def quarter(x, y):
        return jnp.where(x % 2 == 0, y, GROUP - 1 - y)

    def chain_device(i, z):
        x, j = i // GROUP, i % GROUP
        return z * GROUP + quarter(x, j), 2 * x + 1

    def chain_plane(group):
        return (group + 2) % GROUP

    mine = quarter(chip, line)
    chunk = GROUP * chip + mine
    group = (plane + 2) % GROUP
    on_chain = core == 1
    even = chunk % 2 == 0
    chunk_left, chunk_right = chunk > 0, chunk < chunks - 1
    owner = chunk // 2
    beside = jnp.where(even, owner - 1, owner + 1)
    has_beside = (even & chunk_left) | (~even & chunk_right)
    low, high = 2 * sp, 2 * sp + 1

    def remote(src, dst, out_sem, in_sem, device):
        return pltpu.make_async_remote_copy(
            src_ref=src, dst_ref=dst, send_sem=out_sem, recv_sem=in_sem,
            device_id=device, device_id_type=MESH,
        )

    def arrive(dst, in_sem, there=None):
        def wait():
            remote(dst, dst, send_sem.at[0, 0], in_sem, (tm, sp)).wait_recv()

        if there is None:
            wait()
        else:
            pl.when(there)(wait)

    loads = [
        pltpu.make_async_copy(src, dst, load_sem.at[i])
        for i, (src, dst) in enumerate((
            (mixing_h, mixing), (guess_h, guess), (start_h, start), (cols_h, cols), (rates_h, rates),
            (diag_h, diag_v), (off_h, off_v), (fine_h, fine_v),
        ))
    ]
    for load in loads:
        load.start()
    small, large = loads[:5], loads[5:]
    cols_land[...] = jnp.zeros_like(cols_land)

    barrier = pltpu.get_barrier_semaphore()
    my_plane = chain_plane(plane)
    later, before = group < GROUP - 1, group > 0
    after, earlier = (plane + 1) % GROUP, (plane + GROUP - 1) % GROUP
    senders, receivers = [], []

    def both(device, there):
        senders.append((device, there))
        receivers.append(there)

    both((tm, sp - 1), has_left)
    both((tm, sp + 1), has_right)
    for i, there in ((low - 1, has_left), (low, True), (high, True), (high + 1, has_right)):
        both(chain_device(i, my_plane), there)
        senders.append((chain_device(i, chain_plane(plane + GROUP - 1)), there & (line == 0) & (plane > 0)))
    for y in range(GROUP):
        both((group * GROUP + y, owner), on_chain)
        both((group * GROUP + y, beside), on_chain & has_beside)
    receivers.append(on_chain & later)
    receivers.append(on_chain & later & has_beside)
    both(chain_device(chunk - 1, plane), on_chain & chunk_left)
    both(chain_device(chunk + 1, plane), on_chain & chunk_right)
    for i, there in ((chunk, True), (chunk - 1, chunk_left), (chunk + 1, chunk_right)):
        senders.append((chain_device(i, earlier), on_chain & before & there))
        receivers.append(on_chain & later & there)

    for device, there in senders:
        def signal(device=device):
            pl.semaphore_signal(barrier, inc=1, device_id=device, device_id_type=MESH)

        pl.when(there)(signal)

    for load in small:
        load.wait()

    def local_place(b, carry):
        for k in range(K):
            place_of[b, k] = jnp.clip(cols[0, b * K + k] - (sp * rows - W), 0, rows + 2 * W - 1)
        return carry

    lax.fori_loop(0, rows, local_place, 0)
    near[...] = jnp.zeros_like(near)
    near_q[...] = jnp.zeros_like(near_q)
    imp_b[...] = jnp.zeros_like(imp_b)
    exp_b[...] = jnp.zeros_like(exp_b)
    for t in range(SPECIES):
        column = jnp.broadcast_to(mixing[:, t : t + 1], (SPECIES, BS))
        mix_v[t] = jnp.concatenate([column, column], axis=0)

    def cells(b):
        return pl.ds(pl.multiple_of(b * BS, BS), BS)

    def begin(b):
        own = guess[0, :, cells(b)]
        nodes[b, 0:4] = jnp.where(tm == 0, start[:, cells(b)], own)
        nodes[b, 4:8] = own

    rows_loop(0, rows, begin)

    pl.semaphore_wait(barrier, sum(jnp.asarray(there).astype(jnp.int32) for there in receivers))

    def unit_copies(unit, at, device, extra=0):
        src, dst = pl.ds(unit * W, W), pl.ds(pl.multiple_of(at * W, W), W)
        pairs = ((off_h, win_off), (coarse_h, win_coarse), (rates_h, win_rates), (diag_h, win_diag))
        copies = []
        for n, (a, b) in enumerate(pairs):
            if device is None:
                copies.append(pltpu.make_async_copy(a.at[src], b.at[dst], unit_recv.at[at, n]))
            else:
                copies.append(remote(a.at[src], b.at[dst], unit_send.at[4 if extra else unit, n], unit_recv.at[at, n], device))
        return copies

    def unit_plan():
        plan = []
        for unit in range(4):
            at = unit - 2 * mine + 1
            plan.append((unit, at, (tm, sp + 1), (core == 0) & (at >= 0) & (at < 4), 0))
            at = unit + 4 - 2 * mine + 1
            plan.append((unit, at, None, on_chain & (at >= 0) & (at < 4), 0))
        next_low = quarter(chip + 1, line) == 0
        plan.append((3, 0, (tm, sp + 2), on_chain & (chip < n_sp // 2 - 1) & next_low, 1))
        last_high = quarter(chip - 1, line) == GROUP - 1
        plan.append((0, 3, (tm, sp - 1), (core == 0) & (chip > 0) & last_high, 1))
        return plan

    def cols_copy(which):
        slot, device = ((1, (tm, sp + 1)), (3, (tm, sp - 1)), (0, (tm, sp + 2)))[which]
        return remote(cols_h, cols_land.at[slot], cols_send.at[which], cols_recv.at[slot], device)

    def cols_plan():
        next_low = quarter(chip + 1, line) == 0
        last_high = quarter(chip - 1, line) == GROUP - 1
        return (
            (0, core == 0),
            (1, (core == 0) & (chip > 0) & last_high),
            (2, on_chain & (chip < n_sp // 2 - 1) & next_low),
        )

    def weights_out():
        for which, there in cols_plan():
            pl.when(there)(cols_copy(which).start)
        for unit, at, device, there, extra in unit_plan():
            def go(unit=unit, at=at, device=device, extra=extra):
                copies = unit_copies(unit, at, device, extra)
                for copy in copies[:3]:
                    copy.start()
                pl.when((at == 1) | (at == 2))(copies[3].start)

            pl.when(there)(go)

    def weights_sent():
        for which, there in cols_plan():
            pl.when(there)(cols_copy(which).wait_send)
        for unit, at, device, there, extra in unit_plan():
            if device is None:
                continue

            def done(unit=unit, at=at, device=device, extra=extra):
                copies = unit_copies(unit, at, device, extra)
                for copy in copies[:3]:
                    copy.wait_send()
                pl.when((at == 1) | (at == 2))(copies[3].wait_send)

            pl.when(there)(done)

    pl.when(plane == chain_plane(0))(weights_out)

    def halo_copies(kind, count):
        to_left = remote(
            send_b.at[kind, LEFT, pl.ds(0, count)], land.at[kind, RIGHT, pl.ds(0, count)],
            send_sem.at[kind, LEFT], recv_sem.at[kind, RIGHT], (tm, sp - 1),
        )
        to_right = remote(
            send_b.at[kind, RIGHT, pl.ds(0, count)], land.at[kind, LEFT, pl.ds(0, count)],
            send_sem.at[kind, RIGHT], recv_sem.at[kind, LEFT], (tm, sp + 1),
        )
        return to_left, to_right

    def tile(values):
        return jnp.concatenate(values, axis=0).astype(jnp.bfloat16)

    def halo_send(kind, fields):
        for f, field in enumerate(fields):
            for j in range(edge):
                send_b[kind, LEFT, f * edge + j] = tile([field(4 * j + g) for g in range(4)])
                send_b[kind, RIGHT, f * edge + j] = tile([field(rows - W + 4 * j + g) for g in range(4)])
        to_left, to_right = halo_copies(kind, edge * len(fields))
        pl.when(has_left)(to_left.start)
        pl.when(has_right)(to_right.start)

    def halo_wait(kind, count):
        to_left, to_right = halo_copies(kind, edge * count)

        @pl.when(has_left)
        def _():
            to_right.wait_recv()
            to_left.wait_send()

        @pl.when(has_right)
        def _():
            to_left.wait_recv()
            to_right.wait_send()

    def spread(block_tile, target, block, row):
        wide = block_tile.astype(jnp.float32)
        for g in range(4):
            target[block + g, row : row + 4] = wide[4 * g : 4 * g + 4]

    def halo_place(kind, target, count):
        for f in range(count):
            for j in range(edge):
                spread(land[kind, LEFT, f * edge + j], target, 4 * j, 4 * f)
                spread(land[kind, RIGHT, f * edge + j], target, W + rows + 4 * j, 4 * f)

    def gather(source, places, b):
        return jnp.concatenate([source[places[b, k]] for k in range(K)], axis=1)

    def react(v, rate):
        total = None
        for t in range(SPECIES):
            line_t = v[t : t + 1]
            if v.shape[0] == 8:
                second = v[4 + t : 5 + t]
                row = lax.broadcasted_iota(jnp.int32, (8, BS), 0)
                line_t = jnp.where(row < 4, jnp.broadcast_to(line_t, (8, BS)), jnp.broadcast_to(second, (8, BS)))
            term = mix_v[t, : v.shape[0]] * line_t
            total = term if total is None else total + term
        return total * rate

    def paired(first, second, weights):
        got = dot(jnp.concatenate([first, second], axis=0), weights)
        return got[:8, :BS], got[8:, BS:]

    def explicit(b, count):
        got = dot(gather(near, place_of, b), raw_w[b])[: 4 * count]
        return got + react(near[W + b, : 4 * count], rates[pl.ds(b, 1)])

    def transposed(n, carry):
        for r in range(4):
            b, half = 4 * n + r, pl.ds(BS * (r % 2), BS)
            diag_w[2 * n + r // 2, :, half] = diag_v[b].T
            fine_w[2 * n + r // 2, :, half] = fine_v[b].T
            for k in range(K):
                raw_w[b, BS * k : BS * (k + 1)] = off_v[b, k].T
        return carry

    def outer(*bodies):
        for body in bodies:
            rows_loop(0, W // 2, body)
            rows_loop((rows - W) // 2, rows // 2, body)

    def inner(*bodies):
        for body in bodies:
            rows_loop(W // 2, (rows - W) // 2, body)

    def solve(target):
        def pair(i):
            got = paired(right_v[2 * i], right_v[2 * i + 1], fine_w[i])
            target[2 * i], target[2 * i + 1] = got[0][:4], got[1][:4]

        return pair

    def terms_copies(it):
        slot = it * GROUP + line
        main, rest = terms_land.at[slot], rest_land.at[slot]
        to = [chain_device(i, my_plane) for i in (low, high, low - 1, high + 1)]

        def piece(first, count, dst, n, sem, device):
            return remote(
                terms_b.at[it, pl.ds(first, count)], dst, terms_send.at[it, n], terms_recv.at[slot, sem], device
            )

        t_rows = rows // 4
        return (
            (piece(0, 6, main.at[pl.ds(2, 6)], 0, 0, to[0]), True),
            (piece(2, 6, main.at[pl.ds(0, 6)], 1, 0, to[1]), True),
            (piece(0, 2, main.at[pl.ds(6, 2)], 2, 1, to[2]), has_left),
            (piece(6, 2, main.at[pl.ds(0, 2)], 3, 1, to[3]), has_right),
            (piece(t_rows, T_OWN, rest, 4, 2, to[0]), True),
            (piece(t_rows + T_OWN, T_OWN, rest, 5, 2, to[1]), True),
        )

    def fine(it):
        @pl.when(it == 0)
        def _():
            halo_send(NODES, [lambda b: nodes[b, 0:4], lambda b: nodes[b, 4:8]])
            for load in large:
                load.wait()
            lax.fori_loop(0, rows // 4, transposed, 0)
            halo_wait(NODES, 2)
            halo_place(NODES, near, 2)

        @pl.when(it == 1)
        def _():
            @pl.when(tm > 0)
            def _():
                values_wait(0, 0, True)
                for j in range(rows // 4):
                    spread(value_land[0, 0, j], nodes, 4 * j, 0)
                for j in range(edge):
                    spread(value_halo[0, LEFT, j], near, 4 * j, 0)
                    spread(value_halo[0, RIGHT, j], near, W + rows + 4 * j, 0)

            @pl.when(tm == 0)
            def _():
                for j in range(edge):
                    spread(land[NODES, LEFT, j], near, 4 * j, 0)
                    spread(land[NODES, RIGHT, j], near, W + rows + 4 * j, 0)

            values_wait(0, 1, True)
            for j in range(rows // 4):
                spread(value_land[0, 1, j], nodes, 4 * j, 4)
            for j in range(edge):
                spread(value_halo[1, LEFT, j], near, 4 * j, 4)
                spread(value_halo[1, RIGHT, j], near, W + rows + 4 * j, 4)

        def place(b):
            near[W + b] = nodes[b]

        rows_loop(0, rows, place)
        own_part = jnp.where(it == 0, 0.0, 0.5)
        end_part = jnp.where(it == 0, 1.0, 0.5)

        def node_terms(i):
            imps = paired(near[W + 2 * i], near[W + 2 * i + 1], diag_w[i])
            for b, imp in zip((2 * i, 2 * i + 1), imps):
                exp = explicit(b, 2)
                imp_0, exp_0, imp_2, exp_2 = imp[:4], exp[:4], imp[4:], exp[4:]
                one_i = imp_b[b] + own_part * imp_0 + end_part * imp_2
                one_e = exp_b[b] + own_part * exp_0 + end_part * exp_2
                f_0, f_1, f_2 = imp_0 + exp_0, one_i + one_e, imp_2 + exp_2
                right_v[b, 0:4] = (
                    nodes[b, 0:4] - HALF * one_i + STEP * (5 / 24 * f_0 + 1 / 3 * f_1 - 1 / 24 * f_2)
                )
                second_r[b] = STEP * (-1 / 24 * f_0 + 1 / 3 * f_1 + 5 / 24 * f_2) - HALF * (one_e + imp_2)
                sum_c[b] = STEP * (1 / 6 * f_0 - exp_0)
                sum_t[b] = (-STEP / 3) * f_0
                imp_b[b] = -0.5 * imp_0
                exp_b[b] = -0.5 * exp_0

        outer(node_terms, solve(first_v))
        halo_send(FIRST, [lambda b: first_v[b]])
        inner(node_terms, solve(first_v))

        def put_first(b):
            near[W + b, 0:4] = first_v[b]

        rows_loop(0, rows, put_first)
        halo_wait(FIRST, 1)
        halo_place(FIRST, near, 1)

        def first_terms(i):
            imps = paired(near[W + 2 * i], near[W + 2 * i + 1], diag_w[i])
            for b, imp in zip((2 * i, 2 * i + 1), imps):
                imp = imp[:4]
                exp = explicit(b, 1)
                force = STEP * 2 / 3 * (imp + exp)
                right_v[b, 0:4] = first_v[b] + HALF * exp + second_r[b]
                sum_c[b] += force
                sum_t[b] += force
                imp_b[b] += imp
                exp_b[b] += exp

        outer(first_terms, solve(fresh))
        halo_send(SECOND, [lambda b: fresh[b]])
        inner(first_terms, solve(fresh))

        def put_second(b):
            near[W + b, 0:4] = fresh[b]
            mid_b[b] = first_v[b] - 0.5 * (nodes[b, 0:4] + fresh[b])

        rows_loop(0, rows, put_second)

        def second_terms(i):
            imps = paired(near[W + 2 * i], near[W + 2 * i + 1], diag_w[i])
            for b, imp in zip((2 * i, 2 * i + 1), imps):
                imp = imp[:4]
                exp = explicit(b, 1)
                force = imp + exp
                sum_c[b] += STEP * (1 / 6 * force - imp)
                sum_t[b] += (-STEP / 3) * force
                imp_b[b] += -0.5 * imp
                exp_b[b] += -0.5 * exp

        inner(second_terms)
        halo_wait(SECOND, 1)
        halo_place(SECOND, near, 1)
        outer(second_terms)
        for j in range(rows // 4):
            terms_b[it, j] = tile([sum_c[4 * j + g] for g in range(4)])
            terms_b[it, rows // 4 + j] = tile([sum_t[4 * j + g] for g in range(4)])
        for copy, there in terms_copies(it):
            if there is True:
                copy.start()
            else:
                pl.when(there)(copy.start)

    def values_wait(it, which, halos):
        for n in range(2):
            arrive(value_land.at[it, which, pl.ds(n * T_OWN, T_OWN)], value_recv.at[it, which, n])
        if halos:
            arrive(value_halo.at[which, LEFT], value_recv.at[it, which, 2], has_left)
            arrive(value_halo.at[which, RIGHT], value_recv.at[it, which, 3], has_right)

    def value_copies(it, j):
        g = it * GROUP + j
        p = group * GROUP + j
        half = chunk % 2
        copies = []
        for which in (1, 0):
            t = p + 1 - which
            there = (p < n_tm - 1) if which == 0 else True
            copies.append((remote(
                end_b.at[g], value_land.at[it, which, pl.ds(pl.multiple_of(half * T_OWN, T_OWN), T_OWN)],
                value_send.at[g, which, 0], value_recv.at[it, which, half], (t, owner)), there))
            copies.append((remote(
                end_b.at[g, pl.ds(pl.multiple_of(half * (T_OWN - T_EDGE), T_EDGE), T_EDGE)], value_halo.at[which, 1 - half],
                value_send.at[g, which, 1], value_recv.at[it, which, 3 - half], (t, beside)),
                there & has_beside & (it == 0)))
        return copies

    def chain_copies(it, j):
        g = it * GROUP + j
        inside = j < GROUP - 1
        target = jnp.where(inside, g + 1, it * GROUP)
        z = jnp.where(inside, plane, after)
        there = inside | later
        copies = []
        for n, (i, ok) in enumerate(((chunk - 1, chunk_left), (chunk, ~inside), (chunk + 1, chunk_right))):
            part = 2 - n
            copies.append((remote(
                end_b.at[g], chain_land.at[target, part], chain_send.at[g, n], chain_recv.at[target, part],
                chain_device(i, z)), there & ok))
        return copies

    def start_copies():
        copies = []
        for n, (i, part, half, ok) in enumerate((
            (low, 1, 0, True), (low, 2, 1, True), (low - 1, 2, 0, has_left),
            (high, 1, 1, True), (high, 0, 0, True), (high + 1, 0, 1, has_right),
        )):
            copies.append((remote(
                start_b.at[pl.ds(half * T_OWN, T_OWN)], chain_land.at[0, part], start_send.at[n],
                chain_recv.at[0, part], chain_device(i, chain_plane(0))), (tm == 0) & ok))
        return copies

    @pl.when(tm == 0)
    def _():
        for j in range(rows // 4):
            start_b[j] = tile([nodes[4 * j + g, 0:4] for g in range(4)])
        for copy, there in start_copies():
            pl.when(there)(copy.start)

    def window_weights():
        first_unit = 2 * mine - 1
        arrive(cols_land.at[1], cols_recv.at[1])
        arrive(cols_land.at[0], cols_recv.at[0], (mine == 0) & (chip > 0))
        arrive(cols_land.at[3], cols_recv.at[3], (mine == GROUP - 1) & (chip < n_sp // 2 - 1))
        to_scalars = pltpu.make_async_copy(cols_land, cols_s, cols_send.at[3])
        to_scalars.start()
        for at in range(4):
            there = (first_unit + at >= 0) | (chip > 0)
            there = there & ((first_unit + at < 8) | (chip < n_sp // 2 - 1))

            @pl.when(there)
            def _(at=at):
                copies = unit_copies(0, at, (tm, sp))
                for copy in copies[:3] if at in (0, 3) else copies:
                    copy.wait_recv()

        to_scalars.wait()

        def places(w, carry):
            unit = first_unit + w // W
            slot, row = (unit + 4) // 4, (unit + 4) % 4 * W + w % W
            for k in range(K):
                column = jnp.where(slot == 2, cols[0, row * K + k], cols_s[slot, 0, row * K + k])
                place_w[w, k] = jnp.clip(column - (chunk * OWN - 2 * W), 0, OWN + 4 * W - 1)
            return carry

        lax.fori_loop(0, WINDOW, places, 0)

        def composed(n, carry):
            for r in range(4):
                w = 4 * n + r
                inverse = win_coarse[w].T
                comp_w[w, BS : 2 * BS] = inverse
                inverse_w[2 * n + r // 2, :, BS * (r % 2) : BS * (r % 2 + 1)] = inverse
                raw = [win_diag[w]] + [win_off[w, k] for k in range(K)]
                got = (dot(jnp.concatenate([block.T for block in raw], axis=0), inverse) * STEP).astype(jnp.bfloat16)
                comp_w[w, :BS] = got[:BS]
                comp_w[w, 2 * BS :] = got[BS:]
            return carry

        lax.fori_loop(0, WINDOW // 4, composed, 0)

    def chain_step(g, carry):
        it, j = g // GROUP, g % GROUP
        from_start = (j == 0) & (group == 0)
        slot = jnp.where(from_start, 0, g)

        fresh_start = ~(from_start & (it == 1))
        main_at = jnp.where(even, 2, 0)
        halo_at = jnp.where(even, 0, 6)

        @pl.when(j == 0)
        def _():
            arrive(chain_land.at[g, 1], chain_recv.at[g, 1], fresh_start)
            for n in range(T_OWN):
                spread(chain_land[slot, 1, n], near, 2 * W + 4 * n, 0)

        arrive(terms_land.at[g, pl.ds(main_at, 6)], terms_recv.at[g, 0])
        arrive(terms_land.at[g, pl.ds(halo_at, 2)], terms_recv.at[g, 1], has_beside)
        arrive(rest_land.at[g], terms_recv.at[g, 2])

        def prepare(n):
            constant = terms_land[g, n].astype(jnp.float32)
            for r in range(4):
                w = 4 * n + r
                own = near[W + w, 0:4]
                change = STEP * react(own, win_rates[pl.ds(w, 1)])
                right_v[w, 0:4] = own + change + constant[4 * r : 4 * r + 4]
                state[w] = own + 0.5 * change
            for i in (2 * n, 2 * n + 1):
                got = paired(right_v[2 * i], right_v[2 * i + 1], inverse_w[i])
                solved[2 * i], solved[2 * i + 1] = got[0][:4], got[1][:4]

        rows_loop(T_EDGE, T_WINDOW - T_EDGE, prepare)

        def with_rest(n):
            constant = rest_land[g, n].astype(jnp.float32)
            for r in range(4):
                state[W + 4 * n + r] += constant[4 * r : 4 * r + 4]

        rows_loop(0, T_OWN, with_rest)

        @pl.when(fresh_start)
        def _():
            arrive(chain_land.at[g, 0], chain_recv.at[g, 0], chunk_left)
            arrive(chain_land.at[g, 2], chain_recv.at[g, 2], chunk_right)

        for n in range(T_OWN):
            spread(chain_land[slot, 0, n], near, 4 * n, 0)
            spread(chain_land[slot, 2, n], near, 2 * W + OWN + 4 * n, 0)

        rows_loop(0, T_EDGE, prepare)
        rows_loop(T_WINDOW - T_EDGE, T_WINDOW, prepare)

        def middle(w):
            spread_s = dot(gather(near, place_w, w), comp_w[w, 2 * BS :])[:4]
            near_q[W + w, 0:4] = solved[w] + spread_s
            partial[w] = 0.5 * spread_s

        rows_loop(0, WINDOW, middle)

        def end(o):
            w = W + o
            own, mid = near[W + w, 0:4], near_q[W + w, 0:4]
            right = state[w] + HALF * react(mid, win_rates[pl.ds(w, 1)])
            parts = jnp.concatenate([0.5 * (own - mid), right, 0.5 * gather(near_q, place_w, w)[:4]], axis=1)
            near[W + w, 0:4] = partial[w] + dot(parts, comp_w[w])

        rows_loop(0, OWN, end)
        for n in range(T_OWN):
            end_b[g, n] = tile([near[2 * W + 4 * n + r, 0:4] for r in range(4)])
        for copy, there in chain_copies(it, j):
            pl.when(there)(copy.start)
        for copy, there in value_copies(it, j):
            if there is True:
                copy.start()
            else:
                pl.when(there)(copy.start)
        return carry

    def round_of(it, carry):
        fine(it)
        pl.when((it == 0) & (plane != chain_plane(0)))(weights_out)

        @pl.when(on_chain & ((group < 2) == (it == 0)))
        def _():
            window_weights()
            lax.fori_loop(0, ITERS * GROUP, chain_step, 0)

        return carry

    lax.fori_loop(0, ITERS, round_of, 0)

    pl.when(tm > 0)(lambda: values_wait(1, 0, False))
    values_wait(1, 1, False)

    def write(j):
        ends = value_land[1, 1, j].astype(jnp.float32)
        starts = value_land[1, 0, j].astype(jnp.float32)
        for g in range(4):
            b = 4 * j + g
            own = jnp.where(tm == 0, start[:, cells(b)], starts[4 * g : 4 * g + 4])
            last = ends[4 * g : 4 * g + 4]
            out[0, 0, :, cells(b)] = own
            out[0, 1, :, cells(b)] = mid_b[b] + 0.5 * (own + last)
            out[0, 2, :, cells(b)] = last

    rows_loop(0, rows // 4, write)

    weights_sent()
    for copy, there in start_copies():
        pl.when(there)(copy.wait_send)
    for it in range(ITERS):
        for copy, there in terms_copies(it):
            if there is True:
                copy.wait_send()
            else:
                pl.when(there)(copy.wait_send)

    @pl.when(on_chain)
    def _():
        def sent(g, carry):
            it, j = g // GROUP, g % GROUP
            for copy, there in chain_copies(it, j) + value_copies(it, j):
                if there is True:
                    copy.wait_send()
                else:
                    pl.when(there)(copy.wait_send)
            return carry

        lax.fori_loop(0, ITERS * GROUP, sent, 0)


def shards(n_tm, n_sp, start, guess, diag, off, columns, rates, mixing, fine, coarse):
    rows = diag.shape[0]
    f32, bf16 = jnp.float32, jnp.bfloat16
    vmem = pl.BlockSpec(memory_space=pltpu.VMEM)
    hbm = pl.BlockSpec(memory_space=pltpu.HBM)
    dma = pltpu.SemaphoreType.DMA
    edge = W // 4
    slots = ITERS * GROUP

    def tiles(*lead):
        return pltpu.VMEM((*lead, 16, BS), bf16)

    def blocks(*lead):
        return pltpu.VMEM((*lead, BS, BS), bf16)

    pairs = pltpu.VMEM((rows // 2, BS, 2 * BS), bf16)
    scratch = [
        pltpu.VMEM((SPECIES, rows * BS), f32), pltpu.VMEM((1, SPECIES, rows * BS), f32),
        pltpu.SMEM((1, rows * K), jnp.int32), pltpu.VMEM((rows, BS), f32), pltpu.VMEM((SPECIES, SPECIES), f32),
        blocks(rows), blocks(rows, K), blocks(rows),
        pltpu.VMEM((rows, K * BS, BS), bf16), pairs, pairs,
        blocks(WINDOW), blocks(WINDOW, K), blocks(WINDOW), pltpu.VMEM((WINDOW, BS), f32),
        pltpu.VMEM((WINDOW, (K + 2) * BS, BS), bf16),
        pltpu.VMEM((WINDOW // 2, BS, 2 * BS), bf16),
        pltpu.VMEM((rows + 2 * W, 8, BS), f32), pltpu.VMEM((rows + 2 * W, 8, BS), f32),
        pltpu.VMEM((SPECIES, 8, BS), f32), pltpu.VMEM((rows, 8, BS), f32),
        *[pltpu.VMEM((rows, SPECIES, BS), f32)] * 11, pltpu.VMEM((rows, 8, BS), f32),
        tiles(3, 2, 2 * edge), tiles(3, 2, 2 * edge),
        tiles(ITERS, rows // 2), tiles(slots, T_WINDOW), tiles(slots, T_OWN),
        tiles(rows // 4), tiles(slots, 3, T_OWN), tiles(slots, T_OWN),
        tiles(ITERS, 2, rows // 4), tiles(2, 2, edge),
        pltpu.VMEM((4, 1, BS), jnp.int32), pltpu.SMEM((4, 1, BS), jnp.int32),
        pltpu.SMEM((rows, K), jnp.int32), pltpu.SMEM((WINDOW, K), jnp.int32),
        dma((8,)), dma((3, 2)), dma((3, 2)), dma((5, 4)), dma((4, 4)), dma((4,)), dma((4,)),
        dma((ITERS, 6)), dma((slots, 3)), dma((6,)), dma((slots, 3)), dma((slots, 3)),
        dma((slots, 2, 2)), dma((ITERS, 2, 4)),
    ]
    return pl.pallas_call(
        functools.partial(kernel, n_tm, n_sp, rows),
        out_shape=jax.ShapeDtypeStruct((1, 3, SPECIES, rows * BS), f32),
        in_specs=[hbm] * 9,
        out_specs=vmem,
        scratch_shapes=scratch,
        compiler_params=pltpu.CompilerParams(
            collective_id=0, has_side_effects=True, vmem_limit_bytes=48 << 20
        ),
    )(start, guess, columns.reshape(1, rows * K), rates.reshape(rows, BS), mixing, diag, off, fine, coarse)


def solution(mesh):
    in_specs = (
        P(None, "space"),
        P("tm", None, "space"),
        P("space", None, None),
        P("space", None, None, None),
        P("space", None),
        P("space"),
        P(),
        P("space", None, None),
        P("space", None, None),
    )
    out_specs = P("tm", None, None, "space")
    body = functools.partial(shards, mesh.shape["tm"], mesh.shape["space"])
    return jax.shard_map(body, mesh=mesh, in_specs=in_specs, out_specs=out_specs, check_vma=False)
```

```python
import functools

import jax
import jax.numpy as jnp
from jax import lax
from jax.experimental import pallas as pl
from jax.experimental.pallas import tpu as pltpu
from jax.sharding import PartitionSpec as P

BS = 128
K = 4
SPECIES = 4
ITERS = 2
W = 8
STEP = 0.25
HALF = STEP / 2
MESH = pl.DeviceIdType.MESH
NODES, FIRST, SECOND = range(3)
LEFT, RIGHT = 0, 1
GROUP = 4
OWN = 16
WINDOW = OWN + 2 * W
T_OWN, T_WINDOW, T_EDGE = OWN // 4, WINDOW // 4, W // 4
PIECES = ((0, 0, 0, 1), (0, 1, 1, 2), (0, GROUP - 1, 3, 1), (1, 0, 4, 2), (GROUP - 1, 0, 6, 2))


def dot(lhs, rhs):
    return lax.dot_general(
        lhs.astype(jnp.bfloat16), rhs, (((1,), (0,)), ((), ())), preferred_element_type=jnp.float32
    )


def rows_loop(first, last, body):
    def step(i, carry):
        body(i)
        return carry

    lax.fori_loop(first, last, step, 0, unroll=True)


def kernel(
    n_tm, n_sp, rows,
    start_h, guess_h, cols_h, rates_h, mixing_h, diag_h, off_h, fine_h, coarse_h,
    out,
    start, guess, cols, rates, mixing,
    diag_v, off_v, fine_v, raw_w, diag_w, fine_w, win_diag, win_off, win_coarse, win_rates, comp_w, inverse_w,
    near, near_q, mix_v, nodes, imp_b, exp_b, mid_b, first_v, second_r,
    sum_c, sum_t, state, solved, partial, fresh, right_v,
    send_b, land, terms_b, terms_land, rest_land, start_b, chain_land, end_b, value_land, value_halo,
    cols_land, cols_s, place_of, place_w,
    load_sem, send_sem, recv_sem, unit_send, unit_recv, cols_send, cols_recv, piece_send, piece_recv,
    terms_send, terms_recv, start_send, chain_send, chain_recv, value_send, value_recv,
):
    tm = lax.axis_index("tm")
    sp = lax.axis_index("space")
    plane, line, chip, core = tm // GROUP, tm % GROUP, sp // 2, sp % 2
    has_left, has_right = sp > 0, sp < n_sp - 1
    edge = W // 4
    chunks = n_sp * rows // OWN

    def quarter(x, y):
        return jnp.where(x % 2 == 0, y, GROUP - 1 - y)

    def chain_device(i, z):
        x, j = i // GROUP, i % GROUP
        return z * GROUP + quarter(x, j), 2 * x + 1

    def chain_plane(group):
        return (group + 2) % GROUP

    mine = quarter(chip, line)
    chunk = GROUP * chip + mine
    group = (plane + 2) % GROUP
    on_chain = core == 1
    even = chunk % 2 == 0
    chunk_left, chunk_right = chunk > 0, chunk < chunks - 1
    owner = chunk // 2
    beside = jnp.where(even, owner - 1, owner + 1)
    has_beside = (even & chunk_left) | (~even & chunk_right)
    low, high = 2 * sp, 2 * sp + 1

    def remote(src, dst, out_sem, in_sem, device):
        return pltpu.make_async_remote_copy(
            src_ref=src, dst_ref=dst, send_sem=out_sem, recv_sem=in_sem,
            device_id=device, device_id_type=MESH,
        )

    def arrive(dst, in_sem, there=None):
        def wait():
            remote(dst, dst, send_sem.at[0, 0], in_sem, (tm, sp)).wait_recv()

        if there is None:
            wait()
        else:
            pl.when(there)(wait)

    loads = [
        pltpu.make_async_copy(src, dst, load_sem.at[i])
        for i, (src, dst) in enumerate((
            (mixing_h, mixing), (guess_h, guess), (start_h, start), (cols_h, cols), (rates_h, rates),
            (diag_h, diag_v), (off_h, off_v), (fine_h, fine_v),
        ))
    ]
    for load in loads:
        load.start()
    small, large = loads[:5], loads[5:]
    cols_land[...] = jnp.zeros_like(cols_land)

    barrier = pltpu.get_barrier_semaphore()
    my_plane = chain_plane(plane)
    later, before = group < GROUP - 1, group > 0
    after, earlier = (plane + 1) % GROUP, (plane + GROUP - 1) % GROUP
    senders, receivers = [], []

    def both(device, there):
        senders.append((device, there))
        receivers.append(there)

    both((tm, sp - 1), has_left)
    both((tm, sp + 1), has_right)
    for i, there in ((low - 1, has_left), (low, True), (high, True), (high + 1, has_right)):
        both(chain_device(i, my_plane), there)
        senders.append((chain_device(i, chain_plane(plane + GROUP - 1)), there & (line == 0) & (plane > 0)))
    for y in range(GROUP):
        both((group * GROUP + y, owner), on_chain)
        both((group * GROUP + y, beside), on_chain & has_beside)
    receivers.append(on_chain & later)
    receivers.append(on_chain & later & has_beside)
    both(chain_device(chunk - 1, plane), on_chain & chunk_left)
    both(chain_device(chunk + 1, plane), on_chain & chunk_right)
    for i, there in ((chunk, True), (chunk - 1, chunk_left), (chunk + 1, chunk_right)):
        senders.append((chain_device(i, earlier), on_chain & before & there))
        receivers.append(on_chain & later & there)

    first_plane = chain_plane(0)
    lower = on_chain & (mine == 0) & (chip > 0)
    upper = on_chain & (mine == GROUP - 1) & (chip < n_sp // 2 - 1)

    def piece_sources(n):
        z = jnp.where(plane == first_plane, (plane + PIECES[n][0]) % GROUP, plane)
        t = z * GROUP + (line + PIECES[n][1]) % GROUP
        return ((t, sp - 2), lower), ((t, sp + 1), upper)

    def piece_targets(n, early):
        z = (plane + GROUP - PIECES[n][0]) % GROUP if early else plane
        y = (line + GROUP - PIECES[n][1]) % GROUP
        t = z * GROUP + y
        fits = (z == first_plane) if early else (z != first_plane)
        right = on_chain & (chip < n_sp // 2 - 1) & (quarter(chip + 1, y) == 0)
        left = ~on_chain & (chip > 0) & (quarter(chip - 1, y) == GROUP - 1)
        return ((t, sp + 2), fits & right, 3, 0), ((t, sp - 1), fits & left, 0, 3)

    for n in range(len(PIECES)):
        senders.extend(piece_sources(n))
        for early in (True, False):
            receivers.extend(there for _, there, _, _ in piece_targets(n, early))

    for device, there in senders:
        def signal(device=device):
            pl.semaphore_signal(barrier, inc=1, device_id=device, device_id_type=MESH)

        pl.when(there)(signal)

    for load in small:
        load.wait()

    def local_place(b, carry):
        for k in range(K):
            place_of[b, k] = jnp.clip(cols[0, b * K + k] - (sp * rows - W), 0, rows + 2 * W - 1)
        return carry

    lax.fori_loop(0, rows, local_place, 0)
    near[...] = jnp.zeros_like(near)
    near_q[...] = jnp.zeros_like(near_q)
    imp_b[...] = jnp.zeros_like(imp_b)
    exp_b[...] = jnp.zeros_like(exp_b)
    for t in range(SPECIES):
        column = jnp.broadcast_to(mixing[:, t : t + 1], (SPECIES, BS))
        mix_v[t] = jnp.concatenate([column, column], axis=0)

    def cells(b):
        return pl.ds(pl.multiple_of(b * BS, BS), BS)

    def begin(b):
        own = guess[0, :, cells(b)]
        nodes[b, 0:4] = jnp.where(tm == 0, start[:, cells(b)], own)
        nodes[b, 4:8] = own

    rows_loop(0, rows, begin)

    pl.semaphore_wait(barrier, sum(jnp.asarray(there).astype(jnp.int32) for there in receivers))

    def unit_copies(unit, at, device):
        src, dst = pl.ds(unit * W, W), pl.ds(pl.multiple_of(at * W, W), W)
        pairs = ((off_h, win_off), (coarse_h, win_coarse), (rates_h, win_rates), (diag_h, win_diag))
        copies = []
        for n, (a, b) in enumerate(pairs):
            if device is None:
                copies.append(pltpu.make_async_copy(a.at[src], b.at[dst], unit_recv.at[at, n]))
            else:
                copies.append(remote(a.at[src], b.at[dst], unit_send.at[unit, n], unit_recv.at[at, n], device))
        return copies

    def unit_plan():
        plan = []
        for unit in range(4):
            at = unit - 2 * mine + 1
            plan.append((unit, at, (tm, sp + 1), (core == 0) & (at >= 0) & (at < 4)))
            at = unit + 4 - 2 * mine + 1
            plan.append((unit, at, None, on_chain & (at >= 0) & (at < 4)))
        return plan

    def piece_copies(n, unit, at, device, row):
        first, count = PIECES[n][2:]
        src, dst = pl.ds(unit * W + first, count), pl.ds(at * W + first, count)
        copies = [
            remote(off_h.at[src], win_off.at[dst], piece_send.at[row, 0], piece_recv.at[n, 0], device),
            remote(coarse_h.at[src], win_coarse.at[dst], piece_send.at[row, 1], piece_recv.at[n, 1], device),
        ]
        if n == 0:
            src, dst = pl.ds(unit * W, W), pl.ds(at * W, W)
            copies.append(remote(rates_h.at[src], win_rates.at[dst], piece_send.at[row, 2], piece_recv.at[n, 2], device))
        return copies

    def pieces(early, act):
        for n in range(len(PIECES)):
            for device, there, unit, at in piece_targets(n, early):
                def go(n=n, unit=unit, at=at, device=device):
                    for copy in piece_copies(n, unit, at, device, n if early else n + len(PIECES)):
                        act(copy)

                pl.when(there)(go)

    def cols_copy(which):
        slot, device = ((1, (tm, sp + 1)), (3, (tm, sp - 1)), (0, (tm, sp + 2)))[which]
        return remote(cols_h, cols_land.at[slot], cols_send.at[which], cols_recv.at[slot], device)

    def cols_plan():
        next_low = quarter(chip + 1, line) == 0
        last_high = quarter(chip - 1, line) == GROUP - 1
        return (
            (0, core == 0),
            (1, (core == 0) & (chip > 0) & last_high),
            (2, on_chain & (chip < n_sp // 2 - 1) & next_low),
        )

    def weights_out():
        for which, there in cols_plan():
            pl.when(there)(cols_copy(which).start)
        for unit, at, device, there in unit_plan():
            def go(unit=unit, at=at, device=device):
                copies = unit_copies(unit, at, device)
                for copy in copies[:3]:
                    copy.start()
                pl.when((at == 1) | (at == 2))(copies[3].start)

            pl.when(there)(go)

    def weights_sent():
        for which, there in cols_plan():
            pl.when(there)(cols_copy(which).wait_send)
        for unit, at, device, there in unit_plan():
            if device is None:
                continue

            def done(unit=unit, at=at, device=device):
                copies = unit_copies(unit, at, device)
                for copy in copies[:3]:
                    copy.wait_send()
                pl.when((at == 1) | (at == 2))(copies[3].wait_send)

            pl.when(there)(done)

    pieces(True, lambda copy: copy.start())
    pl.when(plane == first_plane)(weights_out)

    def halo_copies(kind, count):
        to_left = remote(
            send_b.at[kind, LEFT, pl.ds(0, count)], land.at[kind, RIGHT, pl.ds(0, count)],
            send_sem.at[kind, LEFT], recv_sem.at[kind, RIGHT], (tm, sp - 1),
        )
        to_right = remote(
            send_b.at[kind, RIGHT, pl.ds(0, count)], land.at[kind, LEFT, pl.ds(0, count)],
            send_sem.at[kind, RIGHT], recv_sem.at[kind, LEFT], (tm, sp + 1),
        )
        return to_left, to_right

    def tile(values):
        return jnp.concatenate(values, axis=0).astype(jnp.bfloat16)

    def halo_send(kind, fields):
        for f, field in enumerate(fields):
            for j in range(edge):
                send_b[kind, LEFT, f * edge + j] = tile([field(4 * j + g) for g in range(4)])
                send_b[kind, RIGHT, f * edge + j] = tile([field(rows - W + 4 * j + g) for g in range(4)])
        to_left, to_right = halo_copies(kind, edge * len(fields))
        pl.when(has_left)(to_left.start)
        pl.when(has_right)(to_right.start)

    def halo_wait(kind, count):
        to_left, to_right = halo_copies(kind, edge * count)

        @pl.when(has_left)
        def _():
            to_right.wait_recv()
            to_left.wait_send()

        @pl.when(has_right)
        def _():
            to_left.wait_recv()
            to_right.wait_send()

    def spread(block_tile, target, block, row):
        wide = block_tile.astype(jnp.float32)
        for g in range(4):
            target[block + g, row : row + 4] = wide[4 * g : 4 * g + 4]

    def halo_place(kind, target, count):
        for f in range(count):
            for j in range(edge):
                spread(land[kind, LEFT, f * edge + j], target, 4 * j, 4 * f)
                spread(land[kind, RIGHT, f * edge + j], target, W + rows + 4 * j, 4 * f)

    def gather(source, places, b):
        return jnp.concatenate([source[places[b, k]] for k in range(K)], axis=1)

    def react(v, rate):
        total = None
        for t in range(SPECIES):
            line_t = v[t : t + 1]
            if v.shape[0] == 8:
                second = v[4 + t : 5 + t]
                row = lax.broadcasted_iota(jnp.int32, (8, BS), 0)
                line_t = jnp.where(row < 4, jnp.broadcast_to(line_t, (8, BS)), jnp.broadcast_to(second, (8, BS)))
            term = mix_v[t, : v.shape[0]] * line_t
            total = term if total is None else total + term
        return total * rate

    def paired(first, second, weights):
        got = dot(jnp.concatenate([first, second], axis=0), weights)
        return got[:8, :BS], got[8:, BS:]

    def explicit(b, count):
        got = dot(gather(near, place_of, b), raw_w[b])[: 4 * count]
        return got + react(near[W + b, : 4 * count], rates[pl.ds(b, 1)])

    def transposed(n, carry):
        for r in range(4):
            b, half = 4 * n + r, pl.ds(BS * (r % 2), BS)
            diag_w[2 * n + r // 2, :, half] = diag_v[b].T
            fine_w[2 * n + r // 2, :, half] = fine_v[b].T
            for k in range(K):
                raw_w[b, BS * k : BS * (k + 1)] = off_v[b, k].T
        return carry

    def outer(*bodies):
        for body in bodies:
            rows_loop(0, W // 2, body)
            rows_loop((rows - W) // 2, rows // 2, body)

    def inner(*bodies):
        for body in bodies:
            rows_loop(W // 2, (rows - W) // 2, body)

    def solve(target):
        def pair(i):
            got = paired(right_v[2 * i], right_v[2 * i + 1], fine_w[i])
            target[2 * i], target[2 * i + 1] = got[0][:4], got[1][:4]

        return pair

    def terms_copies(it):
        slot = it * GROUP + line
        main, rest = terms_land.at[slot], rest_land.at[slot]
        to = [chain_device(i, my_plane) for i in (low, high, low - 1, high + 1)]

        def piece(first, count, dst, n, sem, device):
            return remote(
                terms_b.at[it, pl.ds(first, count)], dst, terms_send.at[it, n], terms_recv.at[slot, sem], device
            )

        t_rows = rows // 4
        return (
            (piece(0, 6, main.at[pl.ds(2, 6)], 0, 0, to[0]), True),
            (piece(2, 6, main.at[pl.ds(0, 6)], 1, 0, to[1]), True),
            (piece(0, 2, main.at[pl.ds(6, 2)], 2, 1, to[2]), has_left),
            (piece(6, 2, main.at[pl.ds(0, 2)], 3, 1, to[3]), has_right),
            (piece(t_rows, T_OWN, rest, 4, 2, to[0]), True),
            (piece(t_rows + T_OWN, T_OWN, rest, 5, 2, to[1]), True),
        )

    def fine(it):
        @pl.when(it == 0)
        def _():
            halo_send(NODES, [lambda b: nodes[b, 0:4], lambda b: nodes[b, 4:8]])
            for load in large:
                load.wait()
            lax.fori_loop(0, rows // 4, transposed, 0)
            halo_wait(NODES, 2)
            halo_place(NODES, near, 2)

        @pl.when(it == 1)
        def _():
            @pl.when(tm > 0)
            def _():
                values_wait(0, 0, True)
                for j in range(rows // 4):
                    spread(value_land[0, 0, j], nodes, 4 * j, 0)
                for j in range(edge):
                    spread(value_halo[0, LEFT, j], near, 4 * j, 0)
                    spread(value_halo[0, RIGHT, j], near, W + rows + 4 * j, 0)

            @pl.when(tm == 0)
            def _():
                for j in range(edge):
                    spread(land[NODES, LEFT, j], near, 4 * j, 0)
                    spread(land[NODES, RIGHT, j], near, W + rows + 4 * j, 0)

            values_wait(0, 1, True)
            for j in range(rows // 4):
                spread(value_land[0, 1, j], nodes, 4 * j, 4)
            for j in range(edge):
                spread(value_halo[1, LEFT, j], near, 4 * j, 4)
                spread(value_halo[1, RIGHT, j], near, W + rows + 4 * j, 4)

        def place(b):
            near[W + b] = nodes[b]

        rows_loop(0, rows, place)
        own_part = jnp.where(it == 0, 0.0, 0.5)
        end_part = jnp.where(it == 0, 1.0, 0.5)

        def node_terms(i):
            imps = paired(near[W + 2 * i], near[W + 2 * i + 1], diag_w[i])
            for b, imp in zip((2 * i, 2 * i + 1), imps):
                exp = explicit(b, 2)
                imp_0, exp_0, imp_2, exp_2 = imp[:4], exp[:4], imp[4:], exp[4:]
                one_i = imp_b[b] + own_part * imp_0 + end_part * imp_2
                one_e = exp_b[b] + own_part * exp_0 + end_part * exp_2
                f_0, f_1, f_2 = imp_0 + exp_0, one_i + one_e, imp_2 + exp_2
                right_v[b, 0:4] = (
                    nodes[b, 0:4] - HALF * one_i + STEP * (5 / 24 * f_0 + 1 / 3 * f_1 - 1 / 24 * f_2)
                )
                second_r[b] = STEP * (-1 / 24 * f_0 + 1 / 3 * f_1 + 5 / 24 * f_2) - HALF * (one_e + imp_2)
                sum_c[b] = STEP * (1 / 6 * f_0 - exp_0)
                sum_t[b] = (-STEP / 3) * f_0
                imp_b[b] = -0.5 * imp_0
                exp_b[b] = -0.5 * exp_0

        outer(node_terms, solve(first_v))
        halo_send(FIRST, [lambda b: first_v[b]])
        inner(node_terms, solve(first_v))

        def put_first(b):
            near[W + b, 0:4] = first_v[b]

        rows_loop(0, rows, put_first)
        halo_wait(FIRST, 1)
        halo_place(FIRST, near, 1)

        def first_terms(i):
            imps = paired(near[W + 2 * i], near[W + 2 * i + 1], diag_w[i])
            for b, imp in zip((2 * i, 2 * i + 1), imps):
                imp = imp[:4]
                exp = explicit(b, 1)
                force = STEP * 2 / 3 * (imp + exp)
                right_v[b, 0:4] = first_v[b] + HALF * exp + second_r[b]
                sum_c[b] += force
                sum_t[b] += force
                imp_b[b] += imp
                exp_b[b] += exp

        outer(first_terms, solve(fresh))
        halo_send(SECOND, [lambda b: fresh[b]])
        inner(first_terms, solve(fresh))

        def put_second(b):
            near[W + b, 0:4] = fresh[b]
            mid_b[b] = first_v[b] - 0.5 * (nodes[b, 0:4] + fresh[b])

        rows_loop(0, rows, put_second)

        def second_terms(i):
            imps = paired(near[W + 2 * i], near[W + 2 * i + 1], diag_w[i])
            for b, imp in zip((2 * i, 2 * i + 1), imps):
                imp = imp[:4]
                exp = explicit(b, 1)
                force = imp + exp
                sum_c[b] += STEP * (1 / 6 * force - imp)
                sum_t[b] += (-STEP / 3) * force
                imp_b[b] += -0.5 * imp
                exp_b[b] += -0.5 * exp

        inner(second_terms)
        halo_wait(SECOND, 1)
        halo_place(SECOND, near, 1)
        outer(second_terms)
        for j in range(rows // 4):
            terms_b[it, j] = tile([sum_c[4 * j + g] for g in range(4)])
            terms_b[it, rows // 4 + j] = tile([sum_t[4 * j + g] for g in range(4)])
        for copy, there in terms_copies(it):
            if there is True:
                copy.start()
            else:
                pl.when(there)(copy.start)

    def values_wait(it, which, halos):
        for n in range(2):
            arrive(value_land.at[it, which, pl.ds(n * T_OWN, T_OWN)], value_recv.at[it, which, n])
        if halos:
            arrive(value_halo.at[which, LEFT], value_recv.at[it, which, 2], has_left)
            arrive(value_halo.at[which, RIGHT], value_recv.at[it, which, 3], has_right)

    def value_copies(it, j):
        g = it * GROUP + j
        p = group * GROUP + j
        half = chunk % 2
        copies = []
        for which in (1, 0):
            t = p + 1 - which
            there = (p < n_tm - 1) if which == 0 else True
            copies.append((remote(
                end_b.at[g], value_land.at[it, which, pl.ds(pl.multiple_of(half * T_OWN, T_OWN), T_OWN)],
                value_send.at[g, which, 0], value_recv.at[it, which, half], (t, owner)), there))
            copies.append((remote(
                end_b.at[g, pl.ds(pl.multiple_of(half * (T_OWN - T_EDGE), T_EDGE), T_EDGE)], value_halo.at[which, 1 - half],
                value_send.at[g, which, 1], value_recv.at[it, which, 3 - half], (t, beside)),
                there & has_beside & (it == 0)))
        return copies

    def chain_copies(it, j):
        g = it * GROUP + j
        inside = j < GROUP - 1
        target = jnp.where(inside, g + 1, it * GROUP)
        z = jnp.where(inside, plane, after)
        there = inside | later
        copies = []
        for n, (i, ok) in enumerate(((chunk - 1, chunk_left), (chunk, ~inside), (chunk + 1, chunk_right))):
            part = 2 - n
            copies.append((remote(
                end_b.at[g], chain_land.at[target, part], chain_send.at[g, n], chain_recv.at[target, part],
                chain_device(i, z)), there & ok))
        return copies

    def start_copies():
        copies = []
        for n, (i, part, half, ok) in enumerate((
            (low, 1, 0, True), (low, 2, 1, True), (low - 1, 2, 0, has_left),
            (high, 1, 1, True), (high, 0, 0, True), (high + 1, 0, 1, has_right),
        )):
            copies.append((remote(
                start_b.at[pl.ds(half * T_OWN, T_OWN)], chain_land.at[0, part], start_send.at[n],
                chain_recv.at[0, part], chain_device(i, chain_plane(0))), (tm == 0) & ok))
        return copies

    @pl.when(tm == 0)
    def _():
        for j in range(rows // 4):
            start_b[j] = tile([nodes[4 * j + g, 0:4] for g in range(4)])
        for copy, there in start_copies():
            pl.when(there)(copy.start)

    def window_weights():
        first_unit = 2 * mine - 1
        arrive(cols_land.at[1], cols_recv.at[1])
        arrive(cols_land.at[0], cols_recv.at[0], (mine == 0) & (chip > 0))
        arrive(cols_land.at[3], cols_recv.at[3], (mine == GROUP - 1) & (chip < n_sp // 2 - 1))
        to_scalars = pltpu.make_async_copy(cols_land, cols_s, cols_send.at[3])
        to_scalars.start()
        for at in range(4):
            @pl.when((first_unit + at >= 0) & (first_unit + at < 8))
            def _(at=at):
                copies = unit_copies(0, at, (tm, sp))
                for copy in copies[:3] if at in (0, 3) else copies:
                    copy.wait_recv()

        for n in range(len(PIECES)):
            for at, there in ((0, lower), (3, upper)):
                @pl.when(there)
                def _(n=n, at=at):
                    for copy in piece_copies(n, 0, at, (tm, sp), n):
                        copy.wait_recv()

        to_scalars.wait()

        def places(w, carry):
            unit = first_unit + w // W
            slot, row = (unit + 4) // 4, (unit + 4) % 4 * W + w % W
            for k in range(K):
                column = jnp.where(slot == 2, cols[0, row * K + k], cols_s[slot, 0, row * K + k])
                place_w[w, k] = jnp.clip(column - (chunk * OWN - 2 * W), 0, OWN + 4 * W - 1)
            return carry

        lax.fori_loop(0, WINDOW, places, 0)

        def composed(n, carry):
            for r in range(4):
                w = 4 * n + r
                inverse = win_coarse[w].T
                comp_w[w, BS : 2 * BS] = inverse
                inverse_w[2 * n + r // 2, :, BS * (r % 2) : BS * (r % 2 + 1)] = inverse
                raw = [win_diag[w]] + [win_off[w, k] for k in range(K)]
                got = (dot(jnp.concatenate([block.T for block in raw], axis=0), inverse) * STEP).astype(jnp.bfloat16)
                comp_w[w, :BS] = got[:BS]
                comp_w[w, 2 * BS :] = got[BS:]
            return carry

        lax.fori_loop(0, WINDOW // 4, composed, 0)

    def chain_step(g, carry):
        it, j = g // GROUP, g % GROUP
        from_start = (j == 0) & (group == 0)
        slot = jnp.where(from_start, 0, g)

        fresh_start = ~(from_start & (it == 1))
        main_at = jnp.where(even, 2, 0)
        halo_at = jnp.where(even, 0, 6)

        @pl.when(j == 0)
        def _():
            arrive(chain_land.at[g, 1], chain_recv.at[g, 1], fresh_start)
            for n in range(T_OWN):
                spread(chain_land[slot, 1, n], near, 2 * W + 4 * n, 0)

        arrive(terms_land.at[g, pl.ds(main_at, 6)], terms_recv.at[g, 0])
        arrive(terms_land.at[g, pl.ds(halo_at, 2)], terms_recv.at[g, 1], has_beside)
        arrive(rest_land.at[g], terms_recv.at[g, 2])

        def prepare(n):
            constant = terms_land[g, n].astype(jnp.float32)
            for r in range(4):
                w = 4 * n + r
                own = near[W + w, 0:4]
                change = STEP * react(own, win_rates[pl.ds(w, 1)])
                right_v[w, 0:4] = own + change + constant[4 * r : 4 * r + 4]
                state[w] = own + 0.5 * change
            for i in (2 * n, 2 * n + 1):
                got = paired(right_v[2 * i], right_v[2 * i + 1], inverse_w[i])
                solved[2 * i], solved[2 * i + 1] = got[0][:4], got[1][:4]

        rows_loop(T_EDGE, T_WINDOW - T_EDGE, prepare)

        def with_rest(n):
            constant = rest_land[g, n].astype(jnp.float32)
            for r in range(4):
                state[W + 4 * n + r] += constant[4 * r : 4 * r + 4]

        rows_loop(0, T_OWN, with_rest)

        @pl.when(fresh_start)
        def _():
            arrive(chain_land.at[g, 0], chain_recv.at[g, 0], chunk_left)
            arrive(chain_land.at[g, 2], chain_recv.at[g, 2], chunk_right)

        for n in range(T_OWN):
            spread(chain_land[slot, 0, n], near, 4 * n, 0)
            spread(chain_land[slot, 2, n], near, 2 * W + OWN + 4 * n, 0)

        rows_loop(0, T_EDGE, prepare)
        rows_loop(T_WINDOW - T_EDGE, T_WINDOW, prepare)

        def middle(w):
            spread_s = dot(gather(near, place_w, w), comp_w[w, 2 * BS :])[:4]
            near_q[W + w, 0:4] = solved[w] + spread_s
            partial[w] = 0.5 * spread_s

        rows_loop(0, WINDOW, middle)

        def end(o):
            w = W + o
            own, mid = near[W + w, 0:4], near_q[W + w, 0:4]
            right = state[w] + HALF * react(mid, win_rates[pl.ds(w, 1)])
            parts = jnp.concatenate([0.5 * (own - mid), right, 0.5 * gather(near_q, place_w, w)[:4]], axis=1)
            near[W + w, 0:4] = partial[w] + dot(parts, comp_w[w])

        rows_loop(0, OWN, end)
        for n in range(T_OWN):
            end_b[g, n] = tile([near[2 * W + 4 * n + r, 0:4] for r in range(4)])
        for copy, there in chain_copies(it, j):
            pl.when(there)(copy.start)
        for copy, there in value_copies(it, j):
            if there is True:
                copy.start()
            else:
                pl.when(there)(copy.start)
        return carry

    def round_of(it, carry):
        fine(it)

        @pl.when((it == 0) & (plane != first_plane))
        def _():
            pieces(False, lambda copy: copy.start())
            weights_out()

        @pl.when(on_chain & ((group < 2) == (it == 0)))
        def _():
            window_weights()
            lax.fori_loop(0, ITERS * GROUP, chain_step, 0)

        return carry

    lax.fori_loop(0, ITERS, round_of, 0)

    pl.when(tm > 0)(lambda: values_wait(1, 0, False))
    values_wait(1, 1, False)

    def write(j):
        ends = value_land[1, 1, j].astype(jnp.float32)
        starts = value_land[1, 0, j].astype(jnp.float32)
        for g in range(4):
            b = 4 * j + g
            own = jnp.where(tm == 0, start[:, cells(b)], starts[4 * g : 4 * g + 4])
            last = ends[4 * g : 4 * g + 4]
            out[0, 0, :, cells(b)] = own
            out[0, 1, :, cells(b)] = mid_b[b] + 0.5 * (own + last)
            out[0, 2, :, cells(b)] = last

    rows_loop(0, rows // 4, write)

    weights_sent()
    for early in (True, False):
        pieces(early, lambda copy: copy.wait_send())
    for copy, there in start_copies():
        pl.when(there)(copy.wait_send)
    for it in range(ITERS):
        for copy, there in terms_copies(it):
            if there is True:
                copy.wait_send()
            else:
                pl.when(there)(copy.wait_send)

    @pl.when(on_chain)
    def _():
        def sent(g, carry):
            it, j = g // GROUP, g % GROUP
            for copy, there in chain_copies(it, j) + value_copies(it, j):
                if there is True:
                    copy.wait_send()
                else:
                    pl.when(there)(copy.wait_send)
            return carry

        lax.fori_loop(0, ITERS * GROUP, sent, 0)


def shards(n_tm, n_sp, start, guess, diag, off, columns, rates, mixing, fine, coarse):
    rows = diag.shape[0]
    f32, bf16 = jnp.float32, jnp.bfloat16
    vmem = pl.BlockSpec(memory_space=pltpu.VMEM)
    hbm = pl.BlockSpec(memory_space=pltpu.HBM)
    dma = pltpu.SemaphoreType.DMA
    edge = W // 4
    slots = ITERS * GROUP

    def tiles(*lead):
        return pltpu.VMEM((*lead, 16, BS), bf16)

    def blocks(*lead):
        return pltpu.VMEM((*lead, BS, BS), bf16)

    pairs = pltpu.VMEM((rows // 2, BS, 2 * BS), bf16)
    scratch = [
        pltpu.VMEM((SPECIES, rows * BS), f32), pltpu.VMEM((1, SPECIES, rows * BS), f32),
        pltpu.SMEM((1, rows * K), jnp.int32), pltpu.VMEM((rows, BS), f32), pltpu.VMEM((SPECIES, SPECIES), f32),
        blocks(rows), blocks(rows, K), blocks(rows),
        pltpu.VMEM((rows, K * BS, BS), bf16), pairs, pairs,
        blocks(WINDOW), blocks(WINDOW, K), blocks(WINDOW), pltpu.VMEM((WINDOW, BS), f32),
        pltpu.VMEM((WINDOW, (K + 2) * BS, BS), bf16),
        pltpu.VMEM((WINDOW // 2, BS, 2 * BS), bf16),
        pltpu.VMEM((rows + 2 * W, 8, BS), f32), pltpu.VMEM((rows + 2 * W, 8, BS), f32),
        pltpu.VMEM((SPECIES, 8, BS), f32), pltpu.VMEM((rows, 8, BS), f32),
        *[pltpu.VMEM((rows, SPECIES, BS), f32)] * 11, pltpu.VMEM((rows, 8, BS), f32),
        tiles(3, 2, 2 * edge), tiles(3, 2, 2 * edge),
        tiles(ITERS, rows // 2), tiles(slots, T_WINDOW), tiles(slots, T_OWN),
        tiles(rows // 4), tiles(slots, 3, T_OWN), tiles(slots, T_OWN),
        tiles(ITERS, 2, rows // 4), tiles(2, 2, edge),
        pltpu.VMEM((4, 1, BS), jnp.int32), pltpu.SMEM((4, 1, BS), jnp.int32),
        pltpu.SMEM((rows, K), jnp.int32), pltpu.SMEM((WINDOW, K), jnp.int32),
        dma((8,)), dma((3, 2)), dma((3, 2)), dma((4, 4)), dma((4, 4)), dma((4,)), dma((4,)),
        dma((2 * len(PIECES), 3)), dma((len(PIECES), 3)),
        dma((ITERS, 6)), dma((slots, 3)), dma((6,)), dma((slots, 3)), dma((slots, 3)),
        dma((slots, 2, 2)), dma((ITERS, 2, 4)),
    ]
    return pl.pallas_call(
        functools.partial(kernel, n_tm, n_sp, rows),
        out_shape=jax.ShapeDtypeStruct((1, 3, SPECIES, rows * BS), f32),
        in_specs=[hbm] * 9,
        out_specs=vmem,
        scratch_shapes=scratch,
        compiler_params=pltpu.CompilerParams(
            collective_id=0, has_side_effects=True, vmem_limit_bytes=60 << 20
        ),
    )(start, guess, columns.reshape(1, rows * K), rates.reshape(rows, BS), mixing, diag, off, fine, coarse)


def solution(mesh):
    in_specs = (
        P(None, "space"),
        P("tm", None, "space"),
        P("space", None, None),
        P("space", None, None, None),
        P("space", None),
        P("space"),
        P(),
        P("space", None, None),
        P("space", None, None),
    )
    out_specs = P("tm", None, None, "space")
    body = functools.partial(shards, mesh.shape["tm"], mesh.shape["space"])
    return jax.shard_map(body, mesh=mesh, in_specs=in_specs, out_specs=out_specs, check_vma=False)
```

```python
import functools

import jax
import jax.numpy as jnp
from jax import lax
from jax.experimental import pallas as pl
from jax.experimental.pallas import tpu as pltpu
from jax.sharding import PartitionSpec as P

BS = 128
K = 4
SPECIES = 4
ITERS = 2
W = 8
STEP = 0.25
HALF = STEP / 2
MESH = pl.DeviceIdType.MESH
NODES, FIRST, SECOND = range(3)
LEFT, RIGHT = 0, 1
GROUP = 4
OWN = 16
WINDOW = OWN + 2 * W
T_OWN, T_WINDOW, T_EDGE = OWN // 4, WINDOW // 4, W // 4
PIECES = ((0, 1), (1, 2), (3, 1), (4, 2), (6, 2))
FIRST_FROM = ((0, 0), (0, 1), (0, GROUP - 1), (1, 0), (GROUP - 1, 0))
OTHERS_FROM = ((0, 0), (0, 1), (0, GROUP - 1), (0, 0), (0, GROUP - 1))


def dot(lhs, rhs):
    return lax.dot_general(
        lhs.astype(jnp.bfloat16), rhs, (((1,), (0,)), ((), ())), preferred_element_type=jnp.float32
    )


def rows_loop(first, last, body):
    def step(i, carry):
        body(i)
        return carry

    lax.fori_loop(first, last, step, 0, unroll=True)


def kernel(
    n_tm, n_sp, rows,
    start_h, guess_h, cols_h, rates_h, mixing_h, diag_h, off_h, fine_h, coarse_h,
    out,
    start, guess, cols, rates, mixing,
    diag_v, off_v, fine_v, raw_w, diag_w, fine_w, win_diag, win_off, win_coarse, win_rates, comp_w, inverse_w,
    near, near_q, mix_v, nodes, imp_b, exp_b, mid_b, first_v, second_r,
    sum_c, sum_t, state, solved, partial, fresh, right_v,
    send_b, land, terms_b, terms_land, rest_land, start_b, chain_land, end_b, value_land, value_halo,
    cols_land, cols_s, place_of, place_w,
    load_sem, send_sem, recv_sem, unit_send, unit_recv, cols_send, cols_recv, piece_send, piece_recv,
    terms_send, terms_recv, start_send, chain_send, chain_recv, value_send, value_recv,
):
    tm = lax.axis_index("tm")
    sp = lax.axis_index("space")
    plane, line, chip, core = tm // GROUP, tm % GROUP, sp // 2, sp % 2
    has_left, has_right = sp > 0, sp < n_sp - 1
    edge = W // 4
    chunks = n_sp * rows // OWN

    def quarter(x, y):
        return jnp.where(x % 2 == 0, y, GROUP - 1 - y)

    def chain_device(i, z):
        x, j = i // GROUP, i % GROUP
        return z * GROUP + quarter(x, j), 2 * x + 1

    def chain_plane(group):
        return (group + 2) % GROUP

    mine = quarter(chip, line)
    chunk = GROUP * chip + mine
    group = (plane + 2) % GROUP
    on_chain = core == 1
    even = chunk % 2 == 0
    chunk_left, chunk_right = chunk > 0, chunk < chunks - 1
    owner = chunk // 2
    beside = jnp.where(even, owner - 1, owner + 1)
    has_beside = (even & chunk_left) | (~even & chunk_right)
    low, high = 2 * sp, 2 * sp + 1

    def remote(src, dst, out_sem, in_sem, device):
        return pltpu.make_async_remote_copy(
            src_ref=src, dst_ref=dst, send_sem=out_sem, recv_sem=in_sem,
            device_id=device, device_id_type=MESH,
        )

    def arrive(dst, in_sem, there=None):
        def wait():
            remote(dst, dst, send_sem.at[0, 0], in_sem, (tm, sp)).wait_recv()

        if there is None:
            wait()
        else:
            pl.when(there)(wait)

    loads = [
        pltpu.make_async_copy(src, dst, load_sem.at[i])
        for i, (src, dst) in enumerate((
            (mixing_h, mixing), (guess_h, guess), (start_h, start), (cols_h, cols), (rates_h, rates),
            (diag_h, diag_v), (off_h, off_v), (fine_h, fine_v),
        ))
    ]
    for load in loads:
        load.start()
    small, large = loads[:5], loads[5:]
    cols_land[...] = jnp.zeros_like(cols_land)

    barrier = pltpu.get_barrier_semaphore()
    my_plane = chain_plane(plane)
    later, before = group < GROUP - 1, group > 0
    after, earlier = (plane + 1) % GROUP, (plane + GROUP - 1) % GROUP
    senders, receivers = [], []

    def both(device, there):
        senders.append((device, there))
        receivers.append(there)

    both((tm, sp - 1), has_left)
    both((tm, sp + 1), has_right)
    for i, there in ((low - 1, has_left), (low, True), (high, True), (high + 1, has_right)):
        both(chain_device(i, my_plane), there)
        senders.append((chain_device(i, chain_plane(plane + GROUP - 1)), there & (line == 0) & (plane > 0)))
    for y in range(GROUP):
        both((group * GROUP + y, owner), on_chain)
        both((group * GROUP + y, beside), on_chain & has_beside)
    receivers.append(on_chain & later)
    receivers.append(on_chain & later & has_beside)
    both(chain_device(chunk - 1, plane), on_chain & chunk_left)
    both(chain_device(chunk + 1, plane), on_chain & chunk_right)
    for i, there in ((chunk, True), (chunk - 1, chunk_left), (chunk + 1, chunk_right)):
        senders.append((chain_device(i, earlier), on_chain & before & there))
        receivers.append(on_chain & later & there)

    first_plane = chain_plane(0)
    lower = on_chain & (mine == 0) & (chip > 0)
    upper = on_chain & (mine == GROUP - 1) & (chip < n_sp // 2 - 1)

    def piece_sources(n):
        t_first, t_others = (
            (plane + dz) % GROUP * GROUP + (line + dy) % GROUP for dz, dy in (FIRST_FROM[n], OTHERS_FROM[n])
        )
        t = jnp.where(plane == first_plane, t_first, t_others)
        return ((t, sp - 2), lower), ((t, sp + 1), upper)

    def piece_targets(n, when):
        dz, dy = OTHERS_FROM[n] if when else FIRST_FROM[n]
        z, y = (plane + GROUP - dz) % GROUP, (line + GROUP - dy) % GROUP
        t = z * GROUP + y
        hurried = z == 0
        fits = z == first_plane if when == 0 else (z != first_plane) & ~hurried if when == 1 else hurried
        right = on_chain & (chip < n_sp // 2 - 1) & (quarter(chip + 1, y) == 0)
        left = ~on_chain & (chip > 0) & (quarter(chip - 1, y) == GROUP - 1)
        return ((t, sp + 2), fits & right, 3, 0), ((t, sp - 1), fits & left, 0, 3)

    for n in range(len(PIECES)):
        senders.extend(piece_sources(n))
        for when in range(3):
            receivers.extend(there for _, there, _, _ in piece_targets(n, when))

    for device, there in senders:
        def signal(device=device):
            pl.semaphore_signal(barrier, inc=1, device_id=device, device_id_type=MESH)

        pl.when(there)(signal)

    for load in small:
        load.wait()

    def cells(b):
        return pl.ds(pl.multiple_of(b * BS, BS), BS)

    def begin(b):
        own = guess[0, :, cells(b)]
        nodes[b, 0:4] = jnp.where(tm == 0, start[:, cells(b)], own)
        nodes[b, 4:8] = own

    rows_loop(0, rows, begin)

    pl.semaphore_wait(barrier, sum(jnp.asarray(there).astype(jnp.int32) for there in receivers))

    def unit_copies(unit, at, device):
        src, dst = pl.ds(unit * W, W), pl.ds(pl.multiple_of(at * W, W), W)
        pairs = ((off_h, win_off), (coarse_h, win_coarse), (rates_h, win_rates), (diag_h, win_diag))
        copies = []
        for n, (a, b) in enumerate(pairs):
            if device is None:
                copies.append(pltpu.make_async_copy(a.at[src], b.at[dst], unit_recv.at[at, n]))
            else:
                copies.append(remote(a.at[src], b.at[dst], unit_send.at[unit, n], unit_recv.at[at, n], device))
        return copies

    def unit_plan():
        plan = []
        for unit in range(4):
            at = unit - 2 * mine + 1
            plan.append((unit, at, (tm, sp + 1), (core == 0) & (at >= 0) & (at < 4)))
            at = unit + 4 - 2 * mine + 1
            plan.append((unit, at, None, on_chain & (at >= 0) & (at < 4)))
        return plan

    def piece_copies(n, unit, at, device, row):
        first, count = PIECES[n]
        src, dst = pl.ds(unit * W + first, count), pl.ds(at * W + first, count)
        copies = [
            remote(off_h.at[src], win_off.at[dst], piece_send.at[row, 0], piece_recv.at[n, 0], device),
            remote(coarse_h.at[src], win_coarse.at[dst], piece_send.at[row, 1], piece_recv.at[n, 1], device),
        ]
        if n == 0:
            src, dst = pl.ds(unit * W, W), pl.ds(at * W, W)
            copies.append(remote(rates_h.at[src], win_rates.at[dst], piece_send.at[row, 2], piece_recv.at[n, 2], device))
        return copies

    def pieces(when, act):
        for n in range(len(PIECES)):
            for device, there, unit, at in piece_targets(n, when):
                def go(n=n, unit=unit, at=at, device=device):
                    for copy in piece_copies(n, unit, at, device, n + when * len(PIECES)):
                        act(copy)

                pl.when(there)(go)

    def cols_copy(which):
        slot, device = ((1, (tm, sp + 1)), (3, (tm, sp - 1)), (0, (tm, sp + 2)))[which]
        return remote(cols_h, cols_land.at[slot], cols_send.at[which], cols_recv.at[slot], device)

    def cols_plan():
        next_low = quarter(chip + 1, line) == 0
        last_high = quarter(chip - 1, line) == GROUP - 1
        return (
            (0, core == 0),
            (1, (core == 0) & (chip > 0) & last_high),
            (2, on_chain & (chip < n_sp // 2 - 1) & next_low),
        )

    def weights_out():
        for which, there in cols_plan():
            pl.when(there)(cols_copy(which).start)
        for unit, at, device, there in unit_plan():
            def go(unit=unit, at=at, device=device):
                copies = unit_copies(unit, at, device)
                for copy in copies[:3]:
                    copy.start()
                pl.when((at == 1) | (at == 2))(copies[3].start)

            pl.when(there)(go)

    def weights_sent():
        for which, there in cols_plan():
            pl.when(there)(cols_copy(which).wait_send)
        for unit, at, device, there in unit_plan():
            if device is None:
                continue

            def done(unit=unit, at=at, device=device):
                copies = unit_copies(unit, at, device)
                for copy in copies[:3]:
                    copy.wait_send()
                pl.when((at == 1) | (at == 2))(copies[3].wait_send)

            pl.when(there)(done)


    def halo_copies(kind, count):
        to_left = remote(
            send_b.at[kind, LEFT, pl.ds(0, count)], land.at[kind, RIGHT, pl.ds(0, count)],
            send_sem.at[kind, LEFT], recv_sem.at[kind, RIGHT], (tm, sp - 1),
        )
        to_right = remote(
            send_b.at[kind, RIGHT, pl.ds(0, count)], land.at[kind, LEFT, pl.ds(0, count)],
            send_sem.at[kind, RIGHT], recv_sem.at[kind, LEFT], (tm, sp + 1),
        )
        return to_left, to_right

    def tile(values):
        return jnp.concatenate(values, axis=0).astype(jnp.bfloat16)

    def halo_send(kind, fields):
        for f, field in enumerate(fields):
            for j in range(edge):
                send_b[kind, LEFT, f * edge + j] = tile([field(4 * j + g) for g in range(4)])
                send_b[kind, RIGHT, f * edge + j] = tile([field(rows - W + 4 * j + g) for g in range(4)])
        to_left, to_right = halo_copies(kind, edge * len(fields))
        pl.when(has_left)(to_left.start)
        pl.when(has_right)(to_right.start)

    def halo_wait(kind, count):
        to_left, to_right = halo_copies(kind, edge * count)

        @pl.when(has_left)
        def _():
            to_right.wait_recv()
            to_left.wait_send()

        @pl.when(has_right)
        def _():
            to_left.wait_recv()
            to_right.wait_send()

    def spread(block_tile, target, block, row):
        wide = block_tile.astype(jnp.float32)
        for g in range(4):
            target[block + g, row : row + 4] = wide[4 * g : 4 * g + 4]

    def halo_place(kind, target, count):
        for f in range(count):
            for j in range(edge):
                spread(land[kind, LEFT, f * edge + j], target, 4 * j, 4 * f)
                spread(land[kind, RIGHT, f * edge + j], target, W + rows + 4 * j, 4 * f)

    def gather(source, places, b):
        return jnp.concatenate([source[places[b, k]] for k in range(K)], axis=1)

    def react(v, rate):
        total = None
        for t in range(SPECIES):
            line_t = v[t : t + 1]
            if v.shape[0] == 8:
                second = v[4 + t : 5 + t]
                row = lax.broadcasted_iota(jnp.int32, (8, BS), 0)
                line_t = jnp.where(row < 4, jnp.broadcast_to(line_t, (8, BS)), jnp.broadcast_to(second, (8, BS)))
            term = mix_v[t, : v.shape[0]] * line_t
            total = term if total is None else total + term
        return total * rate

    def paired(first, second, weights):
        got = dot(jnp.concatenate([first, second], axis=0), weights)
        return got[:8, :BS], got[8:, BS:]

    def explicit(b, count):
        got = dot(gather(near, place_of, b), raw_w[b])[: 4 * count]
        return got + react(near[W + b, : 4 * count], rates[pl.ds(b, 1)])

    def transposed(n, carry):
        for r in range(4):
            b, half = 4 * n + r, pl.ds(BS * (r % 2), BS)
            diag_w[2 * n + r // 2, :, half] = diag_v[b].T
            fine_w[2 * n + r // 2, :, half] = fine_v[b].T
            for k in range(K):
                raw_w[b, BS * k : BS * (k + 1)] = off_v[b, k].T
        return carry

    def outer(*bodies):
        for body in bodies:
            rows_loop(0, W // 2, body)
            rows_loop((rows - W) // 2, rows // 2, body)

    def inner(*bodies):
        for body in bodies:
            rows_loop(W // 2, (rows - W) // 2, body)

    def solve(target):
        def pair(i):
            got = paired(right_v[2 * i], right_v[2 * i + 1], fine_w[i])
            target[2 * i], target[2 * i + 1] = got[0][:4], got[1][:4]

        return pair

    def terms_copies(it):
        slot = it * GROUP + line
        main, rest = terms_land.at[slot], rest_land.at[slot]
        to = [chain_device(i, my_plane) for i in (low, high, low - 1, high + 1)]

        def piece(first, count, dst, n, sem, device):
            return remote(
                terms_b.at[it, pl.ds(first, count)], dst, terms_send.at[it, n], terms_recv.at[slot, sem], device
            )

        t_rows = rows // 4
        return (
            (piece(0, 6, main.at[pl.ds(2, 6)], 0, 0, to[0]), True),
            (piece(2, 6, main.at[pl.ds(0, 6)], 1, 0, to[1]), True),
            (piece(0, 2, main.at[pl.ds(6, 2)], 2, 1, to[2]), has_left),
            (piece(6, 2, main.at[pl.ds(0, 2)], 3, 1, to[3]), has_right),
            (piece(t_rows, T_OWN, rest, 4, 2, to[0]), True),
            (piece(t_rows + T_OWN, T_OWN, rest, 5, 2, to[1]), True),
        )

    def terms_sent(it):
        for copy, there in terms_copies(it):
            if there is True:
                copy.wait_send()
            else:
                pl.when(there)(copy.wait_send)

    def fine(it):
        @pl.when(it == 0)
        def _():
            halo_send(NODES, [lambda b: nodes[b, 0:4], lambda b: nodes[b, 4:8]])
            first_things()
            for load in large:
                load.wait()
            lax.fori_loop(0, rows // 4, transposed, 0)
            halo_wait(NODES, 2)
            halo_place(NODES, near, 2)

        @pl.when(it == 1)
        def _():
            @pl.when(tm > 0)
            def _():
                values_wait(0, 0, True)
                for j in range(rows // 4):
                    spread(value_land[0, 0, j], nodes, 4 * j, 0)
                for j in range(edge):
                    spread(value_halo[0, LEFT, j], near, 4 * j, 0)
                    spread(value_halo[0, RIGHT, j], near, W + rows + 4 * j, 0)

            @pl.when(tm == 0)
            def _():
                for j in range(edge):
                    spread(land[NODES, LEFT, j], near, 4 * j, 0)
                    spread(land[NODES, RIGHT, j], near, W + rows + 4 * j, 0)

            values_wait(0, 1, True)
            for j in range(rows // 4):
                spread(value_land[0, 1, j], nodes, 4 * j, 4)
            for j in range(edge):
                spread(value_halo[1, LEFT, j], near, 4 * j, 4)
                spread(value_halo[1, RIGHT, j], near, W + rows + 4 * j, 4)

        def place(b):
            near[W + b] = nodes[b]

        rows_loop(0, rows, place)
        own_part = jnp.where(it == 0, 0.0, 0.5)
        end_part = jnp.where(it == 0, 1.0, 0.5)

        def node_terms(i):
            imps = paired(near[W + 2 * i], near[W + 2 * i + 1], diag_w[i])
            for b, imp in zip((2 * i, 2 * i + 1), imps):
                exp = explicit(b, 2)
                imp_0, exp_0, imp_2, exp_2 = imp[:4], exp[:4], imp[4:], exp[4:]
                one_i = imp_b[b] + own_part * imp_0 + end_part * imp_2
                one_e = exp_b[b] + own_part * exp_0 + end_part * exp_2
                f_0, f_1, f_2 = imp_0 + exp_0, one_i + one_e, imp_2 + exp_2
                right_v[b, 0:4] = (
                    nodes[b, 0:4] - HALF * one_i + STEP * (5 / 24 * f_0 + 1 / 3 * f_1 - 1 / 24 * f_2)
                )
                second_r[b] = STEP * (-1 / 24 * f_0 + 1 / 3 * f_1 + 5 / 24 * f_2) - HALF * (one_e + imp_2)
                sum_c[b] = STEP * (1 / 6 * f_0 - exp_0)
                sum_t[b] = (-STEP / 3) * f_0
                imp_b[b] = -0.5 * imp_0
                exp_b[b] = -0.5 * exp_0

        outer(node_terms, solve(first_v))
        halo_send(FIRST, [lambda b: first_v[b]])
        inner(node_terms, solve(first_v))

        def put_first(b):
            near[W + b, 0:4] = first_v[b]

        rows_loop(0, rows, put_first)
        early_units(it, 0)
        halo_wait(FIRST, 1)
        halo_place(FIRST, near, 1)

        def first_terms(i):
            imps = paired(near[W + 2 * i], near[W + 2 * i + 1], diag_w[i])
            for b, imp in zip((2 * i, 2 * i + 1), imps):
                imp = imp[:4]
                exp = explicit(b, 1)
                force = STEP * 2 / 3 * (imp + exp)
                right_v[b, 0:4] = first_v[b] + HALF * exp + second_r[b]
                sum_c[b] += force
                sum_t[b] += force
                imp_b[b] += imp
                exp_b[b] += exp

        outer(first_terms, solve(fresh))
        halo_send(SECOND, [lambda b: fresh[b]])
        inner(first_terms, solve(fresh))

        def put_second(b):
            near[W + b, 0:4] = fresh[b]
            mid_b[b] = first_v[b] - 0.5 * (nodes[b, 0:4] + fresh[b])

        rows_loop(0, rows, put_second)

        def second_terms(i):
            imps = paired(near[W + 2 * i], near[W + 2 * i + 1], diag_w[i])
            for b, imp in zip((2 * i, 2 * i + 1), imps):
                imp = imp[:4]
                exp = explicit(b, 1)
                force = imp + exp
                sum_c[b] += STEP * (1 / 6 * force - imp)
                sum_t[b] += (-STEP / 3) * force
                imp_b[b] += -0.5 * imp
                exp_b[b] += -0.5 * exp

        inner(second_terms)
        early_units(it, 1)
        halo_wait(SECOND, 1)
        halo_place(SECOND, near, 1)
        outer(second_terms)
        for j in range(rows // 4):
            terms_b[it, j] = tile([sum_c[4 * j + g] for g in range(4)])
            terms_b[it, rows // 4 + j] = tile([sum_t[4 * j + g] for g in range(4)])
        for copy, there in terms_copies(it):
            if there is True:
                copy.start()
            else:
                pl.when(there)(copy.start)

    def values_wait(it, which, halos):
        for n in range(2):
            arrive(value_land.at[it, which, pl.ds(n * T_OWN, T_OWN)], value_recv.at[it, which, n])
        if halos:
            arrive(value_halo.at[which, LEFT], value_recv.at[it, which, 2], has_left)
            arrive(value_halo.at[which, RIGHT], value_recv.at[it, which, 3], has_right)

    def value_copies(it, j):
        g = it * GROUP + j
        p = group * GROUP + j
        half = chunk % 2
        copies = []
        for which in (1, 0):
            t = p + 1 - which
            there = (p < n_tm - 1) if which == 0 else True
            copies.append((remote(
                end_b.at[g], value_land.at[it, which, pl.ds(pl.multiple_of(half * T_OWN, T_OWN), T_OWN)],
                value_send.at[g, which, 0], value_recv.at[it, which, half], (t, owner)), there))
            copies.append((remote(
                end_b.at[g, pl.ds(pl.multiple_of(half * (T_OWN - T_EDGE), T_EDGE), T_EDGE)], value_halo.at[which, 1 - half],
                value_send.at[g, which, 1], value_recv.at[it, which, 3 - half], (t, beside)),
                there & has_beside & (it == 0)))
        return copies

    def chain_copies(it, j):
        g = it * GROUP + j
        inside = j < GROUP - 1
        target = jnp.where(inside, g + 1, it * GROUP)
        z = jnp.where(inside, plane, after)
        there = inside | later
        copies = []
        for n, (i, ok) in enumerate(((chunk - 1, chunk_left), (chunk, ~inside), (chunk + 1, chunk_right))):
            part = 2 - n
            copies.append((remote(
                end_b.at[g], chain_land.at[target, part], chain_send.at[g, n], chain_recv.at[target, part],
                chain_device(i, z)), there & ok))
        return copies

    def start_copies():
        copies = []
        for n, (i, part, half, ok) in enumerate((
            (low, 1, 0, True), (low, 2, 1, True), (low - 1, 2, 0, has_left),
            (high, 1, 1, True), (high, 0, 0, True), (high + 1, 0, 1, has_right),
        )):
            copies.append((remote(
                start_b.at[pl.ds(half * T_OWN, T_OWN)], chain_land.at[0, part], start_send.at[n],
                chain_recv.at[0, part], chain_device(i, chain_plane(0))), (tm == 0) & ok))
        return copies

    def first_things():
        pieces(0, lambda copy: copy.start())
        pl.when(plane == first_plane)(weights_out)
        def local_place(b, carry):
            for k in range(K):
                place_of[b, k] = jnp.clip(cols[k, b] - (sp * rows - W), 0, rows + 2 * W - 1)
            return carry

        lax.fori_loop(0, rows, local_place, 0)
        near[...] = jnp.zeros_like(near)
        near_q[...] = jnp.zeros_like(near_q)
        imp_b[...] = jnp.zeros_like(imp_b)
        exp_b[...] = jnp.zeros_like(exp_b)
        for t in range(SPECIES):
            column = jnp.broadcast_to(mixing[:, t : t + 1], (SPECIES, BS))
            mix_v[t] = jnp.concatenate([column, column], axis=0)

        @pl.when(tm == 0)
        def _():
            for j in range(rows // 4):
                start_b[j] = tile([nodes[4 * j + g, 0:4] for g in range(4)])
            for copy, there in start_copies():
                pl.when(there)(copy.start)

    def composed(n, carry):
        for r in range(4):
            w = 4 * n + r
            inverse = win_coarse[w].T
            comp_w[w, BS : 2 * BS] = inverse
            inverse_w[2 * n + r // 2, :, BS * (r % 2) : BS * (r % 2 + 1)] = inverse
            raw = [win_diag[w]] + [win_off[w, k] for k in range(K)]
            got = (dot(jnp.concatenate([block.T for block in raw], axis=0), inverse) * STEP).astype(jnp.bfloat16)
            comp_w[w, :BS] = got[:BS]
            comp_w[w, 2 * BS :] = got[BS:]
        return carry

    def window_unit(at, foreign=True):
        unit = 2 * mine - 1 + at

        @pl.when((unit >= 0) & (unit < 8))
        def _():
            copies = unit_copies(0, at, (tm, sp))
            for copy in copies[:3] if at in (0, 3) else copies:
                copy.wait_recv()

        if at in (0, 3) and foreign:
            there = lower if at == 0 else upper
            for n in range(len(PIECES)):
                @pl.when(there)
                def _(n=n):
                    for copy in piece_copies(n, 0, at, (tm, sp), n):
                        copy.wait_recv()

        lax.fori_loop(W // 4 * at, W // 4 * (at + 1), composed, 0)

    def window_places():
        first_unit = 2 * mine - 1
        arrive(cols_land.at[1], cols_recv.at[1])
        arrive(cols_land.at[0], cols_recv.at[0], lower)
        arrive(cols_land.at[3], cols_recv.at[3], upper)
        to_scalars = pltpu.make_async_copy(cols_land, cols_s, cols_send.at[3])
        to_scalars.start()
        to_scalars.wait()

        def places(w, carry):
            unit = first_unit + w // W
            slot, row = (unit + 4) // 4, (unit + 4) % 4 * W + w % W
            for k in range(K):
                column = jnp.where(slot == 2, cols[k, row], cols_s[slot, k, row])
                place_w[w, k] = jnp.clip(column - (chunk * OWN - 2 * W), 0, OWN + 4 * W - 1)
            return carry

        lax.fori_loop(0, WINDOW, places, 0)

    hurry = on_chain & (plane == first_plane)

    def early_units(it, step):
        @pl.when((it == 0) & hurry)
        def _():
            if step == 0:
                window_places()
                window_unit(1)
            else:
                window_unit(2)
                pl.when(mine != GROUP - 1)(functools.partial(window_unit, 3, False))
                pl.when(mine == GROUP - 1)(functools.partial(window_unit, 0, False))

    def window_weights():
        @pl.when(~hurry)
        def _():
            window_places()
            for at in range(4):
                window_unit(at)

        @pl.when(hurry)
        def _():
            pl.when(mine == GROUP - 1)(functools.partial(window_unit, 3))
            pl.when(mine != GROUP - 1)(functools.partial(window_unit, 0))

    def chain_step(g, carry):
        it, j = g // GROUP, g % GROUP
        from_start = (j == 0) & (group == 0)
        slot = jnp.where(from_start, 0, g)

        fresh_start = ~(from_start & (it == 1))
        main_at = jnp.where(even, 2, 0)
        halo_at = jnp.where(even, 0, 6)

        @pl.when(j == 0)
        def _():
            arrive(chain_land.at[g, 1], chain_recv.at[g, 1], fresh_start)
            for n in range(T_OWN):
                spread(chain_land[slot, 1, n], near, 2 * W + 4 * n, 0)

        arrive(terms_land.at[g, pl.ds(main_at, 6)], terms_recv.at[g, 0])
        arrive(terms_land.at[g, pl.ds(halo_at, 2)], terms_recv.at[g, 1], has_beside)
        arrive(rest_land.at[g], terms_recv.at[g, 2])

        def prepare(n):
            constant = terms_land[g, n].astype(jnp.float32)
            for r in range(4):
                w = 4 * n + r
                own = near[W + w, 0:4]
                change = STEP * react(own, win_rates[pl.ds(w, 1)])
                right_v[w, 0:4] = own + change + constant[4 * r : 4 * r + 4]
                state[w] = own + 0.5 * change
            for i in (2 * n, 2 * n + 1):
                got = paired(right_v[2 * i], right_v[2 * i + 1], inverse_w[i])
                solved[2 * i], solved[2 * i + 1] = got[0][:4], got[1][:4]

        rows_loop(T_EDGE, T_WINDOW - T_EDGE, prepare)

        def with_rest(n):
            constant = rest_land[g, n].astype(jnp.float32)
            for r in range(4):
                state[W + 4 * n + r] += constant[4 * r : 4 * r + 4]

        rows_loop(0, T_OWN, with_rest)

        @pl.when(fresh_start)
        def _():
            arrive(chain_land.at[g, 0], chain_recv.at[g, 0], chunk_left)
            arrive(chain_land.at[g, 2], chain_recv.at[g, 2], chunk_right)

        for n in range(T_OWN):
            spread(chain_land[slot, 0, n], near, 4 * n, 0)
            spread(chain_land[slot, 2, n], near, 2 * W + OWN + 4 * n, 0)

        rows_loop(0, T_EDGE, prepare)
        rows_loop(T_WINDOW - T_EDGE, T_WINDOW, prepare)

        def middle(w):
            spread_s = dot(gather(near, place_w, w), comp_w[w, 2 * BS :])[:4]
            near_q[W + w, 0:4] = solved[w] + spread_s
            partial[w] = 0.5 * spread_s

        rows_loop(0, WINDOW, middle)

        def end(o):
            w = W + o
            own, mid = near[W + w, 0:4], near_q[W + w, 0:4]
            right = state[w] + HALF * react(mid, win_rates[pl.ds(w, 1)])
            parts = jnp.concatenate([0.5 * (own - mid), right, 0.5 * gather(near_q, place_w, w)[:4]], axis=1)
            near[W + w, 0:4] = partial[w] + dot(parts, comp_w[w])

        rows_loop(0, OWN, end)
        for n in range(T_OWN):
            end_b[g, n] = tile([near[2 * W + 4 * n + r, 0:4] for r in range(4)])
        for copy, there in chain_copies(it, j):
            pl.when(there)(copy.start)
        for copy, there in value_copies(it, j):
            if there is True:
                copy.start()
            else:
                pl.when(there)(copy.start)
        return carry

    def round_of(it, carry):
        fine(it)

        @pl.when(it == 0)
        def _():
            terms_sent(0)
            pieces(1, lambda copy: copy.start())
            pieces(2, lambda copy: copy.start())
            pl.when(plane != first_plane)(weights_out)

        composes = jnp.where((plane == 0) & (line == 0), 1, 0)
        pl.when(on_chain & (it == composes))(window_weights)

        @pl.when(on_chain & ((group < 2) == (it == 0)))
        def _():
            lax.fori_loop(0, ITERS * GROUP, chain_step, 0)

        return carry

    lax.fori_loop(0, ITERS, round_of, 0)

    weights_sent()
    for when in range(3):
        pieces(when, lambda copy: copy.wait_send())
    for copy, there in start_copies():
        pl.when(there)(copy.wait_send)
    terms_sent(1)

    @pl.when(on_chain)
    def _():
        def sent(g, carry):
            it, j = g // GROUP, g % GROUP
            for copy, there in chain_copies(it, j) + value_copies(it, j):
                if there is True:
                    copy.wait_send()
                else:
                    pl.when(there)(copy.wait_send)
            return carry

        lax.fori_loop(0, ITERS * GROUP, sent, 0)

    pl.when(tm > 0)(lambda: values_wait(1, 0, False))
    values_wait(1, 1, False)

    def write(j):
        ends = value_land[1, 1, j].astype(jnp.float32)
        starts = value_land[1, 0, j].astype(jnp.float32)
        for g in range(4):
            b = 4 * j + g
            own = jnp.where(tm == 0, start[:, cells(b)], starts[4 * g : 4 * g + 4])
            last = ends[4 * g : 4 * g + 4]
            out[0, 0, :, cells(b)] = own
            out[0, 1, :, cells(b)] = mid_b[b] + 0.5 * (own + last)
            out[0, 2, :, cells(b)] = last

    rows_loop(0, rows // 4, write)


def shards(n_tm, n_sp, start, guess, diag, off, columns, rates, mixing, fine, coarse):
    rows = diag.shape[0]
    f32, bf16 = jnp.float32, jnp.bfloat16
    vmem = pl.BlockSpec(memory_space=pltpu.VMEM)
    hbm = pl.BlockSpec(memory_space=pltpu.HBM)
    dma = pltpu.SemaphoreType.DMA
    edge = W // 4
    slots = ITERS * GROUP

    def tiles(*lead):
        return pltpu.VMEM((*lead, 16, BS), bf16)

    def blocks(*lead):
        return pltpu.VMEM((*lead, BS, BS), bf16)

    pairs = pltpu.VMEM((rows // 2, BS, 2 * BS), bf16)
    scratch = [
        pltpu.VMEM((SPECIES, rows * BS), f32), pltpu.VMEM((1, SPECIES, rows * BS), f32),
        pltpu.SMEM((K, rows), jnp.int32), pltpu.VMEM((rows, BS), f32), pltpu.VMEM((SPECIES, SPECIES), f32),
        blocks(rows), blocks(rows, K), blocks(rows),
        pltpu.VMEM((rows, K * BS, BS), bf16), pairs, pairs,
        blocks(WINDOW), blocks(WINDOW, K), blocks(WINDOW), pltpu.VMEM((WINDOW, BS), f32),
        pltpu.VMEM((WINDOW, (K + 2) * BS, BS), bf16),
        pltpu.VMEM((WINDOW // 2, BS, 2 * BS), bf16),
        pltpu.VMEM((rows + 2 * W, 8, BS), f32), pltpu.VMEM((rows + 2 * W, 8, BS), f32),
        pltpu.VMEM((SPECIES, 8, BS), f32), pltpu.VMEM((rows, 8, BS), f32),
        *[pltpu.VMEM((rows, SPECIES, BS), f32)] * 11, pltpu.VMEM((rows, 8, BS), f32),
        tiles(3, 2, 2 * edge), tiles(3, 2, 2 * edge),
        tiles(ITERS, rows // 2), tiles(slots, T_WINDOW), tiles(slots, T_OWN),
        tiles(rows // 4), tiles(slots, 3, T_OWN), tiles(slots, T_OWN),
        tiles(ITERS, 2, rows // 4), tiles(2, 2, edge),
        pltpu.VMEM((4, K, rows), jnp.int32), pltpu.SMEM((4, K, rows), jnp.int32),
        pltpu.SMEM((rows, K), jnp.int32), pltpu.SMEM((WINDOW, K), jnp.int32),
        dma((8,)), dma((3, 2)), dma((3, 2)), dma((4, 4)), dma((4, 4)), dma((4,)), dma((4,)),
        dma((3 * len(PIECES), 3)), dma((len(PIECES), 3)),
        dma((ITERS, 6)), dma((slots, 3)), dma((6,)), dma((slots, 3)), dma((slots, 3)),
        dma((slots, 2, 2)), dma((ITERS, 2, 4)),
    ]
    return pl.pallas_call(
        functools.partial(kernel, n_tm, n_sp, rows),
        out_shape=jax.ShapeDtypeStruct((1, 3, SPECIES, rows * BS), f32),
        in_specs=[hbm] * 9,
        out_specs=vmem,
        scratch_shapes=scratch,
        compiler_params=pltpu.CompilerParams(
            collective_id=0, has_side_effects=True, vmem_limit_bytes=60 << 20
        ),
    )(start, guess, columns.T, rates.reshape(rows, BS), mixing, diag, off, fine, coarse)


def solution(mesh):
    in_specs = (
        P(None, "space"),
        P("tm", None, "space"),
        P("space", None, None),
        P("space", None, None, None),
        P("space", None),
        P("space"),
        P(),
        P("space", None, None),
        P("space", None, None),
    )
    out_specs = P("tm", None, None, "space")
    body = functools.partial(shards, mesh.shape["tm"], mesh.shape["space"])
    return jax.shard_map(body, mesh=mesh, in_specs=in_specs, out_specs=out_specs, check_vma=False)
```

```python
import functools

import jax
import jax.numpy as jnp
from jax import lax
from jax.experimental import pallas as pl
from jax.experimental.pallas import tpu as pltpu
from jax.sharding import PartitionSpec as P

BS = 128
K = 4
SPECIES = 4
ITERS = 2
W = 8
STEP = 0.25
HALF = STEP / 2
MESH = pl.DeviceIdType.MESH
NODES, FIRST, SECOND = range(3)
LEFT, RIGHT = 0, 1
GROUP = 4
STRETCH = 8
OWN = 16
WINDOW = OWN + 2 * W
T_OWN, T_WINDOW, T_EDGE = OWN // 4, WINDOW // 4, W // 4
PIECES = ((0, 1), (1, 2), (3, 1), (4, 2), (6, 2))
FIRST_FROM = ((0, 0), (0, 1), (0, GROUP - 1), (1, 0), (GROUP - 1, 0))
OTHERS_FROM = ((0, 0), (0, 1), (0, GROUP - 1), (0, 0), (0, GROUP - 1))


def dot(lhs, rhs):
    return lax.dot_general(
        lhs.astype(jnp.bfloat16), rhs, (((1,), (0,)), ((), ())), preferred_element_type=jnp.float32
    )


def rows_loop(first, last, body):
    def step(i, carry):
        body(i)
        return carry

    lax.fori_loop(first, last, step, 0, unroll=True)


def kernel(
    n_tm, n_sp, rows,
    start_h, guess_h, cols_h, rates_h, mixing_h, diag_h, off_h, fine_h, coarse_h,
    out,
    start, guess, cols, rates, mixing,
    diag_v, off_v, fine_v, raw_w, diag_w, fine_w, win_diag, win_off, win_coarse, win_rates, comp_w, inverse_w,
    near, near_q, mix_v, nodes, imp_b, exp_b, mid_b, first_v, second_r,
    sum_c, sum_t, state, solved, partial, fresh, right_v,
    send_b, land, terms_b, terms_land, start_b, chain_land, end_b, value_land, value_halo,
    cols_land, cols_s, place_of, place_w,
    load_sem, send_sem, recv_sem, unit_send, unit_recv, cols_send, cols_recv, piece_send, piece_recv,
    terms_send, terms_recv, start_send, chain_send, chain_recv, value_send, value_recv,
):
    tm = lax.axis_index("tm")
    sp = lax.axis_index("space")
    plane, line, chip, core = tm // GROUP, tm % GROUP, sp // 2, sp % 2
    has_left, has_right = sp > 0, sp < n_sp - 1
    edge = W // 4
    chunks = n_sp * rows // OWN

    def quarter(x, y):
        return jnp.where(x % 2 == 0, y, GROUP - 1 - y)

    def chain_device(i, z):
        x, j = i // GROUP, i % GROUP
        return z * GROUP + quarter(x, j), 2 * x + 1

    def chain_plane(it, p):
        return jnp.where(p < STRETCH, 2, 0) + it

    mine = quarter(chip, line)
    chunk = GROUP * chip + mine
    round_here, stretch = plane % 2, jnp.where(plane < 2, 1, 0)
    on_chain = core == 1
    even = chunk % 2 == 0
    chunk_left, chunk_right = chunk > 0, chunk < chunks - 1
    owner = chunk // 2
    beside = jnp.where(even, owner - 1, owner + 1)
    has_beside = (even & chunk_left) | (~even & chunk_right)
    low, high = 2 * sp, 2 * sp + 1

    def remote(src, dst, out_sem, in_sem, device):
        return pltpu.make_async_remote_copy(
            src_ref=src, dst_ref=dst, send_sem=out_sem, recv_sem=in_sem,
            device_id=device, device_id_type=MESH,
        )

    def arrive(dst, in_sem, there=None):
        def wait():
            remote(dst, dst, send_sem.at[0, 0], in_sem, (tm, sp)).wait_recv()

        if there is None:
            wait()
        else:
            pl.when(there)(wait)

    loads = [
        pltpu.make_async_copy(src, dst, load_sem.at[i])
        for i, (src, dst) in enumerate((
            (mixing_h, mixing), (guess_h, guess), (start_h, start), (cols_h, cols), (rates_h, rates),
            (diag_h, diag_v), (off_h, off_v), (fine_h, fine_v),
        ))
    ]
    for load in loads:
        load.start()
    small, large = loads[:5], loads[5:]
    cols_land[...] = jnp.zeros_like(cols_land)

    barrier = pltpu.get_barrier_semaphore()
    later = stretch == 0
    senders, receivers = [], []
    own_next = ((stretch + 1) * STRETCH == tm) & (owner == sp)

    def is_me(device):
        return (device[0] == tm) & (device[1] == sp)


    def both(device, there):
        senders.append((device, there))
        receivers.append(there)

    both((tm, sp - 1), has_left)
    both((tm, sp + 1), has_right)
    for i, there in ((low - 1, has_left), (low, True), (high, True), (high + 1, has_right)):
        for it in range(ITERS):
            both(chain_device(i, chain_plane(it, tm)), there)
            device = chain_device(i, chain_plane(it, 0))
            senders.append((device, there & (tm == STRETCH) & ~is_me(device)))
    for j in range(STRETCH):
        both((stretch * STRETCH + j, owner), on_chain)
        both((stretch * STRETCH + j, beside), on_chain & has_beside)
    receivers.append(on_chain & later & ~own_next)
    receivers.append(on_chain & later & has_beside)
    both(chain_device(chunk - 1, plane), on_chain & chunk_left)
    both(chain_device(chunk + 1, plane), on_chain & chunk_right)
    for i, there in ((chunk, True), (chunk - 1, chunk_left), (chunk + 1, chunk_right)):
        senders.append((chain_device(i, plane + 2), on_chain & ~later & there))
        receivers.append(on_chain & later & there)

    first_plane = 2
    lower = on_chain & (mine == 0) & (chip > 0)
    upper = on_chain & (mine == GROUP - 1) & (chip < n_sp // 2 - 1)

    def piece_sources(n):
        t_first, t_others = (
            (plane + dz) % GROUP * GROUP + (line + dy) % GROUP for dz, dy in (FIRST_FROM[n], OTHERS_FROM[n])
        )
        t = jnp.where(plane == first_plane, t_first, t_others)
        return ((t, sp - 2), lower), ((t, sp + 1), upper)

    def piece_targets(n, when):
        dz, dy = OTHERS_FROM[n] if when else FIRST_FROM[n]
        z, y = (plane + GROUP - dz) % GROUP, (line + GROUP - dy) % GROUP
        t = z * GROUP + y
        hurried = z == 0
        fits = z == first_plane if when == 0 else (z != first_plane) & ~hurried if when == 1 else hurried
        right = on_chain & (chip < n_sp // 2 - 1) & (quarter(chip + 1, y) == 0)
        left = ~on_chain & (chip > 0) & (quarter(chip - 1, y) == GROUP - 1)
        return ((t, sp + 2), fits & right, 3, 0), ((t, sp - 1), fits & left, 0, 3)

    for n in range(len(PIECES)):
        senders.extend(piece_sources(n))
        for when in range(3):
            receivers.extend(there for _, there, _, _ in piece_targets(n, when))

    for device, there in senders:
        def signal(device=device):
            pl.semaphore_signal(barrier, inc=1, device_id=device, device_id_type=MESH)

        pl.when(there)(signal)

    for load in small:
        load.wait()

    def cells(b):
        return pl.ds(pl.multiple_of(b * BS, BS), BS)

    def begin(b):
        own = guess[0, :, cells(b)]
        nodes[b, 0:4] = jnp.where(tm == 0, start[:, cells(b)], own)
        nodes[b, 4:8] = own

    rows_loop(0, rows, begin)

    pl.semaphore_wait(barrier, sum(jnp.asarray(there).astype(jnp.int32) for there in receivers))

    def unit_copies(unit, at, device):
        src, dst = pl.ds(unit * W, W), pl.ds(pl.multiple_of(at * W, W), W)
        pairs = ((off_h, win_off), (coarse_h, win_coarse), (rates_h, win_rates), (diag_h, win_diag))
        copies = []
        for n, (a, b) in enumerate(pairs):
            if device is None:
                copies.append(pltpu.make_async_copy(a.at[src], b.at[dst], unit_recv.at[at, n]))
            else:
                copies.append(remote(a.at[src], b.at[dst], unit_send.at[unit, n], unit_recv.at[at, n], device))
        return copies

    def unit_plan():
        plan = []
        for unit in range(4):
            at = unit - 2 * mine + 1
            plan.append((unit, at, (tm, sp + 1), (core == 0) & (at >= 0) & (at < 4)))
            at = unit + 4 - 2 * mine + 1
            plan.append((unit, at, None, on_chain & (at >= 0) & (at < 4)))
        return plan

    def piece_copies(n, unit, at, device, row):
        first, count = PIECES[n]
        src, dst = pl.ds(unit * W + first, count), pl.ds(at * W + first, count)
        copies = [
            remote(off_h.at[src], win_off.at[dst], piece_send.at[row, 0], piece_recv.at[n, 0], device),
            remote(coarse_h.at[src], win_coarse.at[dst], piece_send.at[row, 1], piece_recv.at[n, 1], device),
        ]
        if n == 0:
            src, dst = pl.ds(unit * W, W), pl.ds(at * W, W)
            copies.append(remote(rates_h.at[src], win_rates.at[dst], piece_send.at[row, 2], piece_recv.at[n, 2], device))
        return copies

    def pieces(when, act):
        for n in range(len(PIECES)):
            for device, there, unit, at in piece_targets(n, when):
                def go(n=n, unit=unit, at=at, device=device):
                    for copy in piece_copies(n, unit, at, device, n + when * len(PIECES)):
                        act(copy)

                pl.when(there)(go)

    def cols_copy(which):
        slot, device = ((1, (tm, sp + 1)), (3, (tm, sp - 1)), (0, (tm, sp + 2)))[which]
        return remote(cols_h, cols_land.at[slot], cols_send.at[which], cols_recv.at[slot], device)

    def cols_plan():
        next_low = quarter(chip + 1, line) == 0
        last_high = quarter(chip - 1, line) == GROUP - 1
        return (
            (0, core == 0),
            (1, (core == 0) & (chip > 0) & last_high),
            (2, on_chain & (chip < n_sp // 2 - 1) & next_low),
        )

    def weights_out():
        for which, there in cols_plan():
            pl.when(there)(cols_copy(which).start)
        for unit, at, device, there in unit_plan():
            def go(unit=unit, at=at, device=device):
                copies = unit_copies(unit, at, device)
                for copy in copies[:3]:
                    copy.start()
                pl.when((at == 1) | (at == 2))(copies[3].start)

            pl.when(there)(go)

    def weights_sent():
        for which, there in cols_plan():
            pl.when(there)(cols_copy(which).wait_send)
        for unit, at, device, there in unit_plan():
            if device is None:
                continue

            def done(unit=unit, at=at, device=device):
                copies = unit_copies(unit, at, device)
                for copy in copies[:3]:
                    copy.wait_send()
                pl.when((at == 1) | (at == 2))(copies[3].wait_send)

            pl.when(there)(done)


    def halo_copies(kind, count):
        to_left = remote(
            send_b.at[kind, LEFT, pl.ds(0, count)], land.at[kind, RIGHT, pl.ds(0, count)],
            send_sem.at[kind, LEFT], recv_sem.at[kind, RIGHT], (tm, sp - 1),
        )
        to_right = remote(
            send_b.at[kind, RIGHT, pl.ds(0, count)], land.at[kind, LEFT, pl.ds(0, count)],
            send_sem.at[kind, RIGHT], recv_sem.at[kind, LEFT], (tm, sp + 1),
        )
        return to_left, to_right

    def tile(values):
        return jnp.concatenate(values, axis=0).astype(jnp.bfloat16)

    def halo_send(kind, fields):
        for f, field in enumerate(fields):
            for j in range(edge):
                send_b[kind, LEFT, f * edge + j] = tile([field(4 * j + g) for g in range(4)])
                send_b[kind, RIGHT, f * edge + j] = tile([field(rows - W + 4 * j + g) for g in range(4)])
        to_left, to_right = halo_copies(kind, edge * len(fields))
        pl.when(has_left)(to_left.start)
        pl.when(has_right)(to_right.start)

    def halo_wait(kind, count):
        to_left, to_right = halo_copies(kind, edge * count)

        @pl.when(has_left)
        def _():
            to_right.wait_recv()
            to_left.wait_send()

        @pl.when(has_right)
        def _():
            to_left.wait_recv()
            to_right.wait_send()

    def spread(block_tile, target, block, row):
        wide = block_tile.astype(jnp.float32)
        for g in range(4):
            target[block + g, row : row + 4] = wide[4 * g : 4 * g + 4]

    def halo_place(kind, target, count):
        for f in range(count):
            for j in range(edge):
                spread(land[kind, LEFT, f * edge + j], target, 4 * j, 4 * f)
                spread(land[kind, RIGHT, f * edge + j], target, W + rows + 4 * j, 4 * f)

    def gather(source, places, b):
        return jnp.concatenate([source[places[b, k]] for k in range(K)], axis=1)

    def react(v, rate):
        total = None
        for t in range(SPECIES):
            line_t = v[t : t + 1]
            if v.shape[0] == 8:
                second = v[4 + t : 5 + t]
                row = lax.broadcasted_iota(jnp.int32, (8, BS), 0)
                line_t = jnp.where(row < 4, jnp.broadcast_to(line_t, (8, BS)), jnp.broadcast_to(second, (8, BS)))
            term = mix_v[t, : v.shape[0]] * line_t
            total = term if total is None else total + term
        return total * rate

    def paired(first, second, weights):
        got = dot(jnp.concatenate([first, second], axis=0), weights)
        return got[:8, :BS], got[8:, BS:]

    def explicit(b, count):
        got = dot(gather(near, place_of, b), raw_w[b])[: 4 * count]
        return got + react(near[W + b, : 4 * count], rates[pl.ds(b, 1)])

    def transposed(n, carry):
        for r in range(4):
            b, half = 4 * n + r, pl.ds(BS * (r % 2), BS)
            diag_w[2 * n + r // 2, :, half] = diag_v[b].T
            fine_w[2 * n + r // 2, :, half] = fine_v[b].T
            for k in range(K):
                raw_w[b, BS * k : BS * (k + 1)] = off_v[b, k].T
        return carry

    def outer(*bodies):
        for body in bodies:
            rows_loop(0, W // 2, body)
            rows_loop((rows - W) // 2, rows // 2, body)

    def inner(*bodies):
        for body in bodies:
            rows_loop(W // 2, (rows - W) // 2, body)

    def solve(target):
        def pair(i):
            got = paired(right_v[2 * i], right_v[2 * i + 1], fine_w[i])
            target[2 * i], target[2 * i + 1] = got[0][:4], got[1][:4]

        return pair

    def terms_copies(it, late):
        slot = tm % STRETCH
        main = terms_land.at[slot]
        to = [chain_device(i, chain_plane(it, tm)) for i in (low, high, low - 1, high + 1)]

        def piece(first, count, at, n, sem, device):
            return remote(
                terms_b.at[it, pl.ds(first, count)], main.at[pl.ds(at, count)], terms_send.at[it, n],
                terms_recv.at[slot, sem], device,
            )

        if late:
            return (
                (piece(0, 2, 2, 0, 0, to[0]), True),
                (piece(6, 2, 4, 1, 0, to[1]), True),
                (piece(0, 2, 6, 2, 1, to[2]), has_left),
                (piece(6, 2, 0, 3, 1, to[3]), has_right),
            )
        return (piece(2, 4, 4, 4, 2, to[0]), True), (piece(2, 4, 0, 5, 2, to[1]), True)

    def terms_out(it, late):
        for j in (0, 1, 6, 7) if late else range(2, 6):
            terms_b[it, j, 0] = tile([sum_c[4 * j + g] for g in range(4)])
            terms_b[it, j, 1] = tile([sum_t[4 * j + g] for g in range(4)])
        for copy, there in terms_copies(it, late):
            if there is True:
                copy.start()
            else:
                pl.when(there)(copy.start)

    def terms_sent(it):
        for copy, there in terms_copies(it, True) + terms_copies(it, False):
            if there is True:
                copy.wait_send()
            else:
                pl.when(there)(copy.wait_send)

    def fine(it):
        @pl.when(it == 0)
        def _():
            halo_send(NODES, [lambda b: nodes[b, 0:4], lambda b: nodes[b, 4:8]])
            first_things()
            for load in large:
                load.wait()
            lax.fori_loop(0, rows // 4, transposed, 0)
            for b in range(rows):
                near[W + b] = nodes[b]
            halo_wait(NODES, 2)
            halo_place(NODES, near, 2)

        @pl.when(it == 1)
        def _():
            @pl.when(tm > 0)
            def _():
                values_wait(0, 0, True)
                for j in range(rows // 4):
                    spread(value_land[0, 0, j], nodes, 4 * j, 0)
                    spread(value_land[0, 0, j], near, W + 4 * j, 0)
                for j in range(edge):
                    spread(value_halo[0, LEFT, j], near, 4 * j, 0)
                    spread(value_halo[0, RIGHT, j], near, W + rows + 4 * j, 0)

            @pl.when(tm == 0)
            def _():
                for b in range(rows):
                    near[W + b, 0:4] = nodes[b, 0:4]
                for j in range(edge):
                    spread(land[NODES, LEFT, j], near, 4 * j, 0)
                    spread(land[NODES, RIGHT, j], near, W + rows + 4 * j, 0)

            values_wait(0, 1, True)
            for j in range(rows // 4):
                spread(value_land[0, 1, j], near, W + 4 * j, 4)
            for j in range(edge):
                spread(value_halo[1, LEFT, j], near, 4 * j, 4)
                spread(value_halo[1, RIGHT, j], near, W + rows + 4 * j, 4)

        own_part = jnp.where(it == 0, 0.0, 0.5)
        end_part = jnp.where(it == 0, 1.0, 0.5)

        def node_terms(i):
            imps = paired(near[W + 2 * i], near[W + 2 * i + 1], diag_w[i])
            for b, imp in zip((2 * i, 2 * i + 1), imps):
                exp = explicit(b, 2)
                imp_0, exp_0, imp_2, exp_2 = imp[:4], exp[:4], imp[4:], exp[4:]
                one_i = imp_b[b] + own_part * imp_0 + end_part * imp_2
                one_e = exp_b[b] + own_part * exp_0 + end_part * exp_2
                f_0, f_1, f_2 = imp_0 + exp_0, one_i + one_e, imp_2 + exp_2
                right_v[b, 0:4] = (
                    nodes[b, 0:4] - HALF * one_i + STEP * (5 / 24 * f_0 + 1 / 3 * f_1 - 1 / 24 * f_2)
                )
                second_r[b] = STEP * (-1 / 24 * f_0 + 1 / 3 * f_1 + 5 / 24 * f_2) - HALF * (one_e + imp_2)
                sum_c[b] = STEP * (1 / 6 * f_0 - exp_0)
                sum_t[b] = (-STEP / 3) * f_0
                imp_b[b] = -0.5 * imp_0
                exp_b[b] = -0.5 * exp_0

        outer(node_terms, solve(first_v))
        halo_send(FIRST, [lambda b: first_v[b]])
        pl.when((it == 0) & (tm == 0))(start_out)
        inner(node_terms, solve(first_v))

        def put_first(b):
            near[W + b, 0:4] = first_v[b]

        rows_loop(0, rows, put_first)
        early_units(it, 0)
        halo_wait(FIRST, 1)
        halo_place(FIRST, near, 1)

        def first_terms(i):
            imps = paired(near[W + 2 * i], near[W + 2 * i + 1], diag_w[i])
            for b, imp in zip((2 * i, 2 * i + 1), imps):
                imp = imp[:4]
                exp = explicit(b, 1)
                force = STEP * 2 / 3 * (imp + exp)
                right_v[b, 0:4] = first_v[b] + HALF * exp + second_r[b]
                sum_c[b] += force
                sum_t[b] += force
                imp_b[b] += imp
                exp_b[b] += exp

        outer(first_terms, solve(fresh))
        halo_send(SECOND, [lambda b: fresh[b]])

        @pl.when((it == 0) & (tm == 0))
        def _():
            for copy, there in start_copies(1):
                pl.when(there)(copy.start)

        inner(first_terms, solve(fresh))

        def put_second(b):
            near[W + b, 0:4] = fresh[b]
            mid_b[b] = first_v[b] - 0.5 * (nodes[b, 0:4] + fresh[b])

        rows_loop(0, rows, put_second)

        def second_terms(i):
            imps = paired(near[W + 2 * i], near[W + 2 * i + 1], diag_w[i])
            for b, imp in zip((2 * i, 2 * i + 1), imps):
                imp = imp[:4]
                exp = explicit(b, 1)
                force = imp + exp
                sum_c[b] += STEP * (1 / 6 * force - imp)
                sum_t[b] += (-STEP / 3) * force
                imp_b[b] += -0.5 * imp
                exp_b[b] += -0.5 * exp

        inner(second_terms)
        terms_out(it, False)
        early_units(it, 1)
        halo_wait(SECOND, 1)
        halo_place(SECOND, near, 1)
        outer(second_terms)
        terms_out(it, True)

    def values_wait(it, which, halos):
        for n in range(2):
            arrive(value_land.at[it, which, pl.ds(n * T_OWN, T_OWN)], value_recv.at[it, which, n])
        if halos:
            arrive(value_halo.at[which, LEFT], value_recv.at[it, which, 2], has_left)
            arrive(value_halo.at[which, RIGHT], value_recv.at[it, which, 3], has_right)

    def value_copies(j):
        it, p = round_here, stretch * STRETCH + j
        half = chunk % 2
        copies = []
        for which in (1, 0):
            t = p + 1 - which
            there = (p < n_tm - 1) & ~((p == STRETCH * (stretch + 1) - 1) & own_next) if which == 0 else True
            copies.append((remote(
                end_b.at[j], value_land.at[it, which, pl.ds(pl.multiple_of(half * T_OWN, T_OWN), T_OWN)],
                value_send.at[j, which, 0], value_recv.at[it, which, half], (t, owner)), there))
            copies.append((remote(
                end_b.at[j, pl.ds(pl.multiple_of(half * (T_OWN - T_EDGE), T_EDGE), T_EDGE)], value_halo.at[which, 1 - half],
                value_send.at[j, which, 1], value_recv.at[it, which, 3 - half], (t, beside)),
                (t < n_tm) & has_beside & (it == 0)))
        return copies

    def value_here(j):
        half = chunk % 2
        return pltpu.make_async_copy(
            end_b.at[j], value_land.at[round_here, 0, pl.ds(pl.multiple_of(half * T_OWN, T_OWN), T_OWN)],
            value_recv.at[round_here, 0, half],
        )

    def chain_copies(j, half):
        inside = j < STRETCH - 1
        target = jnp.where(inside, j + 1, 0)
        z = jnp.where(inside, plane, plane - 2)
        there = inside | later
        at = pl.ds(half * T_EDGE, T_EDGE)
        copies = []
        for n, (i, ok) in enumerate(((chunk - 1, chunk_left), (chunk + 1, chunk_right))):
            part = 2 - 2 * n
            copies.append((remote(
                end_b.at[j, at], chain_land.at[target, part, at], chain_send.at[j, 2 * n, half],
                chain_recv.at[target, part, half], chain_device(i, z)), there & ok))
        if half == 1:
            copies.append((remote(
                end_b.at[j], chain_land.at[target, 1], chain_send.at[j, 1, 0], chain_recv.at[target, 1, 0],
                chain_device(chunk, z)), there & ~inside))
        return copies

    def start_copies(it):
        copies = []
        for n, (i, part, own, ok) in enumerate((
            (low, 1, 0, True), (low, 2, 1, True), (low - 1, 2, 0, has_left),
            (high, 1, 1, True), (high, 0, 0, True), (high + 1, 0, 1, has_right),
        )):
            device = chain_device(i, chain_plane(it, 0))
            for half in range(2):
                count = T_OWN if part == 1 else T_EDGE
                if part == 1 and half == 1:
                    continue
                copies.append((remote(
                    start_b.at[pl.ds(own * T_OWN + half * T_EDGE, count)],
                    chain_land.at[0, part, pl.ds(half * T_EDGE, count)], start_send.at[it, n, half],
                    chain_recv.at[0, part, half], device), (tm == 0) & ok))
        return copies

    def first_things():
        pieces(0, lambda copy: copy.start())
        pl.when(plane == first_plane)(weights_out)
        def local_place(b, carry):
            for k in range(K):
                place_of[b, k] = jnp.clip(cols[k, b] - (sp * rows - W), 0, rows + 2 * W - 1)
            return carry

        lax.fori_loop(0, rows, local_place, 0)
        near[...] = jnp.zeros_like(near)
        near_q[...] = jnp.zeros_like(near_q)
        imp_b[...] = jnp.zeros_like(imp_b)
        exp_b[...] = jnp.zeros_like(exp_b)
        for t in range(SPECIES):
            column = jnp.broadcast_to(mixing[:, t : t + 1], (SPECIES, BS))
            mix_v[t] = jnp.concatenate([column, column], axis=0)

    def start_out():
        for j in range(rows // 4):
            start_b[j] = tile([nodes[4 * j + g, 0:4] for g in range(4)])
        for copy, there in start_copies(0):
            pl.when(there)(copy.start)

    def composed(n, carry):
        for r in range(4):
            w = 4 * n + r
            inverse = win_coarse[w].T
            comp_w[w, BS : 2 * BS] = inverse
            inverse_w[2 * n + r // 2, :, BS * (r % 2) : BS * (r % 2 + 1)] = inverse
            raw = [win_diag[w]] + [win_off[w, k] for k in range(K)]
            got = (dot(jnp.concatenate([block.T for block in raw], axis=0), inverse) * STEP).astype(jnp.bfloat16)
            comp_w[w, :BS] = got[:BS]
            comp_w[w, 2 * BS :] = got[BS:]
        return carry

    def window_unit(at, foreign=True):
        unit = 2 * mine - 1 + at

        @pl.when((unit >= 0) & (unit < 8))
        def _():
            copies = unit_copies(0, at, (tm, sp))
            for copy in copies[:3] if at in (0, 3) else copies:
                copy.wait_recv()

        if at in (0, 3) and foreign:
            there = lower if at == 0 else upper
            for n in range(len(PIECES)):
                @pl.when(there)
                def _(n=n):
                    for copy in piece_copies(n, 0, at, (tm, sp), n):
                        copy.wait_recv()

        lax.fori_loop(W // 4 * at, W // 4 * (at + 1), composed, 0)

    def window_places():
        first_unit = 2 * mine - 1
        arrive(cols_land.at[1], cols_recv.at[1])
        arrive(cols_land.at[0], cols_recv.at[0], lower)
        arrive(cols_land.at[3], cols_recv.at[3], upper)
        to_scalars = pltpu.make_async_copy(cols_land, cols_s, cols_send.at[3])
        to_scalars.start()
        to_scalars.wait()

        def places(w, carry):
            unit = first_unit + w // W
            slot, row = (unit + 4) // 4, (unit + 4) % 4 * W + w % W
            for k in range(K):
                column = jnp.where(slot == 2, cols[k, row], cols_s[slot, k, row])
                place_w[w, k] = jnp.clip(column - (chunk * OWN - 2 * W), 0, OWN + 4 * W - 1)
            return carry

        lax.fori_loop(0, WINDOW, places, 0)

    hurry = on_chain & (plane == first_plane)

    def early_units(it, step):
        @pl.when((it == 0) & hurry)
        def _():
            if step == 0:
                window_places()
                window_unit(1)
            else:
                window_unit(2)
                pl.when(mine != GROUP - 1)(functools.partial(window_unit, 3, False))
                pl.when(mine == GROUP - 1)(functools.partial(window_unit, 0, False))

    def window_weights():
        @pl.when(~hurry)
        def _():
            window_places()
            for at in range(4):
                window_unit(at)

        @pl.when(hurry)
        def _():
            pl.when(mine == GROUP - 1)(functools.partial(window_unit, 3))
            pl.when(mine != GROUP - 1)(functools.partial(window_unit, 0))

    def chain_step(g, carry):
        halo_at = jnp.where(even, 0, 6)
        early_at, late_at = jnp.where(even, 4, 0), jnp.where(even, 2, 4)

        @pl.when(g == 0)
        def _():
            arrive(chain_land.at[g, 1], chain_recv.at[g, 1, 0])
            for n in range(T_OWN):
                spread(chain_land[g, 1, n], near, 2 * W + 4 * n, 0)

        arrive(terms_land.at[g, pl.ds(early_at, 4)], terms_recv.at[g, 2])
        arrive(terms_land.at[g, pl.ds(late_at, 2)], terms_recv.at[g, 0])
        arrive(terms_land.at[g, pl.ds(halo_at, 2)], terms_recv.at[g, 1], has_beside)

        def prepare(n):
            constant = terms_land[g, n, 0].astype(jnp.float32)
            for r in range(4):
                w = 4 * n + r
                own = near[W + w, 0:4]
                change = STEP * react(own, win_rates[pl.ds(w, 1)])
                right_v[w, 0:4] = own + change + constant[4 * r : 4 * r + 4]
                state[w] = 2.0 * own + change
            for i in (2 * n, 2 * n + 1):
                got = paired(right_v[2 * i], right_v[2 * i + 1], inverse_w[i])
                solved[2 * i], solved[2 * i + 1] = got[0][:4], got[1][:4]

        rows_loop(T_EDGE, T_WINDOW - T_EDGE, prepare)

        def with_rest(n):
            constant = terms_land[g, T_EDGE + n, 1].astype(jnp.float32)
            for r in range(4):
                state[W + 4 * n + r] += 2.0 * constant[4 * r : 4 * r + 4]

        rows_loop(0, T_OWN, with_rest)

        def middle(w):
            spread_s = dot(gather(near, place_w, w), comp_w[w, 2 * BS :])[:4]
            near_q[W + w, 0:4] = solved[w] + spread_s
            partial[w] = 0.5 * spread_s

        first, last = pl.ds(0, T_EDGE), pl.ds(T_EDGE, T_EDGE)
        arrive(chain_land.at[g, 2, first], chain_recv.at[g, 2, 0], chunk_right)
        for n in range(T_EDGE):
            spread(chain_land[g, 2, n], near, 2 * W + OWN + 4 * n, 0)
        rows_loop(T_WINDOW - T_EDGE, T_WINDOW, prepare)
        rows_loop(2 * W, 2 * W + W, middle)
        arrive(chain_land.at[g, 0, first], chain_recv.at[g, 0, 0], chunk_left)
        arrive(chain_land.at[g, 0, last], chain_recv.at[g, 0, 1], chunk_left)
        arrive(chain_land.at[g, 2, last], chain_recv.at[g, 2, 1], chunk_right)
        for n in range(T_OWN):
            spread(chain_land[g, 0, n], near, 4 * n, 0)
        for n in range(T_EDGE, T_OWN):
            spread(chain_land[g, 2, n], near, 2 * W + OWN + 4 * n, 0)
        rows_loop(0, T_EDGE, prepare)
        rows_loop(0, 2 * W, middle)
        rows_loop(3 * W, WINDOW, middle)

        def end(o):
            w = W + o
            own, mid = near[W + w, 0:4], near_q[W + w, 0:4]
            right = state[w] + STEP * react(mid, win_rates[pl.ds(w, 1)])
            parts = jnp.concatenate([own - mid, right, gather(near_q, place_w, w)[:4]], axis=1)
            near[W + w, 0:4] = partial[w] + 0.5 * dot(parts, comp_w[w])

        for half in range(2):
            rows_loop(half * W, (half + 1) * W, end)
            for n in range(half * T_EDGE, (half + 1) * T_EDGE):
                end_b[g, n] = tile([near[2 * W + 4 * n + r, 0:4] for r in range(4)])
            for copy, there in chain_copies(g, half):
                pl.when(there)(copy.start)
        pl.when((g == STRETCH - 1) & own_next)(lambda: value_here(g).start())
        for copy, there in value_copies(g):
            if there is True:
                copy.start()
            else:
                pl.when(there)(copy.start)
        return carry

    def round_of(it, carry):
        fine(it)

        @pl.when(it == 0)
        def _():
            terms_sent(0)
            pieces(1, lambda copy: copy.start())
            pieces(2, lambda copy: copy.start())
            pl.when(plane != first_plane)(weights_out)

        composes = jnp.where((plane == 0) & (line == 0), 1, 0)
        pl.when(on_chain & (it == composes))(window_weights)

        @pl.when(on_chain & (it == stretch))
        def _():
            lax.fori_loop(0, STRETCH, chain_step, 0)

        return carry

    lax.fori_loop(0, ITERS, round_of, 0)

    weights_sent()
    for when in range(3):
        pieces(when, lambda copy: copy.wait_send())
    for it in range(ITERS):
        for copy, there in start_copies(it):
            pl.when(there)(copy.wait_send)
    terms_sent(1)

    @pl.when(on_chain)
    def _():
        def sent(g, carry):
            for copy, there in chain_copies(g, 0) + chain_copies(g, 1) + value_copies(g):
                if there is True:
                    copy.wait_send()
                else:
                    pl.when(there)(copy.wait_send)
            return carry

        lax.fori_loop(0, STRETCH, sent, 0)

    pl.when(tm > 0)(lambda: values_wait(1, 0, False))
    values_wait(1, 1, False)

    def write(j):
        ends = value_land[1, 1, j].astype(jnp.float32)
        starts = value_land[1, 0, j].astype(jnp.float32)
        for g in range(4):
            b = 4 * j + g
            own = jnp.where(tm == 0, start[:, cells(b)], starts[4 * g : 4 * g + 4])
            last = ends[4 * g : 4 * g + 4]
            out[0, 0, :, cells(b)] = own
            out[0, 1, :, cells(b)] = mid_b[b] + 0.5 * (own + last)
            out[0, 2, :, cells(b)] = last

    rows_loop(0, rows // 4, write)


def shards(n_tm, n_sp, start, guess, diag, off, columns, rates, mixing, fine, coarse):
    rows = diag.shape[0]
    f32, bf16 = jnp.float32, jnp.bfloat16
    vmem = pl.BlockSpec(memory_space=pltpu.VMEM)
    hbm = pl.BlockSpec(memory_space=pltpu.HBM)
    dma = pltpu.SemaphoreType.DMA
    edge = W // 4
    slots = STRETCH

    def tiles(*lead):
        return pltpu.VMEM((*lead, 16, BS), bf16)

    def blocks(*lead):
        return pltpu.VMEM((*lead, BS, BS), bf16)

    pairs = pltpu.VMEM((rows // 2, BS, 2 * BS), bf16)
    scratch = [
        pltpu.VMEM((SPECIES, rows * BS), f32), pltpu.VMEM((1, SPECIES, rows * BS), f32),
        pltpu.SMEM((K, rows), jnp.int32), pltpu.VMEM((rows, BS), f32), pltpu.VMEM((SPECIES, SPECIES), f32),
        blocks(rows), blocks(rows, K), blocks(rows),
        pltpu.VMEM((rows, K * BS, BS), bf16), pairs, pairs,
        blocks(WINDOW), blocks(WINDOW, K), blocks(WINDOW), pltpu.VMEM((WINDOW, BS), f32),
        pltpu.VMEM((WINDOW, (K + 2) * BS, BS), bf16),
        pltpu.VMEM((WINDOW // 2, BS, 2 * BS), bf16),
        pltpu.VMEM((rows + 2 * W, 8, BS), f32), pltpu.VMEM((rows + 2 * W, 8, BS), f32),
        pltpu.VMEM((SPECIES, 8, BS), f32), pltpu.VMEM((rows, 8, BS), f32),
        *[pltpu.VMEM((rows, SPECIES, BS), f32)] * 11, pltpu.VMEM((rows, 8, BS), f32),
        tiles(3, 2, 2 * edge), tiles(3, 2, 2 * edge),
        tiles(ITERS, rows // 4, 2), tiles(slots, T_WINDOW, 2),
        tiles(rows // 4), tiles(slots, 3, T_OWN), tiles(slots, T_OWN),
        tiles(ITERS, 2, rows // 4), tiles(2, 2, edge),
        pltpu.VMEM((4, K, rows), jnp.int32), pltpu.SMEM((4, K, rows), jnp.int32),
        pltpu.SMEM((rows, K), jnp.int32), pltpu.SMEM((WINDOW, K), jnp.int32),
        dma((8,)), dma((3, 2)), dma((3, 2)), dma((4, 4)), dma((4, 4)), dma((4,)), dma((4,)),
        dma((3 * len(PIECES), 3)), dma((len(PIECES), 3)),
        dma((ITERS, 6)), dma((slots, 3)), dma((ITERS, 6, 2)), dma((slots, 3, 2)), dma((slots, 3, 2)),
        dma((slots, 2, 2)), dma((ITERS, 2, 4)),
    ]
    return pl.pallas_call(
        functools.partial(kernel, n_tm, n_sp, rows),
        out_shape=jax.ShapeDtypeStruct((1, 3, SPECIES, rows * BS), f32),
        in_specs=[hbm] * 9,
        out_specs=vmem,
        scratch_shapes=scratch,
        compiler_params=pltpu.CompilerParams(
            collective_id=0, has_side_effects=True, vmem_limit_bytes=60 << 20
        ),
    )(start, guess, columns.T, rates.reshape(rows, BS), mixing, diag, off, fine, coarse)


def solution(mesh):
    in_specs = (
        P(None, "space"),
        P("tm", None, "space"),
        P("space", None, None),
        P("space", None, None, None),
        P("space", None),
        P("space"),
        P(),
        P("space", None, None),
        P("space", None, None),
    )
    out_specs = P("tm", None, None, "space")
    body = functools.partial(shards, mesh.shape["tm"], mesh.shape["space"])
    return jax.shard_map(body, mesh=mesh, in_specs=in_specs, out_specs=out_specs, check_vma=False)
```

```python
import functools

import jax
import jax.numpy as jnp
from jax import lax
from jax.experimental import pallas as pl
from jax.experimental.pallas import tpu as pltpu
from jax.sharding import PartitionSpec as P

BS = 128
K = 4
SPECIES = 4
ITERS = 2
W = 8
STEP = 0.25
HALF = STEP / 2
MESH = pl.DeviceIdType.MESH
NODES, FIRST, SECOND = range(3)
LEFT, RIGHT = 0, 1
GROUP = 4
STRETCH = 8
OWN = 16
WINDOW = OWN + 2 * W
T_OWN, T_WINDOW, T_EDGE = OWN // 4, WINDOW // 4, W // 4
PIECES = ((0, 1), (1, 2), (3, 1), (4, 2), (6, 2))
FIRST_FROM = ((0, 0), (0, 1), (0, GROUP - 1), (1, 0), (GROUP - 1, 0))
OTHERS_FROM = ((0, 0), (0, 1), (0, GROUP - 1), (0, 0), (0, GROUP - 1))


def dot(lhs, rhs):
    return lax.dot_general(
        lhs.astype(jnp.bfloat16), rhs, (((1,), (0,)), ((), ())), preferred_element_type=jnp.float32
    )


def rows_loop(first, last, body):
    def step(i, carry):
        body(i)
        return carry

    lax.fori_loop(first, last, step, 0, unroll=True)


def kernel(
    n_tm, n_sp, rows,
    start_h, guess_h, cols_h, rates_h, mixing_h, diag_h, off_h, fine_h, coarse_h,
    out,
    start, guess, cols, rates, mixing,
    diag_v, off_v, fine_v, raw_w, diag_w, fine_w, win_diag, win_off, win_coarse, win_rates, comp_w, inverse_w,
    near, near_q, mix_v, nodes, imp_b, exp_b, mid_b, first_v, second_r,
    sum_c, sum_t, state, solved, partial, fresh, right_v,
    send_b, land, terms_b, terms_land, start_b, chain_land, end_b, value_land, value_halo,
    cols_land, cols_s, place_of, place_w,
    load_sem, send_sem, recv_sem, unit_send, unit_recv, cols_send, cols_recv, piece_send, piece_recv,
    terms_send, terms_recv, start_send, chain_send, chain_recv, value_send, value_recv,
):
    tm = lax.axis_index("tm")
    sp = lax.axis_index("space")
    plane, line, chip, core = tm // GROUP, tm % GROUP, sp // 2, sp % 2
    has_left, has_right = sp > 0, sp < n_sp - 1
    edge = W // 4
    chunks = n_sp * rows // OWN

    def quarter(x, y):
        return jnp.where(x % 2 == 0, y, GROUP - 1 - y)

    def chain_device(i, z):
        x, j = i // GROUP, i % GROUP
        return z * GROUP + quarter(x, j), 2 * x + 1

    def chain_plane(it, p):
        return jnp.where(p < STRETCH, 2, 0) + it

    mine = quarter(chip, line)
    chunk = GROUP * chip + mine
    round_here, stretch = plane % 2, jnp.where(plane < 2, 1, 0)
    on_chain = core == 1
    even = chunk % 2 == 0
    chunk_left, chunk_right = chunk > 0, chunk < chunks - 1
    owner = chunk // 2
    beside = jnp.where(even, owner - 1, owner + 1)
    has_beside = (even & chunk_left) | (~even & chunk_right)
    low, high = 2 * sp, 2 * sp + 1

    def remote(src, dst, out_sem, in_sem, device):
        return pltpu.make_async_remote_copy(
            src_ref=src, dst_ref=dst, send_sem=out_sem, recv_sem=in_sem,
            device_id=device, device_id_type=MESH,
        )

    def arrive(dst, in_sem, there=None):
        def wait():
            remote(dst, dst, send_sem.at[0, 0], in_sem, (tm, sp)).wait_recv()

        if there is None:
            wait()
        else:
            pl.when(there)(wait)

    loads = [
        pltpu.make_async_copy(src, dst, load_sem.at[i])
        for i, (src, dst) in enumerate((
            (mixing_h, mixing), (guess_h, guess), (start_h, start), (cols_h, cols), (rates_h, rates),
            (diag_h, diag_v), (off_h, off_v), (fine_h, fine_v),
        ))
    ]
    for load in loads:
        load.start()
    small, large = loads[:5], loads[5:]
    cols_land[...] = jnp.zeros_like(cols_land)

    barrier = pltpu.get_barrier_semaphore()
    later = stretch == 0
    senders, receivers = [], []
    own_next = ((stretch + 1) * STRETCH == tm) & (owner == sp)

    def is_me(device):
        return (device[0] == tm) & (device[1] == sp)


    def both(device, there):
        senders.append((device, there))
        receivers.append(there)

    both((tm, sp - 1), has_left)
    both((tm, sp + 1), has_right)
    for i, there in ((low - 1, has_left), (low, True), (high, True), (high + 1, has_right)):
        for it in range(ITERS):
            both(chain_device(i, chain_plane(it, tm)), there)
            device = chain_device(i, chain_plane(it, 0))
            senders.append((device, there & (tm == STRETCH) & ~is_me(device)))
    for j in range(STRETCH):
        both((stretch * STRETCH + j, owner), on_chain)
        both((stretch * STRETCH + j, beside), on_chain & has_beside)
    receivers.append(on_chain & later & ~own_next)
    receivers.append(on_chain & later & has_beside)
    both(chain_device(chunk - 1, plane), on_chain & chunk_left)
    both(chain_device(chunk + 1, plane), on_chain & chunk_right)
    for i, there in ((chunk, True), (chunk - 1, chunk_left), (chunk + 1, chunk_right)):
        senders.append((chain_device(i, plane + 2), on_chain & ~later & there))
        receivers.append(on_chain & later & there)

    first_plane = 2
    lower = on_chain & (mine == 0) & (chip > 0)
    upper = on_chain & (mine == GROUP - 1) & (chip < n_sp // 2 - 1)

    def piece_sources(n):
        t_first, t_others = (
            (plane + dz) % GROUP * GROUP + (line + dy) % GROUP for dz, dy in (FIRST_FROM[n], OTHERS_FROM[n])
        )
        t = jnp.where(plane == first_plane, t_first, t_others)
        return ((t, sp - 2), lower), ((t, sp + 1), upper)

    def piece_targets(n, when):
        dz, dy = OTHERS_FROM[n] if when else FIRST_FROM[n]
        z, y = (plane + GROUP - dz) % GROUP, (line + GROUP - dy) % GROUP
        t = z * GROUP + y
        hurried = z == 0
        fits = z == first_plane if when == 0 else (z != first_plane) & ~hurried if when == 1 else hurried
        right = on_chain & (chip < n_sp // 2 - 1) & (quarter(chip + 1, y) == 0)
        left = ~on_chain & (chip > 0) & (quarter(chip - 1, y) == GROUP - 1)
        return ((t, sp + 2), fits & right, 3, 0), ((t, sp - 1), fits & left, 0, 3)

    for n in range(len(PIECES)):
        senders.extend(piece_sources(n))
        for when in range(3):
            receivers.extend(there for _, there, _, _ in piece_targets(n, when))

    for device, there in senders:
        def signal(device=device):
            pl.semaphore_signal(barrier, inc=1, device_id=device, device_id_type=MESH)

        pl.when(there)(signal)

    for load in small:
        load.wait()

    def cells(b):
        return pl.ds(pl.multiple_of(b * BS, BS), BS)

    def begin(b):
        own = guess[0, :, cells(b)]
        nodes[b, 0:4] = jnp.where(tm == 0, start[:, cells(b)], own)
        nodes[b, 4:8] = own

    rows_loop(0, rows, begin)

    pl.semaphore_wait(barrier, sum(jnp.asarray(there).astype(jnp.int32) for there in receivers))

    def unit_copies(unit, at, device):
        src, dst = pl.ds(unit * W, W), pl.ds(pl.multiple_of(at * W, W), W)
        pairs = ((off_h, win_off), (coarse_h, win_coarse), (rates_h, win_rates), (diag_h, win_diag))
        copies = []
        for n, (a, b) in enumerate(pairs):
            if device is None:
                copies.append(pltpu.make_async_copy(a.at[src], b.at[dst], unit_recv.at[at, n]))
            else:
                copies.append(remote(a.at[src], b.at[dst], unit_send.at[unit, n], unit_recv.at[at, n], device))
        return copies

    def unit_plan():
        plan = []
        for unit in range(4):
            at = unit - 2 * mine + 1
            plan.append((unit, at, (tm, sp + 1), (core == 0) & (at >= 0) & (at < 4)))
            at = unit + 4 - 2 * mine + 1
            plan.append((unit, at, None, on_chain & (at >= 0) & (at < 4)))
        return plan

    def piece_copies(n, unit, at, device, row):
        first, count = PIECES[n]
        src, dst = pl.ds(unit * W + first, count), pl.ds(at * W + first, count)
        copies = [
            remote(off_h.at[src], win_off.at[dst], piece_send.at[row, 0], piece_recv.at[n, 0], device),
            remote(coarse_h.at[src], win_coarse.at[dst], piece_send.at[row, 1], piece_recv.at[n, 1], device),
        ]
        if n == 0:
            src, dst = pl.ds(unit * W, W), pl.ds(at * W, W)
            copies.append(remote(rates_h.at[src], win_rates.at[dst], piece_send.at[row, 2], piece_recv.at[n, 2], device))
        return copies

    def pieces(when, act):
        for n in range(len(PIECES)):
            for device, there, unit, at in piece_targets(n, when):
                def go(n=n, unit=unit, at=at, device=device):
                    for copy in piece_copies(n, unit, at, device, n + when * len(PIECES)):
                        act(copy)

                pl.when(there)(go)

    def cols_copy(which):
        slot, device = ((1, (tm, sp + 1)), (3, (tm, sp - 1)), (0, (tm, sp + 2)))[which]
        return remote(cols_h, cols_land.at[slot], cols_send.at[which], cols_recv.at[slot], device)

    def cols_plan():
        next_low = quarter(chip + 1, line) == 0
        last_high = quarter(chip - 1, line) == GROUP - 1
        return (
            (0, core == 0),
            (1, (core == 0) & (chip > 0) & last_high),
            (2, on_chain & (chip < n_sp // 2 - 1) & next_low),
        )

    def weights_out():
        for which, there in cols_plan():
            pl.when(there)(cols_copy(which).start)
        for unit, at, device, there in unit_plan():
            def go(unit=unit, at=at, device=device):
                copies = unit_copies(unit, at, device)
                for copy in copies[:3]:
                    copy.start()
                pl.when((at == 1) | (at == 2))(copies[3].start)

            pl.when(there)(go)

    def weights_sent():
        for which, there in cols_plan():
            pl.when(there)(cols_copy(which).wait_send)
        for unit, at, device, there in unit_plan():
            if device is None:
                continue

            def done(unit=unit, at=at, device=device):
                copies = unit_copies(unit, at, device)
                for copy in copies[:3]:
                    copy.wait_send()
                pl.when((at == 1) | (at == 2))(copies[3].wait_send)

            pl.when(there)(done)


    def halo_copies(kind, count):
        to_left = remote(
            send_b.at[kind, LEFT, pl.ds(0, count)], land.at[kind, RIGHT, pl.ds(0, count)],
            send_sem.at[kind, LEFT], recv_sem.at[kind, RIGHT], (tm, sp - 1),
        )
        to_right = remote(
            send_b.at[kind, RIGHT, pl.ds(0, count)], land.at[kind, LEFT, pl.ds(0, count)],
            send_sem.at[kind, RIGHT], recv_sem.at[kind, LEFT], (tm, sp + 1),
        )
        return to_left, to_right

    def tile(values):
        return jnp.concatenate(values, axis=0).astype(jnp.bfloat16)

    def halo_send(kind, fields):
        for f, field in enumerate(fields):
            for j in range(edge):
                send_b[kind, LEFT, f * edge + j] = tile([field(4 * j + g) for g in range(4)])
                send_b[kind, RIGHT, f * edge + j] = tile([field(rows - W + 4 * j + g) for g in range(4)])
        to_left, to_right = halo_copies(kind, edge * len(fields))
        pl.when(has_left)(to_left.start)
        pl.when(has_right)(to_right.start)

    def halo_wait(kind, count):
        to_left, to_right = halo_copies(kind, edge * count)

        @pl.when(has_left)
        def _():
            to_right.wait_recv()
            to_left.wait_send()

        @pl.when(has_right)
        def _():
            to_left.wait_recv()
            to_right.wait_send()

    def spread(block_tile, target, block, row):
        wide = block_tile.astype(jnp.float32)
        for g in range(4):
            target[block + g, row : row + 4] = wide[4 * g : 4 * g + 4]

    def halo_place(kind, target, count):
        for f in range(count):
            for j in range(edge):
                spread(land[kind, LEFT, f * edge + j], target, 4 * j, 4 * f)
                spread(land[kind, RIGHT, f * edge + j], target, W + rows + 4 * j, 4 * f)

    def gather(source, places, b):
        return jnp.concatenate([source[places[b, k]] for k in range(K)], axis=1)

    def react(v, rate):
        total = None
        for t in range(SPECIES):
            line_t = v[t : t + 1]
            if v.shape[0] == 8:
                second = v[4 + t : 5 + t]
                row = lax.broadcasted_iota(jnp.int32, (8, BS), 0)
                line_t = jnp.where(row < 4, jnp.broadcast_to(line_t, (8, BS)), jnp.broadcast_to(second, (8, BS)))
            term = mix_v[t, : v.shape[0]] * line_t
            total = term if total is None else total + term
        return total * rate

    def paired(first, second, weights):
        got = dot(jnp.concatenate([first, second], axis=0), weights)
        return got[:8, :BS], got[8:, BS:]

    def explicit(b, count):
        got = dot(gather(near, place_of, b), raw_w[b])[: 4 * count]
        return got + react(near[W + b, : 4 * count], rates[pl.ds(b, 1)])

    def transposed(n, carry):
        for r in range(4):
            b, half = 4 * n + r, pl.ds(BS * (r % 2), BS)
            diag_w[2 * n + r // 2, :, half] = diag_v[b].T
            fine_w[2 * n + r // 2, :, half] = fine_v[b].T
            for k in range(K):
                raw_w[b, BS * k : BS * (k + 1)] = off_v[b, k].T
        return carry

    def outer(*bodies):
        for body in bodies:
            rows_loop(0, W // 2, body)
            rows_loop((rows - W) // 2, rows // 2, body)

    def inner(*bodies):
        for body in bodies:
            rows_loop(W // 2, (rows - W) // 2, body)

    def solve(target):
        def pair(i):
            got = paired(right_v[2 * i], right_v[2 * i + 1], fine_w[i])
            target[2 * i], target[2 * i + 1] = got[0][:4], got[1][:4]

        return pair

    def terms_copies(it, late):
        slot = tm % STRETCH
        main = terms_land.at[slot]
        to = [chain_device(i, chain_plane(it, tm)) for i in (low, high, low - 1, high + 1)]

        def piece(first, count, at, n, sem, device):
            return remote(
                terms_b.at[it, pl.ds(first, count)], main.at[pl.ds(at, count)], terms_send.at[it, n],
                terms_recv.at[slot, sem], device,
            )

        if late:
            return (
                (piece(0, 2, 2, 0, 0, to[0]), True),
                (piece(6, 2, 4, 1, 0, to[1]), True),
                (piece(0, 2, 6, 2, 1, to[2]), has_left),
                (piece(6, 2, 0, 3, 1, to[3]), has_right),
            )
        return (piece(2, 4, 4, 4, 2, to[0]), True), (piece(2, 4, 0, 5, 2, to[1]), True)

    def terms_out(it, late):
        for j in (0, 1, 6, 7) if late else range(2, 6):
            terms_b[it, j, 0] = tile([sum_c[4 * j + g] for g in range(4)])
            terms_b[it, j, 1] = tile([sum_t[4 * j + g] for g in range(4)])
        for copy, there in terms_copies(it, late):
            if there is True:
                copy.start()
            else:
                pl.when(there)(copy.start)

    def terms_sent(it):
        for copy, there in terms_copies(it, True) + terms_copies(it, False):
            if there is True:
                copy.wait_send()
            else:
                pl.when(there)(copy.wait_send)

    def fine(it):
        @pl.when(it == 0)
        def _():
            halo_send(NODES, [lambda b: nodes[b, 0:4], lambda b: nodes[b, 4:8]])
            first_things()
            pl.when(tm == 0)(start_out)
            for load in large:
                load.wait()
            lax.fori_loop(0, rows // 4, transposed, 0)
            for b in range(rows):
                near[W + b] = nodes[b]
            halo_wait(NODES, 2)
            halo_place(NODES, near, 2)

        @pl.when(it == 1)
        def _():
            @pl.when(tm > 0)
            def _():
                values_wait(0, 0, True)
                for j in range(rows // 4):
                    spread(value_land[0, 0, j], nodes, 4 * j, 0)
                    spread(value_land[0, 0, j], near, W + 4 * j, 0)
                for j in range(edge):
                    spread(value_halo[0, LEFT, j], near, 4 * j, 0)
                    spread(value_halo[0, RIGHT, j], near, W + rows + 4 * j, 0)

            @pl.when(tm == 0)
            def _():
                for b in range(rows):
                    near[W + b, 0:4] = nodes[b, 0:4]
                for j in range(edge):
                    spread(land[NODES, LEFT, j], near, 4 * j, 0)
                    spread(land[NODES, RIGHT, j], near, W + rows + 4 * j, 0)

            values_wait(0, 1, True)
            for j in range(rows // 4):
                spread(value_land[0, 1, j], near, W + 4 * j, 4)
            for j in range(edge):
                spread(value_halo[1, LEFT, j], near, 4 * j, 4)
                spread(value_halo[1, RIGHT, j], near, W + rows + 4 * j, 4)

        own_part = jnp.where(it == 0, 0.0, 0.5)
        end_part = jnp.where(it == 0, 1.0, 0.5)

        def node_terms(i):
            imps = paired(near[W + 2 * i], near[W + 2 * i + 1], diag_w[i])
            for b, imp in zip((2 * i, 2 * i + 1), imps):
                exp = explicit(b, 2)
                imp_0, exp_0, imp_2, exp_2 = imp[:4], exp[:4], imp[4:], exp[4:]
                one_i = imp_b[b] + own_part * imp_0 + end_part * imp_2
                one_e = exp_b[b] + own_part * exp_0 + end_part * exp_2
                f_0, f_1, f_2 = imp_0 + exp_0, one_i + one_e, imp_2 + exp_2
                right_v[b, 0:4] = (
                    nodes[b, 0:4] - HALF * one_i + STEP * (5 / 24 * f_0 + 1 / 3 * f_1 - 1 / 24 * f_2)
                )
                second_r[b] = STEP * (-1 / 24 * f_0 + 1 / 3 * f_1 + 5 / 24 * f_2) - HALF * (one_e + imp_2)
                sum_c[b] = STEP * (1 / 6 * f_0 - exp_0)
                sum_t[b] = (-STEP / 3) * f_0
                imp_b[b] = -0.5 * imp_0
                exp_b[b] = -0.5 * exp_0

        outer(node_terms, solve(first_v))
        halo_send(FIRST, [lambda b: first_v[b]])
        inner(node_terms, solve(first_v))

        def put_first(b):
            near[W + b, 0:4] = first_v[b]

        rows_loop(0, rows, put_first)
        early_units(it, 0)
        halo_wait(FIRST, 1)
        halo_place(FIRST, near, 1)

        def first_terms(i):
            imps = paired(near[W + 2 * i], near[W + 2 * i + 1], diag_w[i])
            for b, imp in zip((2 * i, 2 * i + 1), imps):
                imp = imp[:4]
                exp = explicit(b, 1)
                force = STEP * 2 / 3 * (imp + exp)
                right_v[b, 0:4] = first_v[b] + HALF * exp + second_r[b]
                sum_c[b] += force
                sum_t[b] += force
                imp_b[b] += imp
                exp_b[b] += exp

        outer(first_terms, solve(fresh))
        halo_send(SECOND, [lambda b: fresh[b]])
        inner(first_terms, solve(fresh))

        def put_second(b):
            near[W + b, 0:4] = fresh[b]
            mid_b[b] = first_v[b] - 0.5 * (nodes[b, 0:4] + fresh[b])

        rows_loop(0, rows, put_second)

        def second_terms(i):
            imps = paired(near[W + 2 * i], near[W + 2 * i + 1], diag_w[i])
            for b, imp in zip((2 * i, 2 * i + 1), imps):
                imp = imp[:4]
                exp = explicit(b, 1)
                force = imp + exp
                sum_c[b] += STEP * (1 / 6 * force - imp)
                sum_t[b] += (-STEP / 3) * force
                imp_b[b] += -0.5 * imp
                exp_b[b] += -0.5 * exp

        inner(second_terms)
        terms_out(it, False)
        early_units(it, 1)
        halo_wait(SECOND, 1)
        halo_place(SECOND, near, 1)
        outer(second_terms)
        terms_out(it, True)

    def values_wait(it, which, halos):
        for n in range(2):
            arrive(value_land.at[it, which, pl.ds(n * T_OWN, T_OWN)], value_recv.at[it, which, n])
        if halos:
            arrive(value_halo.at[which, LEFT], value_recv.at[it, which, 2], has_left)
            arrive(value_halo.at[which, RIGHT], value_recv.at[it, which, 3], has_right)

    def value_copies(j):
        it, p = round_here, stretch * STRETCH + j
        half = chunk % 2
        copies = []
        for which in (1, 0):
            t = p + 1 - which
            there = (p < n_tm - 1) & ~((p == STRETCH * (stretch + 1) - 1) & own_next) if which == 0 else True
            copies.append((remote(
                end_b.at[j], value_land.at[it, which, pl.ds(pl.multiple_of(half * T_OWN, T_OWN), T_OWN)],
                value_send.at[j, which, 0], value_recv.at[it, which, half], (t, owner)), there))
            copies.append((remote(
                end_b.at[j, pl.ds(pl.multiple_of(half * (T_OWN - T_EDGE), T_EDGE), T_EDGE)], value_halo.at[which, 1 - half],
                value_send.at[j, which, 1], value_recv.at[it, which, 3 - half], (t, beside)),
                (t < n_tm) & has_beside & (it == 0)))
        return copies

    def value_here(j):
        half = chunk % 2
        return pltpu.make_async_copy(
            end_b.at[j], value_land.at[round_here, 0, pl.ds(pl.multiple_of(half * T_OWN, T_OWN), T_OWN)],
            value_recv.at[round_here, 0, half],
        )

    def chain_copies(j, half):
        inside = j < STRETCH - 1
        target = jnp.where(inside, j + 1, 0)
        z = jnp.where(inside, plane, plane - 2)
        there = inside | later
        at = pl.ds(half * T_EDGE, T_EDGE)
        copies = []
        for n, (i, ok) in enumerate(((chunk - 1, chunk_left), (chunk + 1, chunk_right))):
            part = 2 - 2 * n
            copies.append((remote(
                end_b.at[j, at], chain_land.at[target, part, at], chain_send.at[j, 2 * n, half],
                chain_recv.at[target, part, half], chain_device(i, z)), there & ok))
        if half == 1:
            copies.append((remote(
                end_b.at[j], chain_land.at[target, 1], chain_send.at[j, 1, 0], chain_recv.at[target, 1, 0],
                chain_device(chunk, z)), there & ~inside))
        return copies

    def start_copies(it):
        copies = []
        for n, (i, part, own, ok) in enumerate((
            (low, 1, 0, True), (low, 2, 1, True), (low - 1, 2, 0, has_left),
            (high, 1, 1, True), (high, 0, 0, True), (high + 1, 0, 1, has_right),
        )):
            device = chain_device(i, chain_plane(it, 0))
            for half in range(2):
                count = T_OWN if part == 1 else T_EDGE
                if part == 1 and half == 1:
                    continue
                copies.append((remote(
                    start_b.at[pl.ds(own * T_OWN + half * T_EDGE, count)],
                    chain_land.at[0, part, pl.ds(half * T_EDGE, count)], start_send.at[it, n, half],
                    chain_recv.at[0, part, half], device), (tm == 0) & ok))
        return copies

    def first_things():
        pieces(0, lambda copy: copy.start())
        pl.when(plane == first_plane)(weights_out)
        def local_place(b, carry):
            for k in range(K):
                place_of[b, k] = jnp.clip(cols[k, b] - (sp * rows - W), 0, rows + 2 * W - 1)
            return carry

        lax.fori_loop(0, rows, local_place, 0)
        near[...] = jnp.zeros_like(near)
        near_q[...] = jnp.zeros_like(near_q)
        imp_b[...] = jnp.zeros_like(imp_b)
        exp_b[...] = jnp.zeros_like(exp_b)
        for t in range(SPECIES):
            column = jnp.broadcast_to(mixing[:, t : t + 1], (SPECIES, BS))
            mix_v[t] = jnp.concatenate([column, column], axis=0)

    def start_out():
        for j in range(rows // 4):
            start_b[j] = tile([nodes[4 * j + g, 0:4] for g in range(4)])
        for copy, there in start_copies(0):
            pl.when(there)(copy.start)

    def composed(n, carry):
        for r in range(4):
            w = 4 * n + r
            inverse = win_coarse[w].T
            comp_w[w, BS : 2 * BS] = inverse
            inverse_w[2 * n + r // 2, :, BS * (r % 2) : BS * (r % 2 + 1)] = inverse
            raw = [win_diag[w]] + [win_off[w, k] for k in range(K)]
            got = (dot(jnp.concatenate([block.T for block in raw], axis=0), inverse) * STEP).astype(jnp.bfloat16)
            comp_w[w, :BS] = got[:BS]
            comp_w[w, 2 * BS :] = got[BS:]
        return carry

    def window_unit(at, foreign=True):
        unit = 2 * mine - 1 + at

        @pl.when((unit >= 0) & (unit < 8))
        def _():
            copies = unit_copies(0, at, (tm, sp))
            for copy in copies[:3] if at in (0, 3) else copies:
                copy.wait_recv()

        if at in (0, 3) and foreign:
            there = lower if at == 0 else upper
            for n in range(len(PIECES)):
                @pl.when(there)
                def _(n=n):
                    for copy in piece_copies(n, 0, at, (tm, sp), n):
                        copy.wait_recv()

        lax.fori_loop(W // 4 * at, W // 4 * (at + 1), composed, 0)

    def window_places():
        first_unit = 2 * mine - 1
        arrive(cols_land.at[1], cols_recv.at[1])
        arrive(cols_land.at[0], cols_recv.at[0], lower)
        arrive(cols_land.at[3], cols_recv.at[3], upper)
        to_scalars = pltpu.make_async_copy(cols_land, cols_s, cols_send.at[3])
        to_scalars.start()
        to_scalars.wait()

        def places(w, carry):
            unit = first_unit + w // W
            slot, row = (unit + 4) // 4, (unit + 4) % 4 * W + w % W
            for k in range(K):
                column = jnp.where(slot == 2, cols[k, row], cols_s[slot, k, row])
                place_w[w, k] = jnp.clip(column - (chunk * OWN - 2 * W), 0, OWN + 4 * W - 1)
            return carry

        lax.fori_loop(0, WINDOW, places, 0)

    hurry = on_chain & (plane == first_plane)

    def early_units(it, step):
        @pl.when((it == 0) & hurry)
        def _():
            if step == 0:
                window_places()
                window_unit(1)
            else:
                window_unit(2)
                pl.when(mine != GROUP - 1)(functools.partial(window_unit, 3, False))
                pl.when(mine == GROUP - 1)(functools.partial(window_unit, 0, False))

    def window_weights():
        @pl.when(~hurry)
        def _():
            window_places()
            for at in range(4):
                window_unit(at)

        @pl.when(hurry)
        def _():
            pl.when(mine == GROUP - 1)(functools.partial(window_unit, 3))
            pl.when(mine != GROUP - 1)(functools.partial(window_unit, 0))

    def chain_step(g, carry):
        halo_at = jnp.where(even, 0, 6)
        early_at, late_at = jnp.where(even, 4, 0), jnp.where(even, 2, 4)

        @pl.when(g == 0)
        def _():
            arrive(chain_land.at[g, 1], chain_recv.at[g, 1, 0])
            for n in range(T_OWN):
                spread(chain_land[g, 1, n], near, 2 * W + 4 * n, 0)

        arrive(terms_land.at[g, pl.ds(early_at, 4)], terms_recv.at[g, 2])
        arrive(terms_land.at[g, pl.ds(late_at, 2)], terms_recv.at[g, 0])
        arrive(terms_land.at[g, pl.ds(halo_at, 2)], terms_recv.at[g, 1], has_beside)

        def prepare(n):
            constant = terms_land[g, n, 0].astype(jnp.float32)
            for r in range(4):
                w = 4 * n + r
                own = near[W + w, 0:4]
                change = STEP * react(own, win_rates[pl.ds(w, 1)])
                right_v[w, 0:4] = own + change + constant[4 * r : 4 * r + 4]
                state[w] = 2.0 * own + change
            for i in (2 * n, 2 * n + 1):
                got = paired(right_v[2 * i], right_v[2 * i + 1], inverse_w[i])
                solved[2 * i], solved[2 * i + 1] = got[0][:4], got[1][:4]

        rows_loop(T_EDGE, T_WINDOW - T_EDGE, prepare)

        def with_rest(n):
            constant = terms_land[g, T_EDGE + n, 1].astype(jnp.float32)
            for r in range(4):
                state[W + 4 * n + r] += 2.0 * constant[4 * r : 4 * r + 4]

        rows_loop(0, T_OWN, with_rest)

        def middle(w):
            spread_s = dot(gather(near, place_w, w), comp_w[w, 2 * BS :])[:4]
            near_q[W + w, 0:4] = solved[w] + spread_s
            partial[w] = 0.5 * spread_s

        first, last = pl.ds(0, T_EDGE), pl.ds(T_EDGE, T_EDGE)
        arrive(chain_land.at[g, 2, first], chain_recv.at[g, 2, 0], chunk_right)
        for n in range(T_EDGE):
            spread(chain_land[g, 2, n], near, 2 * W + OWN + 4 * n, 0)
        rows_loop(T_WINDOW - T_EDGE, T_WINDOW, prepare)
        rows_loop(2 * W, 2 * W + W, middle)
        arrive(chain_land.at[g, 0, first], chain_recv.at[g, 0, 0], chunk_left)
        arrive(chain_land.at[g, 0, last], chain_recv.at[g, 0, 1], chunk_left)
        arrive(chain_land.at[g, 2, last], chain_recv.at[g, 2, 1], chunk_right)
        for n in range(T_OWN):
            spread(chain_land[g, 0, n], near, 4 * n, 0)
        for n in range(T_EDGE, T_OWN):
            spread(chain_land[g, 2, n], near, 2 * W + OWN + 4 * n, 0)
        rows_loop(0, T_EDGE, prepare)
        rows_loop(0, 2 * W, middle)
        rows_loop(3 * W, WINDOW, middle)

        def end(o):
            w = W + o
            own, mid = near[W + w, 0:4], near_q[W + w, 0:4]
            right = state[w] + STEP * react(mid, win_rates[pl.ds(w, 1)])
            parts = jnp.concatenate([own - mid, right, gather(near_q, place_w, w)[:4]], axis=1)
            near[W + w, 0:4] = partial[w] + 0.5 * dot(parts, comp_w[w])

        for half in range(2):
            rows_loop(half * W, (half + 1) * W, end)
            for n in range(half * T_EDGE, (half + 1) * T_EDGE):
                end_b[g, n] = tile([near[2 * W + 4 * n + r, 0:4] for r in range(4)])
            for copy, there in chain_copies(g, half):
                pl.when(there)(copy.start)
        pl.when((g == STRETCH - 1) & own_next)(lambda: value_here(g).start())
        for copy, there in value_copies(g):
            if there is True:
                copy.start()
            else:
                pl.when(there)(copy.start)
        return carry

    def round_of(it, carry):
        fine(it)

        @pl.when(it == 0)
        def _():
            terms_sent(0)

            @pl.when(tm == 0)
            def _():
                for copy, there in start_copies(1):
                    pl.when(there)(copy.start)

            pieces(1, lambda copy: copy.start())
            pieces(2, lambda copy: copy.start())
            pl.when(plane != first_plane)(weights_out)

        composes = jnp.where((plane == 0) & (line == 0), 1, 0)
        pl.when(on_chain & (it == composes))(window_weights)

        @pl.when(on_chain & (it == stretch))
        def _():
            lax.fori_loop(0, STRETCH, chain_step, 0)

        return carry

    lax.fori_loop(0, ITERS, round_of, 0)

    weights_sent()
    for when in range(3):
        pieces(when, lambda copy: copy.wait_send())
    for it in range(ITERS):
        for copy, there in start_copies(it):
            pl.when(there)(copy.wait_send)
    terms_sent(1)

    @pl.when(on_chain)
    def _():
        def sent(g, carry):
            for copy, there in chain_copies(g, 0) + chain_copies(g, 1) + value_copies(g):
                if there is True:
                    copy.wait_send()
                else:
                    pl.when(there)(copy.wait_send)
            return carry

        lax.fori_loop(0, STRETCH, sent, 0)

    pl.when(tm > 0)(lambda: values_wait(1, 0, False))
    values_wait(1, 1, False)

    def write(j):
        ends = value_land[1, 1, j].astype(jnp.float32)
        starts = value_land[1, 0, j].astype(jnp.float32)
        for g in range(4):
            b = 4 * j + g
            own = jnp.where(tm == 0, start[:, cells(b)], starts[4 * g : 4 * g + 4])
            last = ends[4 * g : 4 * g + 4]
            out[0, 0, :, cells(b)] = own
            out[0, 1, :, cells(b)] = mid_b[b] + 0.5 * (own + last)
            out[0, 2, :, cells(b)] = last

    rows_loop(0, rows // 4, write)


def shards(n_tm, n_sp, start, guess, diag, off, columns, rates, mixing, fine, coarse):
    rows = diag.shape[0]
    f32, bf16 = jnp.float32, jnp.bfloat16
    vmem = pl.BlockSpec(memory_space=pltpu.VMEM)
    hbm = pl.BlockSpec(memory_space=pltpu.HBM)
    dma = pltpu.SemaphoreType.DMA
    edge = W // 4
    slots = STRETCH

    def tiles(*lead):
        return pltpu.VMEM((*lead, 16, BS), bf16)

    def blocks(*lead):
        return pltpu.VMEM((*lead, BS, BS), bf16)

    pairs = pltpu.VMEM((rows // 2, BS, 2 * BS), bf16)
    scratch = [
        pltpu.VMEM((SPECIES, rows * BS), f32), pltpu.VMEM((1, SPECIES, rows * BS), f32),
        pltpu.SMEM((K, rows), jnp.int32), pltpu.VMEM((rows, BS), f32), pltpu.VMEM((SPECIES, SPECIES), f32),
        blocks(rows), blocks(rows, K), blocks(rows),
        pltpu.VMEM((rows, K * BS, BS), bf16), pairs, pairs,
        blocks(WINDOW), blocks(WINDOW, K), blocks(WINDOW), pltpu.VMEM((WINDOW, BS), f32),
        pltpu.VMEM((WINDOW, (K + 2) * BS, BS), bf16),
        pltpu.VMEM((WINDOW // 2, BS, 2 * BS), bf16),
        pltpu.VMEM((rows + 2 * W, 8, BS), f32), pltpu.VMEM((rows + 2 * W, 8, BS), f32),
        pltpu.VMEM((SPECIES, 8, BS), f32), pltpu.VMEM((rows, 8, BS), f32),
        *[pltpu.VMEM((rows, SPECIES, BS), f32)] * 11, pltpu.VMEM((rows, 8, BS), f32),
        tiles(3, 2, 2 * edge), tiles(3, 2, 2 * edge),
        tiles(ITERS, rows // 4, 2), tiles(slots, T_WINDOW, 2),
        tiles(rows // 4), tiles(slots, 3, T_OWN), tiles(slots, T_OWN),
        tiles(ITERS, 2, rows // 4), tiles(2, 2, edge),
        pltpu.VMEM((4, K, rows), jnp.int32), pltpu.SMEM((4, K, rows), jnp.int32),
        pltpu.SMEM((rows, K), jnp.int32), pltpu.SMEM((WINDOW, K), jnp.int32),
        dma((8,)), dma((3, 2)), dma((3, 2)), dma((4, 4)), dma((4, 4)), dma((4,)), dma((4,)),
        dma((3 * len(PIECES), 3)), dma((len(PIECES), 3)),
        dma((ITERS, 6)), dma((slots, 3)), dma((ITERS, 6, 2)), dma((slots, 3, 2)), dma((slots, 3, 2)),
        dma((slots, 2, 2)), dma((ITERS, 2, 4)),
    ]
    return pl.pallas_call(
        functools.partial(kernel, n_tm, n_sp, rows),
        out_shape=jax.ShapeDtypeStruct((1, 3, SPECIES, rows * BS), f32),
        in_specs=[hbm] * 9,
        out_specs=vmem,
        scratch_shapes=scratch,
        compiler_params=pltpu.CompilerParams(
            collective_id=0, has_side_effects=True, vmem_limit_bytes=60 << 20
        ),
    )(start, guess, columns.T, rates.reshape(rows, BS), mixing, diag, off, fine, coarse)


def solution(mesh):
    in_specs = (
        P(None, "space"),
        P("tm", None, "space"),
        P("space", None, None),
        P("space", None, None, None),
        P("space", None),
        P("space"),
        P(),
        P("space", None, None),
        P("space", None, None),
    )
    out_specs = P("tm", None, None, "space")
    body = functools.partial(shards, mesh.shape["tm"], mesh.shape["space"])
    return jax.shard_map(body, mesh=mesh, in_specs=in_specs, out_specs=out_specs, check_vma=False)
```

```python
import functools

import jax
import jax.numpy as jnp
from jax import lax
from jax.experimental import pallas as pl
from jax.experimental.pallas import tpu as pltpu
from jax.sharding import PartitionSpec as P

BS = 128
K = 4
SPECIES = 4
ITERS = 2
W = 8
STEP = 0.25
HALF = STEP / 2
MESH = pl.DeviceIdType.MESH
NODES, FIRST, SECOND = range(3)
LEFT, RIGHT = 0, 1
GROUP = 4
STRETCH = 8
OWN = 16
WINDOW = OWN + 2 * W
T_OWN, T_WINDOW, T_EDGE = OWN // 4, WINDOW // 4, W // 4
PIECES = ((0, 1), (1, 2), (3, 1), (4, 2), (6, 2))
FIRST_FROM = ((0, 0), (0, 1), (0, GROUP - 1), (1, 0), (GROUP - 1, 0))
OTHERS_FROM = ((0, 0), (0, 1), (0, GROUP - 1), (0, 0), (0, GROUP - 1))


def dot(lhs, rhs):
    return lax.dot_general(
        lhs.astype(jnp.bfloat16), rhs, (((1,), (0,)), ((), ())), preferred_element_type=jnp.float32
    )


def rows_loop(first, last, body):
    def step(i, carry):
        body(i)
        return carry

    lax.fori_loop(first, last, step, 0, unroll=True)


def kernel(
    n_tm, n_sp, rows,
    start_h, guess_h, cols_h, rates_h, mixing_h, diag_h, off_h, fine_h, coarse_h,
    out,
    start, guess, cols, rates, mixing,
    diag_v, off_v, fine_v, raw_w, diag_w, fine_w, win_diag, win_off, win_coarse, win_rates, comp_w, inverse_w,
    near, near_q, mix_v, nodes, imp_b, exp_b, mid_b, first_v, second_r,
    sum_c, sum_t, state, solved, partial, fresh, right_v,
    send_b, land, terms_b, terms_land, start_b, chain_land, end_b, value_land, value_halo,
    cols_land, cols_s, place_of, place_w,
    load_sem, send_sem, recv_sem, unit_send, unit_recv, cols_send, cols_recv, piece_send, piece_recv,
    terms_send, terms_recv, start_send, chain_send, chain_recv, value_send, value_recv,
):
    tm = lax.axis_index("tm")
    sp = lax.axis_index("space")
    plane, line, chip, core = tm // GROUP, tm % GROUP, sp // 2, sp % 2
    has_left, has_right = sp > 0, sp < n_sp - 1
    edge = W // 4
    chunks = n_sp * rows // OWN

    def quarter(x, y):
        return jnp.where(x % 2 == 0, y, GROUP - 1 - y)

    def chain_device(i, z):
        x, j = i // GROUP, i % GROUP
        return z * GROUP + quarter(x, j), 2 * x + 1

    def chain_plane(it, p):
        return jnp.where(p < STRETCH, 2, 0) + it

    mine = quarter(chip, line)
    chunk = GROUP * chip + mine
    round_here, stretch = plane % 2, jnp.where(plane < 2, 1, 0)
    on_chain = core == 1
    even = chunk % 2 == 0
    chunk_left, chunk_right = chunk > 0, chunk < chunks - 1
    owner = chunk // 2
    beside = jnp.where(even, owner - 1, owner + 1)
    has_beside = (even & chunk_left) | (~even & chunk_right)
    low, high = 2 * sp, 2 * sp + 1

    def remote(src, dst, out_sem, in_sem, device):
        return pltpu.make_async_remote_copy(
            src_ref=src, dst_ref=dst, send_sem=out_sem, recv_sem=in_sem,
            device_id=device, device_id_type=MESH,
        )

    def arrive(dst, in_sem, there=None):
        def wait():
            remote(dst, dst, send_sem.at[0, 0], in_sem, (tm, sp)).wait_recv()

        if there is None:
            wait()
        else:
            pl.when(there)(wait)

    loads = [
        pltpu.make_async_copy(src, dst, load_sem.at[i])
        for i, (src, dst) in enumerate((
            (mixing_h, mixing), (guess_h, guess), (start_h, start), (cols_h, cols), (rates_h, rates),
            (diag_h, diag_v), (off_h, off_v), (fine_h, fine_v),
        ))
    ]
    for load in loads:
        load.start()
    small, large = loads[:5], loads[5:]
    cols_land[...] = jnp.zeros_like(cols_land)

    barrier = pltpu.get_barrier_semaphore()
    later = stretch == 0
    senders, receivers = [], []
    own_next = ((stretch + 1) * STRETCH == tm) & (owner == sp)

    def is_me(device):
        return (device[0] == tm) & (device[1] == sp)


    def both(device, there):
        senders.append((device, there))
        receivers.append(there)

    both((tm, sp - 1), has_left)
    both((tm, sp + 1), has_right)
    for i, there in ((low - 1, has_left), (low, True), (high, True), (high + 1, has_right)):
        for it in range(ITERS):
            both(chain_device(i, chain_plane(it, tm)), there)
            device = chain_device(i, chain_plane(it, 0))
            senders.append((device, there & (tm == STRETCH) & ~is_me(device)))
    for j in range(STRETCH):
        both((stretch * STRETCH + j, owner), on_chain)
        both((stretch * STRETCH + j, beside), on_chain & has_beside)
    receivers.append(on_chain & later & ~own_next)
    receivers.append(on_chain & later & has_beside)
    both(chain_device(chunk - 1, plane), on_chain & chunk_left)
    both(chain_device(chunk + 1, plane), on_chain & chunk_right)
    for i, there in ((chunk, True), (chunk - 1, chunk_left), (chunk + 1, chunk_right)):
        senders.append((chain_device(i, plane + 2), on_chain & ~later & there))
        receivers.append(on_chain & later & there)

    first_plane = 2
    lower = on_chain & (mine == 0) & (chip > 0)
    upper = on_chain & (mine == GROUP - 1) & (chip < n_sp // 2 - 1)

    def piece_sources(n):
        t_first, t_others = (
            (plane + dz) % GROUP * GROUP + (line + dy) % GROUP for dz, dy in (FIRST_FROM[n], OTHERS_FROM[n])
        )
        t = jnp.where(plane == first_plane, t_first, t_others)
        return ((t, sp - 2), lower), ((t, sp + 1), upper)

    def piece_targets(n, when):
        dz, dy = OTHERS_FROM[n] if when else FIRST_FROM[n]
        z, y = (plane + GROUP - dz) % GROUP, (line + GROUP - dy) % GROUP
        t = z * GROUP + y
        hurried = z == 0
        fits = z == first_plane if when == 0 else (z != first_plane) & ~hurried if when == 1 else hurried
        right = on_chain & (chip < n_sp // 2 - 1) & (quarter(chip + 1, y) == 0)
        left = ~on_chain & (chip > 0) & (quarter(chip - 1, y) == GROUP - 1)
        return ((t, sp + 2), fits & right, 3, 0), ((t, sp - 1), fits & left, 0, 3)

    for n in range(len(PIECES)):
        senders.extend(piece_sources(n))
        for when in range(3):
            receivers.extend(there for _, there, _, _ in piece_targets(n, when))

    for device, there in senders:
        def signal(device=device):
            pl.semaphore_signal(barrier, inc=1, device_id=device, device_id_type=MESH)

        pl.when(there)(signal)

    for load in small:
        load.wait()

    def cells(b):
        return pl.ds(pl.multiple_of(b * BS, BS), BS)

    def begin(b):
        own = guess[0, :, cells(b)]
        nodes[b, 0:4] = jnp.where(tm == 0, start[:, cells(b)], own)
        nodes[b, 4:8] = own

    rows_loop(0, rows, begin)

    pl.semaphore_wait(barrier, sum(jnp.asarray(there).astype(jnp.int32) for there in receivers))

    def unit_copies(unit, at, device):
        src, dst = pl.ds(unit * W, W), pl.ds(pl.multiple_of(at * W, W), W)
        pairs = ((off_h, win_off), (coarse_h, win_coarse), (rates_h, win_rates), (diag_h, win_diag))
        copies = []
        for n, (a, b) in enumerate(pairs):
            if device is None:
                copies.append(pltpu.make_async_copy(a.at[src], b.at[dst], unit_recv.at[at, n]))
            else:
                copies.append(remote(a.at[src], b.at[dst], unit_send.at[unit, n], unit_recv.at[at, n], device))
        return copies

    def unit_plan():
        plan = []
        for unit in range(4):
            at = unit - 2 * mine + 1
            plan.append((unit, at, (tm, sp + 1), (core == 0) & (at >= 0) & (at < 4)))
            at = unit + 4 - 2 * mine + 1
            plan.append((unit, at, None, on_chain & (at >= 0) & (at < 4)))
        return plan

    def piece_copies(n, unit, at, device, row):
        first, count = PIECES[n]
        src, dst = pl.ds(unit * W + first, count), pl.ds(at * W + first, count)
        copies = [
            remote(off_h.at[src], win_off.at[dst], piece_send.at[row, 0], piece_recv.at[n, 0], device),
            remote(coarse_h.at[src], win_coarse.at[dst], piece_send.at[row, 1], piece_recv.at[n, 1], device),
        ]
        if n == 0:
            src, dst = pl.ds(unit * W, W), pl.ds(at * W, W)
            copies.append(remote(rates_h.at[src], win_rates.at[dst], piece_send.at[row, 2], piece_recv.at[n, 2], device))
        return copies

    def pieces(when, act):
        for n in range(len(PIECES)):
            for device, there, unit, at in piece_targets(n, when):
                def go(n=n, unit=unit, at=at, device=device):
                    for copy in piece_copies(n, unit, at, device, n + when * len(PIECES)):
                        act(copy)

                pl.when(there)(go)

    def cols_copy(which):
        slot, device = ((1, (tm, sp + 1)), (3, (tm, sp - 1)), (0, (tm, sp + 2)))[which]
        return remote(cols_h, cols_land.at[slot], cols_send.at[which], cols_recv.at[slot], device)

    def cols_plan():
        next_low = quarter(chip + 1, line) == 0
        last_high = quarter(chip - 1, line) == GROUP - 1
        return (
            (0, core == 0),
            (1, (core == 0) & (chip > 0) & last_high),
            (2, on_chain & (chip < n_sp // 2 - 1) & next_low),
        )

    def weights_out():
        for which, there in cols_plan():
            pl.when(there)(cols_copy(which).start)
        for unit, at, device, there in unit_plan():
            def go(unit=unit, at=at, device=device):
                copies = unit_copies(unit, at, device)
                for copy in copies[:3]:
                    copy.start()
                pl.when((at == 1) | (at == 2))(copies[3].start)

            pl.when(there)(go)

    def weights_sent():
        for which, there in cols_plan():
            pl.when(there)(cols_copy(which).wait_send)
        for unit, at, device, there in unit_plan():
            if device is None:
                continue

            def done(unit=unit, at=at, device=device):
                copies = unit_copies(unit, at, device)
                for copy in copies[:3]:
                    copy.wait_send()
                pl.when((at == 1) | (at == 2))(copies[3].wait_send)

            pl.when(there)(done)


    def halo_copies(kind, count):
        to_left = remote(
            send_b.at[kind, LEFT, pl.ds(0, count)], land.at[kind, RIGHT, pl.ds(0, count)],
            send_sem.at[kind, LEFT], recv_sem.at[kind, RIGHT], (tm, sp - 1),
        )
        to_right = remote(
            send_b.at[kind, RIGHT, pl.ds(0, count)], land.at[kind, LEFT, pl.ds(0, count)],
            send_sem.at[kind, RIGHT], recv_sem.at[kind, LEFT], (tm, sp + 1),
        )
        return to_left, to_right

    def tile(values):
        return jnp.concatenate(values, axis=0).astype(jnp.bfloat16)

    def halo_send(kind, fields):
        for f, field in enumerate(fields):
            for j in range(edge):
                send_b[kind, LEFT, f * edge + j] = tile([field(4 * j + g) for g in range(4)])
                send_b[kind, RIGHT, f * edge + j] = tile([field(rows - W + 4 * j + g) for g in range(4)])
        to_left, to_right = halo_copies(kind, edge * len(fields))
        pl.when(has_left)(to_left.start)
        pl.when(has_right)(to_right.start)

    def halo_wait(kind, count):
        to_left, to_right = halo_copies(kind, edge * count)

        @pl.when(has_left)
        def _():
            to_right.wait_recv()
            to_left.wait_send()

        @pl.when(has_right)
        def _():
            to_left.wait_recv()
            to_right.wait_send()

    def spread(block_tile, target, block, row):
        wide = block_tile.astype(jnp.float32)
        for g in range(4):
            target[block + g, row : row + 4] = wide[4 * g : 4 * g + 4]

    def halo_place(kind, target, count):
        for f in range(count):
            for j in range(edge):
                spread(land[kind, LEFT, f * edge + j], target, 4 * j, 4 * f)
                spread(land[kind, RIGHT, f * edge + j], target, W + rows + 4 * j, 4 * f)

    def gather(source, places, b):
        return jnp.concatenate([source[places[b, k]] for k in range(K)], axis=1)

    def react(v, rate):
        total = None
        for t in range(SPECIES):
            line_t = v[t : t + 1]
            if v.shape[0] == 8:
                second = v[4 + t : 5 + t]
                row = lax.broadcasted_iota(jnp.int32, (8, BS), 0)
                line_t = jnp.where(row < 4, jnp.broadcast_to(line_t, (8, BS)), jnp.broadcast_to(second, (8, BS)))
            term = mix_v[t, : v.shape[0]] * line_t
            total = term if total is None else total + term
        return total * rate

    def paired(first, second, weights):
        got = dot(jnp.concatenate([first, second], axis=0), weights)
        return got[:8, :BS], got[8:, BS:]

    def explicit(b, count):
        got = dot(gather(near, place_of, b), raw_w[b])[: 4 * count]
        return got + react(near[W + b, : 4 * count], rates[pl.ds(b, 1)])

    def transposed(n, carry):
        for r in range(4):
            b, half = 4 * n + r, pl.ds(BS * (r % 2), BS)
            diag_w[2 * n + r // 2, :, half] = diag_v[b].T
            fine_w[2 * n + r // 2, :, half] = fine_v[b].T
            for k in range(K):
                raw_w[b, BS * k : BS * (k + 1)] = off_v[b, k].T
        return carry

    def outer(*bodies):
        for body in bodies:
            rows_loop(0, W // 2, body)
            rows_loop((rows - W) // 2, rows // 2, body)

    def inner(*bodies):
        for body in bodies:
            rows_loop(W // 2, (rows - W) // 2, body)

    def solve(target):
        def pair(i):
            got = paired(right_v[2 * i], right_v[2 * i + 1], fine_w[i])
            target[2 * i], target[2 * i + 1] = got[0][:4], got[1][:4]

        return pair

    def terms_copies(it, late):
        slot = tm % STRETCH
        main = terms_land.at[slot]
        to = [chain_device(i, chain_plane(it, tm)) for i in (low, high, low - 1, high + 1)]

        def piece(first, count, at, n, sem, device):
            return remote(
                terms_b.at[it, pl.ds(first, count)], main.at[pl.ds(at, count)], terms_send.at[it, n],
                terms_recv.at[slot, sem], device,
            )

        if late:
            return (
                (piece(0, 2, 2, 0, 0, to[0]), True),
                (piece(6, 2, 4, 1, 0, to[1]), True),
                (piece(0, 2, 6, 2, 1, to[2]), has_left),
                (piece(6, 2, 0, 3, 1, to[3]), has_right),
            )
        return (piece(2, 4, 4, 4, 2, to[0]), True), (piece(2, 4, 0, 5, 2, to[1]), True)

    def terms_out(it, late):
        for j in (0, 1, 6, 7) if late else range(2, 6):
            terms_b[it, j, 0] = tile([sum_c[4 * j + g] for g in range(4)])
            terms_b[it, j, 1] = tile([sum_t[4 * j + g] for g in range(4)])
        for copy, there in terms_copies(it, late):
            if there is True:
                copy.start()
            else:
                pl.when(there)(copy.start)

    def terms_sent(it):
        for copy, there in terms_copies(it, True) + terms_copies(it, False):
            if there is True:
                copy.wait_send()
            else:
                pl.when(there)(copy.wait_send)

    def fine(it):
        @pl.when(it == 0)
        def _():
            halo_send(NODES, [lambda b: nodes[b, 0:4], lambda b: nodes[b, 4:8]])
            first_things()
            pl.when(tm == 0)(start_out)
            for load in large:
                load.wait()
            lax.fori_loop(0, rows // 4, transposed, 0)
            for b in range(rows):
                near[W + b] = nodes[b]
            halo_wait(NODES, 2)
            halo_place(NODES, near, 2)

        @pl.when(it == 1)
        def _():
            @pl.when(tm > 0)
            def _():
                values_wait(0, 0, True)
                for j in range(rows // 4):
                    spread(value_land[0, 0, j], nodes, 4 * j, 0)
                    spread(value_land[0, 0, j], near, W + 4 * j, 0)
                for j in range(edge):
                    spread(value_halo[0, LEFT, j], near, 4 * j, 0)
                    spread(value_halo[0, RIGHT, j], near, W + rows + 4 * j, 0)

            @pl.when(tm == 0)
            def _():
                for b in range(rows):
                    near[W + b, 0:4] = nodes[b, 0:4]
                for j in range(edge):
                    spread(land[NODES, LEFT, j], near, 4 * j, 0)
                    spread(land[NODES, RIGHT, j], near, W + rows + 4 * j, 0)

            values_wait(0, 1, True)
            for j in range(rows // 4):
                spread(value_land[0, 1, j], near, W + 4 * j, 4)
            for j in range(edge):
                spread(value_halo[1, LEFT, j], near, 4 * j, 4)
                spread(value_halo[1, RIGHT, j], near, W + rows + 4 * j, 4)

        own_part = jnp.where(it == 0, 0.0, 0.5)
        end_part = jnp.where(it == 0, 1.0, 0.5)

        def node_terms(i):
            imps = paired(near[W + 2 * i], near[W + 2 * i + 1], diag_w[i])
            for b, imp in zip((2 * i, 2 * i + 1), imps):
                exp = explicit(b, 2)
                imp_0, exp_0, imp_2, exp_2 = imp[:4], exp[:4], imp[4:], exp[4:]
                one_i = imp_b[b] + own_part * imp_0 + end_part * imp_2
                one_e = exp_b[b] + own_part * exp_0 + end_part * exp_2
                f_0, f_1, f_2 = imp_0 + exp_0, one_i + one_e, imp_2 + exp_2
                right_v[b, 0:4] = (
                    nodes[b, 0:4] - HALF * one_i + STEP * (5 / 24 * f_0 + 1 / 3 * f_1 - 1 / 24 * f_2)
                )
                second_r[b] = STEP * (-1 / 24 * f_0 + 1 / 3 * f_1 + 5 / 24 * f_2) - HALF * (one_e + imp_2)
                sum_c[b] = STEP * (1 / 6 * f_0 - exp_0)
                sum_t[b] = (-STEP / 3) * f_0
                imp_b[b] = -0.5 * imp_0
                exp_b[b] = -0.5 * exp_0

        outer(node_terms, solve(first_v))
        halo_send(FIRST, [lambda b: first_v[b]])
        inner(node_terms, solve(first_v))

        def put_first(b):
            near[W + b, 0:4] = first_v[b]

        rows_loop(0, rows, put_first)
        early_units(it, 0)
        halo_wait(FIRST, 1)
        halo_place(FIRST, near, 1)

        def first_terms(i):
            imps = paired(near[W + 2 * i], near[W + 2 * i + 1], diag_w[i])
            for b, imp in zip((2 * i, 2 * i + 1), imps):
                imp = imp[:4]
                exp = explicit(b, 1)
                force = STEP * 2 / 3 * (imp + exp)
                right_v[b, 0:4] = first_v[b] + HALF * exp + second_r[b]
                sum_c[b] += force
                sum_t[b] += force
                imp_b[b] += imp
                exp_b[b] += exp

        outer(first_terms, solve(fresh))
        halo_send(SECOND, [lambda b: fresh[b]])
        inner(first_terms, solve(fresh))

        def put_second(b):
            near[W + b, 0:4] = fresh[b]
            mid_b[b] = first_v[b] - 0.5 * (nodes[b, 0:4] + fresh[b])

        rows_loop(0, rows, put_second)

        def second_terms(i):
            imps = paired(near[W + 2 * i], near[W + 2 * i + 1], diag_w[i])
            for b, imp in zip((2 * i, 2 * i + 1), imps):
                imp = imp[:4]
                exp = explicit(b, 1)
                force = imp + exp
                sum_c[b] += STEP * (1 / 6 * force - imp)
                sum_t[b] += (-STEP / 3) * force
                imp_b[b] += -0.5 * imp
                exp_b[b] += -0.5 * exp

        inner(second_terms)
        terms_out(it, False)
        early_units(it, 1)
        halo_wait(SECOND, 1)
        halo_place(SECOND, near, 1)
        outer(second_terms)
        terms_out(it, True)

    def values_wait(it, which, halos):
        for n in range(2):
            arrive(value_land.at[it, which, pl.ds(n * T_OWN, T_OWN)], value_recv.at[it, which, n])
        if halos:
            arrive(value_halo.at[which, LEFT], value_recv.at[it, which, 2], has_left)
            arrive(value_halo.at[which, RIGHT], value_recv.at[it, which, 3], has_right)

    def value_copies(j):
        it, p = round_here, stretch * STRETCH + j
        half = chunk % 2
        copies = []
        for which in (1, 0):
            t = p + 1 - which
            there = (p < n_tm - 1) & ~((p == STRETCH * (stretch + 1) - 1) & own_next) if which == 0 else True
            copies.append((remote(
                end_b.at[j], value_land.at[it, which, pl.ds(pl.multiple_of(half * T_OWN, T_OWN), T_OWN)],
                value_send.at[j, which, 0], value_recv.at[it, which, half], (t, owner)), there))
            copies.append((remote(
                end_b.at[j, pl.ds(pl.multiple_of(half * (T_OWN - T_EDGE), T_EDGE), T_EDGE)], value_halo.at[which, 1 - half],
                value_send.at[j, which, 1], value_recv.at[it, which, 3 - half], (t, beside)),
                (t < n_tm) & has_beside & (it == 0)))
        return copies

    def value_here(j):
        half = chunk % 2
        return pltpu.make_async_copy(
            end_b.at[j], value_land.at[round_here, 0, pl.ds(pl.multiple_of(half * T_OWN, T_OWN), T_OWN)],
            value_recv.at[round_here, 0, half],
        )

    def chain_copies(j, half):
        inside = j < STRETCH - 1
        target = jnp.where(inside, j + 1, 0)
        z = jnp.where(inside, plane, plane - 2)
        there = inside | later
        at = pl.ds(half * T_EDGE, T_EDGE)
        copies = []
        for n, (i, ok) in enumerate(((chunk - 1, chunk_left), (chunk + 1, chunk_right))):
            part = 2 - 2 * n
            copies.append((remote(
                end_b.at[j, at], chain_land.at[target, part, at], chain_send.at[j, 2 * n, half],
                chain_recv.at[target, part, half], chain_device(i, z)), there & ok))
        if half == 1:
            copies.append((remote(
                end_b.at[j], chain_land.at[target, 1], chain_send.at[j, 1, 0], chain_recv.at[target, 1, 0],
                chain_device(chunk, z)), there & ~inside))
        return copies

    def start_copies(it):
        copies = []
        for n, (i, part, own, ok) in enumerate((
            (low, 1, 0, True), (low, 2, 1, True), (low - 1, 2, 0, has_left),
            (high, 1, 1, True), (high, 0, 0, True), (high + 1, 0, 1, has_right),
        )):
            device = chain_device(i, chain_plane(it, 0))
            for half in range(2):
                count = T_OWN if part == 1 else T_EDGE
                if part == 1 and half == 1:
                    continue
                copies.append((remote(
                    start_b.at[pl.ds(own * T_OWN + half * T_EDGE, count)],
                    chain_land.at[0, part, pl.ds(half * T_EDGE, count)], start_send.at[it, n, half],
                    chain_recv.at[0, part, half], device), (tm == 0) & ok))
        return copies

    def first_things():
        pieces(0, lambda copy: copy.start())
        pl.when(plane == first_plane)(weights_out)
        def local_place(b, carry):
            for k in range(K):
                place_of[b, k] = jnp.clip(cols[k, b] - (sp * rows - W), 0, rows + 2 * W - 1)
            return carry

        lax.fori_loop(0, rows, local_place, 0)
        near[...] = jnp.zeros_like(near)
        near_q[...] = jnp.zeros_like(near_q)
        imp_b[...] = jnp.zeros_like(imp_b)
        exp_b[...] = jnp.zeros_like(exp_b)
        for t in range(SPECIES):
            column = jnp.broadcast_to(mixing[:, t : t + 1], (SPECIES, BS))
            mix_v[t] = jnp.concatenate([column, column], axis=0)

    def start_out():
        for j in range(rows // 4):
            start_b[j] = tile([nodes[4 * j + g, 0:4] for g in range(4)])
        for copy, there in start_copies(0):
            pl.when(there)(copy.start)

    def composed(n, carry):
        for r in range(4):
            w = 4 * n + r
            inverse = win_coarse[w].T
            comp_w[w, BS : 2 * BS] = inverse
            inverse_w[2 * n + r // 2, :, BS * (r % 2) : BS * (r % 2 + 1)] = inverse
            raw = [win_diag[w]] + [win_off[w, k] for k in range(K)]
            got = (dot(jnp.concatenate([block.T for block in raw], axis=0), inverse) * STEP).astype(jnp.bfloat16)
            comp_w[w, :BS] = got[:BS]
            comp_w[w, 2 * BS :] = got[BS:]
        return carry

    def window_unit(at, foreign=True):
        unit = 2 * mine - 1 + at

        @pl.when((unit >= 0) & (unit < 8))
        def _():
            copies = unit_copies(0, at, (tm, sp))
            for copy in copies[:3] if at in (0, 3) else copies:
                copy.wait_recv()

        if at in (0, 3) and foreign:
            there = lower if at == 0 else upper
            for n in range(len(PIECES)):
                @pl.when(there)
                def _(n=n):
                    for copy in piece_copies(n, 0, at, (tm, sp), n):
                        copy.wait_recv()

        lax.fori_loop(W // 4 * at, W // 4 * (at + 1), composed, 0)

    def window_places():
        first_unit = 2 * mine - 1
        arrive(cols_land.at[1], cols_recv.at[1])
        arrive(cols_land.at[0], cols_recv.at[0], lower)
        arrive(cols_land.at[3], cols_recv.at[3], upper)
        to_scalars = pltpu.make_async_copy(cols_land, cols_s, cols_send.at[3])
        to_scalars.start()
        to_scalars.wait()

        def places(w, carry):
            unit = first_unit + w // W
            slot, row = (unit + 4) // 4, (unit + 4) % 4 * W + w % W
            for k in range(K):
                column = jnp.where(slot == 2, cols[k, row], cols_s[slot, k, row])
                place_w[w, k] = jnp.clip(column - (chunk * OWN - 2 * W), 0, OWN + 4 * W - 1)
            return carry

        lax.fori_loop(0, WINDOW, places, 0)

    hurry = on_chain & (plane == first_plane)

    def early_units(it, step):
        @pl.when((it == 0) & hurry)
        def _():
            if step == 0:
                window_places()
                window_unit(1)
            else:
                window_unit(2)
                pl.when(mine != GROUP - 1)(functools.partial(window_unit, 3, False))
                pl.when(mine == GROUP - 1)(functools.partial(window_unit, 0, False))

    def window_weights():
        @pl.when(~hurry)
        def _():
            window_places()
            for at in range(4):
                window_unit(at)

        @pl.when(hurry)
        def _():
            pl.when(mine == GROUP - 1)(functools.partial(window_unit, 3))
            pl.when(mine != GROUP - 1)(functools.partial(window_unit, 0))

    def chain_step(g, carry):
        halo_at = jnp.where(even, 0, 6)
        early_at, late_at = jnp.where(even, 4, 0), jnp.where(even, 2, 4)

        @pl.when(g == 0)
        def _():
            arrive(chain_land.at[g, 1], chain_recv.at[g, 1, 0])
            for n in range(T_OWN):
                spread(chain_land[g, 1, n], near, 2 * W + 4 * n, 0)

        arrive(terms_land.at[g, pl.ds(early_at, 4)], terms_recv.at[g, 2])
        arrive(terms_land.at[g, pl.ds(late_at, 2)], terms_recv.at[g, 0])
        arrive(terms_land.at[g, pl.ds(halo_at, 2)], terms_recv.at[g, 1], has_beside)

        def prepare(n):
            constant = terms_land[g, n, 0].astype(jnp.float32)
            for r in range(4):
                w = 4 * n + r
                own = near[W + w, 0:4]
                change = STEP * react(own, win_rates[pl.ds(w, 1)])
                right_v[w, 0:4] = own + change + constant[4 * r : 4 * r + 4]
                state[w] = 2.0 * own + change
            for i in (2 * n, 2 * n + 1):
                got = paired(right_v[2 * i], right_v[2 * i + 1], inverse_w[i])
                solved[2 * i], solved[2 * i + 1] = got[0][:4], got[1][:4]

        rows_loop(T_EDGE, T_WINDOW - T_EDGE, prepare)

        def with_rest(n):
            constant = terms_land[g, T_EDGE + n, 1].astype(jnp.float32)
            for r in range(4):
                state[W + 4 * n + r] += 2.0 * constant[4 * r : 4 * r + 4]

        rows_loop(0, T_OWN, with_rest)

        def far_part(w):
            partial[w] = 0.5 * dot(gather(near, place_w, w), comp_w[w, 2 * BS :])[:4]

        def middle_sum(w):
            near_q[W + w, 0:4] = solved[w] + 2.0 * partial[w]

        def middle(w):
            spread_s = dot(gather(near, place_w, w), comp_w[w, 2 * BS :])[:4]
            near_q[W + w, 0:4] = solved[w] + spread_s
            partial[w] = 0.5 * spread_s

        first, last = pl.ds(0, T_EDGE), pl.ds(T_EDGE, T_EDGE)
        arrive(chain_land.at[g, 2, first], chain_recv.at[g, 2, 0], chunk_right)
        for n in range(T_EDGE):
            spread(chain_land[g, 2, n], near, 2 * W + OWN + 4 * n, 0)
        rows_loop(2 * W, 2 * W + W, middle)
        rows_loop(T_WINDOW - T_EDGE, T_WINDOW, prepare)
        arrive(chain_land.at[g, 0, first], chain_recv.at[g, 0, 0], chunk_left)
        arrive(chain_land.at[g, 0, last], chain_recv.at[g, 0, 1], chunk_left)
        arrive(chain_land.at[g, 2, last], chain_recv.at[g, 2, 1], chunk_right)
        for n in range(T_OWN):
            spread(chain_land[g, 0, n], near, 4 * n, 0)
        for n in range(T_EDGE, T_OWN):
            spread(chain_land[g, 2, n], near, 2 * W + OWN + 4 * n, 0)
        rows_loop(0, W, far_part)
        rows_loop(0, T_EDGE, prepare)
        rows_loop(W, 2 * W, middle)
        rows_loop(0, W, middle_sum)
        rows_loop(3 * W, WINDOW, middle)

        def end_far(o):
            fresh[o] = dot(gather(near_q, place_w, W + o), comp_w[W + o, 2 * BS :])[:4]

        def end(o):
            w = W + o
            own, mid = near[W + w, 0:4], near_q[W + w, 0:4]
            right = state[w] + STEP * react(mid, win_rates[pl.ds(w, 1)])
            parts = jnp.concatenate([own - mid, right], axis=1)
            near[W + w, 0:4] = partial[w] + 0.5 * (fresh[o] + dot(parts, comp_w[w, : 2 * BS]))

        for half in range(2):
            rows_loop(half * W, (half + 1) * W, end_far)
            rows_loop(half * W, (half + 1) * W, end)
            for n in range(half * T_EDGE, (half + 1) * T_EDGE):
                end_b[g, n] = tile([near[2 * W + 4 * n + r, 0:4] for r in range(4)])
            for copy, there in chain_copies(g, half):
                pl.when(there)(copy.start)
        pl.when((g == STRETCH - 1) & own_next)(lambda: value_here(g).start())
        for copy, there in value_copies(g):
            if there is True:
                copy.start()
            else:
                pl.when(there)(copy.start)
        return carry

    def round_of(it, carry):
        fine(it)

        @pl.when(it == 0)
        def _():
            terms_sent(0)

            @pl.when(tm == 0)
            def _():
                for copy, there in start_copies(1):
                    pl.when(there)(copy.start)

            pieces(1, lambda copy: copy.start())
            pieces(2, lambda copy: copy.start())
            pl.when(plane != first_plane)(weights_out)

        composes = jnp.where((plane == 0) & (line == 0), 1, 0)
        pl.when(on_chain & (it == composes))(window_weights)

        @pl.when(on_chain & (it == stretch))
        def _():
            lax.fori_loop(0, STRETCH, chain_step, 0)

        return carry

    lax.fori_loop(0, ITERS, round_of, 0)

    weights_sent()
    for when in range(3):
        pieces(when, lambda copy: copy.wait_send())
    for it in range(ITERS):
        for copy, there in start_copies(it):
            pl.when(there)(copy.wait_send)
    terms_sent(1)

    @pl.when(on_chain)
    def _():
        def sent(g, carry):
            for copy, there in chain_copies(g, 0) + chain_copies(g, 1) + value_copies(g):
                if there is True:
                    copy.wait_send()
                else:
                    pl.when(there)(copy.wait_send)
            return carry

        lax.fori_loop(0, STRETCH, sent, 0)

    pl.when(tm > 0)(lambda: values_wait(1, 0, False))

    def write_start(j):
        starts = value_land[1, 0, j].astype(jnp.float32)
        for g in range(4):
            b = 4 * j + g
            own = jnp.where(tm == 0, start[:, cells(b)], starts[4 * g : 4 * g + 4])
            out[0, 0, :, cells(b)] = own
            mid_b[b] += 0.5 * own

    rows_loop(0, rows // 4, write_start)
    values_wait(1, 1, False)

    def write(j):
        ends = value_land[1, 1, j].astype(jnp.float32)
        for g in range(4):
            b = 4 * j + g
            last = ends[4 * g : 4 * g + 4]
            out[0, 1, :, cells(b)] = mid_b[b] + 0.5 * last
            out[0, 2, :, cells(b)] = last

    rows_loop(0, rows // 4, write)


def shards(n_tm, n_sp, start, guess, diag, off, columns, rates, mixing, fine, coarse):
    rows = diag.shape[0]
    f32, bf16 = jnp.float32, jnp.bfloat16
    vmem = pl.BlockSpec(memory_space=pltpu.VMEM)
    hbm = pl.BlockSpec(memory_space=pltpu.HBM)
    dma = pltpu.SemaphoreType.DMA
    edge = W // 4
    slots = STRETCH

    def tiles(*lead):
        return pltpu.VMEM((*lead, 16, BS), bf16)

    def blocks(*lead):
        return pltpu.VMEM((*lead, BS, BS), bf16)

    pairs = pltpu.VMEM((rows // 2, BS, 2 * BS), bf16)
    scratch = [
        pltpu.VMEM((SPECIES, rows * BS), f32), pltpu.VMEM((1, SPECIES, rows * BS), f32),
        pltpu.SMEM((K, rows), jnp.int32), pltpu.VMEM((rows, BS), f32), pltpu.VMEM((SPECIES, SPECIES), f32),
        blocks(rows), blocks(rows, K), blocks(rows),
        pltpu.VMEM((rows, K * BS, BS), bf16), pairs, pairs,
        blocks(WINDOW), blocks(WINDOW, K), blocks(WINDOW), pltpu.VMEM((WINDOW, BS), f32),
        pltpu.VMEM((WINDOW, (K + 2) * BS, BS), bf16),
        pltpu.VMEM((WINDOW // 2, BS, 2 * BS), bf16),
        pltpu.VMEM((rows + 2 * W, 8, BS), f32), pltpu.VMEM((rows + 2 * W, 8, BS), f32),
        pltpu.VMEM((SPECIES, 8, BS), f32), pltpu.VMEM((rows, 8, BS), f32),
        *[pltpu.VMEM((rows, SPECIES, BS), f32)] * 11, pltpu.VMEM((rows, 8, BS), f32),
        tiles(3, 2, 2 * edge), tiles(3, 2, 2 * edge),
        tiles(ITERS, rows // 4, 2), tiles(slots, T_WINDOW, 2),
        tiles(rows // 4), tiles(slots, 3, T_OWN), tiles(slots, T_OWN),
        tiles(ITERS, 2, rows // 4), tiles(2, 2, edge),
        pltpu.VMEM((4, K, rows), jnp.int32), pltpu.SMEM((4, K, rows), jnp.int32),
        pltpu.SMEM((rows, K), jnp.int32), pltpu.SMEM((WINDOW, K), jnp.int32),
        dma((8,)), dma((3, 2)), dma((3, 2)), dma((4, 4)), dma((4, 4)), dma((4,)), dma((4,)),
        dma((3 * len(PIECES), 3)), dma((len(PIECES), 3)),
        dma((ITERS, 6)), dma((slots, 3)), dma((ITERS, 6, 2)), dma((slots, 3, 2)), dma((slots, 3, 2)),
        dma((slots, 2, 2)), dma((ITERS, 2, 4)),
    ]
    return pl.pallas_call(
        functools.partial(kernel, n_tm, n_sp, rows),
        out_shape=jax.ShapeDtypeStruct((1, 3, SPECIES, rows * BS), f32),
        in_specs=[hbm] * 9,
        out_specs=vmem,
        scratch_shapes=scratch,
        compiler_params=pltpu.CompilerParams(
            collective_id=0, has_side_effects=True, vmem_limit_bytes=60 << 20
        ),
    )(start, guess, columns.T, rates.reshape(rows, BS), mixing, diag, off, fine, coarse)


def solution(mesh):
    in_specs = (
        P(None, "space"),
        P("tm", None, "space"),
        P("space", None, None),
        P("space", None, None, None),
        P("space", None),
        P("space"),
        P(),
        P("space", None, None),
        P("space", None, None),
    )
    out_specs = P("tm", None, None, "space")
    body = functools.partial(shards, mesh.shape["tm"], mesh.shape["space"])
    return jax.shard_map(body, mesh=mesh, in_specs=in_specs, out_specs=out_specs, check_vma=False)
```
